32 devices in a mesh: lat: 16 (over z, y, core), ha: 2 (over x).
Axes of the slice: x: 2, y: 2, z: 4, core: 2. Of those that a mesh axis runs over, the one named last changes fastest.
Arguments:
- adjoint_e: float32 [3, 8, 1024, 128], P(None, 'ha', 'lat'), may hold values from -6 to 6
- adjoint_h: float32 [3, 8, 1024, 128], P(None, 'ha', 'lat'), may hold values from -6 to 6
- saved_e: bfloat16 [2, 3, 8, 1024, 128], P(None, None, 'ha', 'lat'), may hold values from -5 to 5
- labels: int32 [8, 1024, 128], P('ha', 'lat'), may hold values from 0 to 3
- eps_table: float32 [4], replicated, may hold values from 1 to 12
- chi_table: float32 [4], replicated, may hold values from 0.05 to 0.5
- density: float32 [1024, 128], P('lat'), may hold values from 0 to 1
- mon_cells: int32 [16384], P(('lat', 'ha')), may hold values from 0 to 32767
- mon_weight: float32 [16384], P(('lat', 'ha')), may hold values from 0.25 to 6.75
Outputs:
- final_e: float32 [3, 8, 1024, 128], P(None, 'ha', 'lat')
- final_h: float32 [3, 8, 1024, 128], P(None, 'ha', 'lat')
- design_grad: float32 [1024, 128], P('lat')
The draws below stay inside these ranges and needn't reach their ends.
Inputs may be any that keep to these rules, and one draw needn't show every extreme that they name: `labels`: label 0 marks design cells. `mon_cells`: entry m names a cell of the block of block number m // 512 (lat major, ha minor), numbered in z, x, y order within the block; entries may repeat.
All inputs are finite; a program needn't handle non-finite values.
Results may differ from the reference program's by a relative error of at most 0.0003.
Values sent between devices are 32-bit elements; how exact they have to be, the bound alone decides.
A program may use at most 64 MiB of HBM per device.

```python
import jax
import jax.numpy as jnp
from jax import lax

CX = 64
CZ = 4
NY = 128
STEPS = 2
NREG = 4
MON_DEV = 512
RADIUS = 16
NX = 1024
NZ = 8
MON_ALL = 16384
N_HA = 2


def draw_mon_weight(key, part):
    position = jnp.arange(MON_ALL, dtype=jnp.float32) / MON_ALL
    base = jax.random.uniform(key, (MON_ALL,), jnp.float32, 0.5, 1.5)
    return base * (1.0 + 2.0 * position)


def plant(values, stream_key, smallest, top_value):
    longest = values.shape.index(max(values.shape))
    spots = []
    for shift in (0, 1):
        where = [jax.random.randint(jax.random.fold_in(stream_key, axis), (), 0, length) for axis, length in enumerate(values.shape)]
        where[longest] = (where[longest] + shift) % values.shape[longest]
        spots.append(tuple(where))
    return values.at[spots[0]].set(smallest).at[spots[1]].set(top_value)


def level_of(own_key, dims, split, smallest, high):
    gain, own = 1.0, jax.random.fold_in(own_key, 6)
    for dim, parts in split:
        heights = jnp.exp(jax.random.uniform(jax.random.fold_in(own, dim), (parts,), jnp.float32, smallest / len(split), high / len(split)))
        gain = gain * jnp.repeat(heights, dims[dim] // parts).reshape([-1 if axis == dim else 1 for axis in range(len(dims))])
    return gain


def centred(own_key, extent, scale, most, split=(), kind=jnp.bfloat16):
    factor_of = level_of(own_key, extent, split, -0.22, 0.18) if split else 1.0
    result = jax.random.normal(own_key, extent, jnp.float32) * scale * factor_of
    return jnp.minimum(jnp.maximum(result, -most), most).astype(kind)


def setup_inputs(seed: int = 0) -> dict:
    splits = jax.random.split(jax.random.key(seed), 10)
    adjoint_e = centred(splits[0], (3, NZ, NX, NY), 1.0, 6.0, ((1, 2), (2, 16)), jnp.float32)
    adjoint_h = centred(splits[1], (3, NZ, NX, NY), 1.0, 6.0, ((1, 2), (2, 16)), jnp.float32)
    saved_e = centred(splits[2], (STEPS, 3, NZ, NX, NY), 1.0, 5.0, ((2, 2), (3, 16)))
    labels = plant(jax.random.randint(splits[3], (NZ, NX, NY), 0, NREG), jax.random.fold_in(splits[3], 1), 0, NREG - 1).astype(jnp.int32)
    eps_table = jnp.clip(jax.random.uniform(splits[4], (NREG,), jnp.float32, 1.0, 12.0), 1.0, 12.0)
    chi_table = jnp.clip(jax.random.uniform(splits[5], (NREG,), jnp.float32, 0.05, 0.5), 0.05, 0.5)
    density = jnp.clip(1.0 * jax.random.uniform(splits[6], (NX, NY), jnp.float32) ** level_of(splits[6], (NX, NY), ((0, 16),), -0.2, 0.2), 0.0, 1.0)
    mon_cells = plant(jax.random.randint(splits[7], (MON_ALL,), 0, CZ * CX * NY), jax.random.fold_in(splits[7], 1), 0, (CZ * CX * NY) - 1).astype(jnp.int32)
    mon_weight = draw_mon_weight(jax.random.fold_in(splits[9], 71), 0)
    return dict(adjoint_e=adjoint_e, adjoint_h=adjoint_h, saved_e=saved_e, labels=labels, eps_table=eps_table, chi_table=chi_table, density=density, mon_cells=mon_cells, mon_weight=mon_weight)


sharpness = 8.0
threshold = 0.5
time_step = 0.5
epsilon = 1e-5


def lower(field, axis):
    length = field.shape[axis]
    first = jnp.zeros_like(lax.slice_in_dim(field, 0, 1, axis=axis))
    return jnp.concatenate([first, lax.slice_in_dim(field, 0, length - 1, axis=axis)], axis)


def upper(field, axis):
    length = field.shape[axis]
    last = jnp.zeros_like(lax.slice_in_dim(field, 0, 1, axis=axis))
    return jnp.concatenate([lax.slice_in_dim(field, 1, length, axis=axis), last], axis)


def curl_lower(field):
    field_x, field_y, field_z = field[0], field[1], field[2]
    curl_x = (field_z - lower(field_z, 2)) - (field_y - lower(field_y, 0))
    curl_y = (field_x - lower(field_x, 0)) - (field_z - lower(field_z, 1))
    curl_z = (field_y - lower(field_y, 1)) - (field_x - lower(field_x, 2))
    return jnp.stack([curl_x, curl_y, curl_z])


def curl_upper(field):
    field_x, field_y, field_z = field[0], field[1], field[2]
    curl_x = (upper(field_z, 2) - field_z) - (upper(field_y, 0) - field_y)
    curl_y = (upper(field_x, 0) - field_x) - (upper(field_z, 1) - field_z)
    curl_z = (upper(field_y, 1) - field_y) - (upper(field_x, 2) - field_x)
    return jnp.stack([curl_x, curl_y, curl_z])


def smooth_axis(field, axis):
    widths = [(0, 0), (0, 0)]
    widths[axis] = (RADIUS, RADIUS)
    padded = jnp.pad(field, widths)
    total = jnp.zeros_like(field)
    for position in range(2 * RADIUS + 1):
        weight = (RADIUS + 1 - abs(position - RADIUS)) / (RADIUS + 1) ** 2
        total = total + weight * lax.slice_in_dim(padded, position, position + field.shape[axis], axis=axis)
    return total


def smooth(field):
    return smooth_axis(smooth_axis(field, 1), 0)


def reference(adjoint_e, adjoint_h, saved_e, labels, eps_table, chi_table, density, mon_cells, mon_weight):
    eps_cell = eps_table[labels]
    chi_cell = chi_table[labels]
    design = (labels == 0).astype(jnp.float32)
    block = jnp.arange(MON_ALL, dtype=jnp.int32) // MON_DEV
    lat_index = block // N_HA
    ha_index = block % N_HA
    depth = mon_cells // (CX * NY)
    across = (mon_cells // NY) % CX
    column = mon_cells % NY
    flat = (((ha_index * CZ + depth) * NX + lat_index * CX + across) * NY + column).astype(jnp.int32)
    shape = adjoint_e.shape
    lam_e = adjoint_e
    lam_h = adjoint_h
    plane = jnp.zeros((NX, NY), jnp.float32)
    for index in reversed(range(STEPS)):
        forward = saved_e[index].astype(jnp.float32)
        jacobian = eps_cell[None] + 3.0 * chi_cell[None] * forward * forward
        picked = forward.reshape(3, -1)[:, flat]
        power = jnp.sum(mon_weight * jnp.sum(picked * picked, 0)) / MON_ALL + epsilon
        lam_e = lam_e.reshape(3, -1).at[:, flat].add(mon_weight * picked / power).reshape(shape)
        scaled = lam_e / jacobian
        plane = plane + jnp.sum(design * jnp.sum(scaled * forward, 0), 0)
        lam_h = lam_h - time_step * curl_lower(scaled)
        lam_e = lam_e + time_step * curl_upper(lam_h)
    filtered = smooth(density)
    slope = jnp.tanh(sharpness * (filtered - threshold))
    derivative = sharpness * (1.0 - slope * slope) / (jnp.tanh(sharpness * threshold) + jnp.tanh(sharpness * (1.0 - threshold)))
    design_grad = smooth(derivative * plane)
    return lam_e, lam_h, design_grad
```

```python
import functools

import jax
import jax.numpy as jnp
from jax import lax
from jax.experimental import pallas as pl
from jax.experimental.pallas import tpu as pltpu
from jax.sharding import PartitionSpec as P

RADIUS = 16

sharpness = 8.0
threshold = 0.5
time_step = 0.5
epsilon = 1e-05

MESH = pl.DeviceIdType.MESH


def cone(offset):
    return jnp.maximum(RADIUS + 1 - jnp.abs(offset), 0).astype(jnp.float32) / (RADIUS + 1) ** 2


def filter_rows(padded, rows):
    width = padded.shape[1]
    i = lax.broadcasted_iota(jnp.int32, (width, width), 0)
    j = lax.broadcasted_iota(jnp.int32, (width, width), 1)
    smoothed = jnp.dot(
        padded, cone(i - j), precision=lax.Precision.HIGHEST, preferred_element_type=jnp.float32
    )
    row_out = lax.broadcasted_iota(jnp.int32, (rows, rows + 2 * RADIUS), 0)
    row_in = lax.broadcasted_iota(jnp.int32, (rows, rows + 2 * RADIUS), 1)
    return jnp.dot(
        cone(row_in - RADIUS - row_out),
        smoothed,
        precision=lax.Precision.HIGHEST,
        preferred_element_type=jnp.float32,
    )


def kernel(
    n_lat,
    n_ha,
    adj_e,
    adj_h,
    saved,
    labels,
    eps_table,
    chi_table,
    density,
    cells,
    weight,
    out_e,
    out_h,
    out_g,
    e,
    h0,
    sv,
    lb,
    dens,
    cl,
    wt,
    wgrid,
    ab,
    s,
    hh,
    rinv,
    plane,
    grad,
    dens_lo,
    dens_hi,
    deriv,
    zab,
    rab_out,
    rab,
    zl,
    rl_out,
    rl,
    zu,
    ru_out,
    ru,
    pw_out,
    pw_ha,
    pw_sum,
    pw_lat,
    plane_ha,
    plane_lo,
    plane_hi,
    local_sem,
    send_sem,
    recv_sem,
):
    steps, comps, depth, rows, width = sv.shape
    regions = eps_table.shape[0]
    entries = cl.shape[1]
    lat = lax.axis_index("lat")
    ha = lax.axis_index("ha")
    lat_dn, lat_up = lat > 0, lat < n_lat - 1
    ha_dn, ha_up = ha > 0, ha < n_ha - 1
    lat_prev, lat_next = jnp.maximum(lat - 1, 0), jnp.minimum(lat + 1, n_lat - 1)
    ha_prev, ha_next = jnp.maximum(ha - 1, 0), jnp.minimum(ha + 1, n_ha - 1)

    pairs = [
        (cells, cl),
        (weight, wt),
        (saved, sv),
        (adj_e, e),
        (labels, lb),
        (density, dens),
        (adj_h, h0),
    ]
    loads = [pltpu.make_async_copy(a, b, local_sem.at[i]) for i, (a, b) in enumerate(pairs)]
    for load in loads:
        load.start()

    barrier = pltpu.get_barrier_semaphore()

    def greet(l, k):
        pl.semaphore_signal(barrier, inc=1, device_id=(l, k), device_id_type=MESH)

    for d in range(1, n_lat):
        greet(lax.rem(lat + d, n_lat), ha)
    for d in range(1, n_ha):
        other = lax.rem(ha + d, n_ha)
        greet(lat, other)
        pl.when(lat_dn)(functools.partial(greet, lat_prev, other))
        pl.when(lat_up)(functools.partial(greet, lat_next, other))

    issued = []

    def exchange(src, dst, target, sends=None, receives=None):
        index = len(issued)

        def copy():
            return pltpu.make_async_remote_copy(
                src_ref=src,
                dst_ref=dst,
                send_sem=send_sem.at[index],
                recv_sem=recv_sem.at[index],
                device_id=target,
                device_id_type=MESH,
            )

        def guarded(condition, action):
            if condition is None:
                action()
            else:
                pl.when(condition)(action)

        issued.append(lambda: guarded(sends, lambda: copy().wait_send()))
        guarded(sends, lambda: copy().start())

        def arrive():
            guarded(receives, lambda: copy().wait_recv())
            if receives is not None:

                @pl.when(jnp.logical_not(receives))
                def _():
                    dst[...] = jnp.zeros(dst.shape, dst.dtype)

        return arrive

    loads[0].wait()
    loads[1].wait()
    cell = cl[...]
    amount = wt[...]
    first = amount.astype(jnp.bfloat16)
    left = amount - first.astype(jnp.float32)
    second = left.astype(jnp.bfloat16)
    third = (left - second.astype(jnp.float32)).astype(jnp.bfloat16)
    line = lax.broadcasted_iota(jnp.int32, (depth * rows, entries), 0) == cell // width
    lane_hit = lax.broadcasted_iota(jnp.int32, (width, entries), 0) == lax.rem(cell, width)
    line = jnp.where(line, 1.0, 0.0).astype(jnp.bfloat16)
    total = jnp.zeros((depth * rows, width), jnp.float32)
    for part in (third, second, first):
        spread = jnp.where(lane_hit, part.astype(jnp.float32), 0.0).astype(jnp.bfloat16)
        total = total + lax.dot_general(
            line, spread, (((1,), (1,)), ((), ())), preferred_element_type=jnp.float32
        )
    for z in range(depth):
        wgrid[z] = total[z * rows : (z + 1) * rows]

    loads[2].wait()

    def field(k, c, z):
        return sv[k, c, z].astype(jnp.float32)

    for k in range(steps):
        acc = jnp.zeros((rows, width), jnp.float32)
        for z in range(depth):
            square = jnp.zeros((rows, width), jnp.float32)
            for c in range(comps):
                f = field(k, c, z)
                square = square + f * f
            acc = acc + wgrid[z] * square
        pw_out[k : k + 1, :] = jnp.sum(acc, 0, keepdims=True)

    greeted = (n_lat - 1) + (n_ha - 1) * (1 + lat_dn.astype(jnp.int32) + lat_up.astype(jnp.int32))
    pl.semaphore_wait(barrier, greeted)

    over_ha = [
        exchange(pw_out, pw_ha.at[d - 1], (lat, lax.rem(ha + d, n_ha))) for d in range(1, n_ha)
    ]

    loads[3].wait()
    loads[4].wait()

    def material(z):
        label = lb[z]
        eps = jnp.full((rows, width), eps_table[0], jnp.float32)
        chi = jnp.full((rows, width), 3.0 * chi_table[0], jnp.float32)
        for region in range(1, regions):
            member = label == region
            eps = jnp.where(member, eps_table[region], eps)
            chi = jnp.where(member, 3.0 * chi_table[region], chi)
        return eps, chi

    last = steps - 1
    for z in reversed(range(depth)):
        eps, chi = material(z)
        for c in range(comps):
            f = field(last, c, z)
            inverse = 1.0 / (eps + chi * f * f)
            plain = e[c, z] * inverse
            driven = wgrid[z] * f * inverse
            ab[0, c, z] = plain
            ab[1, c, z] = driven
            if c > 0:
                slot = (c - 1) * depth + z
                rab_out[slot : slot + 1, :] = plain[rows - 1 : rows]
                slot = slot + 2 * depth
                rab_out[slot : slot + 1, :] = driven[rows - 1 : rows]

    zab_in = exchange(ab.at[:, pl.ds(0, 2), depth - 1], zab, (lat, ha_next), ha_up, ha_dn)
    rab_in = exchange(rab_out, rab, (lat_next, ha), lat_up, lat_dn)

    for arrive in over_ha:
        arrive()
    power_rows = pw_out[...]
    for d in range(1, n_ha):
        power_rows = power_rows + pw_ha[d - 1]
    pw_sum[...] = power_rows
    over_lat = [
        exchange(pw_sum, pw_lat.at[d - 1], (lax.rem(lat + d, n_lat), ha)) for d in range(1, n_lat)
    ]

    loads[5].wait()
    dens_lo_in = exchange(
        dens.at[pl.ds(rows - 2 * RADIUS, 2 * RADIUS)], dens_lo, (lat_next, ha), lat_up, lat_dn
    )
    dens_hi_in = exchange(
        dens.at[pl.ds(0, 2 * RADIUS)], dens_hi, (lat_prev, ha), lat_dn, lat_up
    )

    for k in range(last):
        for z in range(depth):
            eps, chi = material(z)
            for c in range(comps):
                f = field(k, c, z)
                rinv[k, c, z] = 1.0 / (eps + chi * f * f)

    for arrive in over_lat:
        arrive()
    for d in range(1, n_lat):
        power_rows = power_rows + pw_lat[d - 1]
    count_all = entries * n_lat * n_ha
    power = jnp.sum(power_rows, 1, keepdims=True) / count_all + epsilon
    inverse_power = 1.0 / power

    lane = lax.broadcasted_iota(jnp.int32, (rows, width), 1)
    row = lax.broadcasted_iota(jnp.int32, (rows, width), 0)

    def y_lower(v):
        return jnp.where(lane == 0, 0.0, pltpu.roll(v, 1, 1))

    def y_upper(v):
        return jnp.where(lane == width - 1, 0.0, pltpu.roll(v, width - 1, 1))

    def x_lower(v, edge):
        return jnp.where(row == 0, edge, pltpu.roll(v, 1, 0))

    def x_upper(v, edge):
        return jnp.where(row == rows - 1, edge, pltpu.roll(v, rows - 1, 0))

    def add_plane(k, z, values, acc):
        inner = jnp.zeros((rows, width), jnp.float32)
        for c in range(comps):
            inner = inner + values[c] * field(k, c, z)
        return acc + jnp.where(lb[z] == 0, inner, 0.0)

    acc = jnp.zeros((rows, width), jnp.float32)
    h_prev = h0
    for k in reversed(range(steps)):
        gain = inverse_power[k : k + 1, :]
        if k == last:
            for z in range(depth):
                values = [ab[0, c, z] + gain * ab[1, c, z] for c in range(comps)]
                for c in range(comps):
                    s[k, c, z] = values[c]
                acc = add_plane(k, z, values, acc)
            rab_in()
            low_rows = rab[pl.ds(0, 2 * depth), :] + gain * rab[pl.ds(2 * depth, 2 * depth), :]
            loads[6].wait()
        else:
            rl_in()
            low_rows = rl[k]

        def lower_layer(z, below_x, below_y):
            sx, sy, sz = s[k, 0, z], s[k, 1, z], s[k, 2, z]
            edge_y = low_rows[z : z + 1]
            edge_z = low_rows[depth + z : depth + z + 1]
            curl_x = sz - y_lower(sz) - (sy - below_y)
            curl_y = sx - below_x - (sz - x_lower(sz, edge_z))
            curl_z = sy - x_lower(sy, edge_y) - (sx - y_lower(sx))
            new = (
                h_prev_at(0, z) - time_step * curl_x,
                h_prev_at(1, z) - time_step * curl_y,
                h_prev_at(2, z) - time_step * curl_z,
            )
            for c in range(comps):
                hh[k, c, z] = new[c]
            ru_out[k, z : z + 1, :] = new[1][0:1]
            ru_out[k, depth + z : depth + z + 1, :] = new[2][0:1]

        def h_prev_at(c, z):
            return h0[c, z] if k == last else hh[k + 1, c, z]

        for z in range(1, depth):
            lower_layer(z, s[k, 0, z - 1], s[k, 1, z - 1])
        if k == last:
            zab_in()
            lower_layer(0, zab[0, 0] + gain * zab[1, 0], zab[0, 1] + gain * zab[1, 1])
        else:
            zl_in()
            lower_layer(0, zl[k, 0], zl[k, 1])

        zu_in = exchange(hh.at[k, pl.ds(0, 2), 0], zu.at[k], (lat, ha_prev), ha_dn, ha_up)
        ru_in = exchange(ru_out.at[k], ru.at[k], (lat_prev, ha), lat_dn, lat_up)

        if k == last:
            dens_lo_in()
            dens_hi_in()
            extended = jnp.concatenate([dens_lo[...], dens[...], dens_hi[...]], 0)
            filtered = filter_rows(extended, rows + 2 * RADIUS)
            slope = jnp.tanh(sharpness * (filtered - threshold))
            deriv[...] = (
                sharpness
                * (1.0 - slope * slope)
                / (jnp.tanh(sharpness * threshold) + jnp.tanh(sharpness * (1.0 - threshold)))
            )
        if k == 0:
            store_h = pltpu.make_async_copy(hh.at[0], out_h, local_sem.at[len(loads)])
            store_h.start()
            for arrive in plane_in:
                arrive()
            middle = plane[...]
            head = plane_lo[0]
            tail = plane_hi[0]
            for d in range(1, n_ha):
                middle = middle + plane_ha[d - 1]
                head = head + plane_lo[d]
                tail = tail + plane_hi[d]
            product = jnp.concatenate([head, middle, tail], 0) * deriv[...]
            grad[...] = filter_rows(product, rows)
            store_g = pltpu.make_async_copy(grad, out_g, local_sem.at[len(loads) + 1])
            store_g.start()

        ru_in()
        high_rows = ru[k]

        def upper_layer(z, above_x, above_y):
            hx, hy, hz = hh[k, 0, z], hh[k, 1, z], hh[k, 2, z]
            edge_y = high_rows[z : z + 1]
            edge_z = high_rows[depth + z : depth + z + 1]
            curl_x = y_upper(hz) - hz - (above_y - hy)
            curl_y = above_x - hx - (x_upper(hz, edge_z) - hz)
            curl_z = x_upper(hy, edge_y) - hy - (y_upper(hx) - hx)
            curl = (curl_x, curl_y, curl_z)
            values = []
            for c in range(comps):
                now = e[c, z] + time_step * curl[c]
                if k == last:
                    now = now + gain * (wgrid[z] * field(k, c, z))
                if k > 0:
                    after = inverse_power[k - 1 : k, :]
                    now = now + after * (wgrid[z] * field(k - 1, c, z))
                    value = now * rinv[k - 1, c, z]
                    s[k - 1, c, z] = value
                    values.append(value)
                    if c > 0:
                        slot = (c - 1) * depth + z
                        rl_out[k - 1, slot : slot + 1, :] = value[rows - 1 : rows]
                e[c, z] = now
            return values

        for z in range(depth):
            if z == depth - 1:
                zu_in()
                values = upper_layer(z, zu[k, 0], zu[k, 1])
            else:
                values = upper_layer(z, hh[k, 0, z + 1], hh[k, 1, z + 1])
            if k > 0:
                acc = add_plane(k - 1, z, values, acc)

        if k > 0:
            zl_in = exchange(
                s.at[k - 1, pl.ds(0, 2), depth - 1], zl.at[k - 1], (lat, ha_next), ha_up, ha_dn
            )
            rl_in = exchange(rl_out.at[k - 1], rl.at[k - 1], (lat_next, ha), lat_up, lat_dn)
        if k == 1:
            plane[...] = acc
            plane_in = []
            for d in range(n_ha):
                other = lax.rem(ha + d, n_ha)
                if d > 0:
                    plane_in.append(exchange(plane, plane_ha.at[d - 1], (lat, other)))
                plane_in.append(
                    exchange(
                        plane.at[pl.ds(rows - RADIUS, RADIUS)],
                        plane_lo.at[d],
                        (lat_next, other),
                        lat_up,
                        lat_dn,
                    )
                )
                plane_in.append(
                    exchange(
                        plane.at[pl.ds(0, RADIUS)],
                        plane_hi.at[d],
                        (lat_prev, other),
                        lat_dn,
                        lat_up,
                    )
                )

    store_e = pltpu.make_async_copy(e, out_e, local_sem.at[len(loads) + 2])
    store_e.start()
    for finish in issued:
        finish()
    store_h.wait()
    store_g.wait()
    store_e.wait()


def body(
    adjoint_e, adjoint_h, saved_e, labels, eps_table, chi_table, density, mon_cells, mon_weight
):
    n_lat, n_ha = lax.axis_size("lat"), lax.axis_size("ha")
    steps, comps, depth, rows, width = saved_e.shape
    entries = mon_cells.shape[0]
    f32 = jnp.float32
    block = (comps, depth, rows, width)
    copies = (n_ha - 1) + (n_lat - 1) + 4 + 4 * steps - 2 + 3 * n_ha - 1
    anywhere = pl.BlockSpec(memory_space=pl.ANY)
    scalars = pl.BlockSpec(memory_space=pltpu.SMEM)
    scratch = [
        pltpu.VMEM(block, f32),
        pltpu.VMEM(block, f32),
        pltpu.VMEM(saved_e.shape, saved_e.dtype),
        pltpu.VMEM(labels.shape, labels.dtype),
        pltpu.VMEM((rows, width), f32),
        pltpu.VMEM((1, entries), mon_cells.dtype),
        pltpu.VMEM((1, entries), f32),
        pltpu.VMEM((depth, rows, width), f32),
        pltpu.VMEM((2,) + block, f32),
        pltpu.VMEM((steps,) + block, f32),
        pltpu.VMEM((steps,) + block, f32),
        pltpu.VMEM((max(steps - 1, 1),) + block, f32),
        pltpu.VMEM((rows, width), f32),
        pltpu.VMEM((rows, width), f32),
        pltpu.VMEM((2 * RADIUS, width), f32),
        pltpu.VMEM((2 * RADIUS, width), f32),
        pltpu.VMEM((rows + 2 * RADIUS, width), f32),
        pltpu.VMEM((2, 2, rows, width), f32),
        pltpu.VMEM((4 * depth, width), f32),
        pltpu.VMEM((4 * depth, width), f32),
        pltpu.VMEM((steps, 2, rows, width), f32),
        pltpu.VMEM((steps, 2 * depth, width), f32),
        pltpu.VMEM((steps, 2 * depth, width), f32),
        pltpu.VMEM((steps, 2, rows, width), f32),
        pltpu.VMEM((steps, 2 * depth, width), f32),
        pltpu.VMEM((steps, 2 * depth, width), f32),
        pltpu.VMEM((steps, width), f32),
        pltpu.VMEM((max(n_ha - 1, 1), steps, width), f32),
        pltpu.VMEM((steps, width), f32),
        pltpu.VMEM((max(n_lat - 1, 1), steps, width), f32),
        pltpu.VMEM((max(n_ha - 1, 1), rows, width), f32),
        pltpu.VMEM((n_ha, RADIUS, width), f32),
        pltpu.VMEM((n_ha, RADIUS, width), f32),
        pltpu.SemaphoreType.DMA((10,)),
        pltpu.SemaphoreType.DMA((copies,)),
        pltpu.SemaphoreType.DMA((copies,)),
    ]
    return pl.pallas_call(
        functools.partial(kernel, n_lat, n_ha),
        out_shape=(
            jax.ShapeDtypeStruct(block, f32),
            jax.ShapeDtypeStruct(block, f32),
            jax.ShapeDtypeStruct((rows, width), f32),
        ),
        in_specs=[anywhere] * 4 + [scalars] * 2 + [anywhere] * 3,
        out_specs=(anywhere, anywhere, anywhere),
        scratch_shapes=scratch,
        compiler_params=pltpu.CompilerParams(
            collective_id=0, has_side_effects=True, vmem_limit_bytes=40 * 2**20
        ),
    )(
        adjoint_e,
        adjoint_h,
        saved_e,
        labels,
        eps_table,
        chi_table,
        density,
        mon_cells.reshape(1, entries),
        mon_weight.reshape(1, entries),
    )


def solution(mesh):
    return jax.shard_map(
        body,
        mesh=mesh,
        in_specs=(
            P(None, "ha", "lat", None),
            P(None, "ha", "lat", None),
            P(None, None, "ha", "lat", None),
            P("ha", "lat", None),
            P(),
            P(),
            P("lat", None),
            P(("lat", "ha")),
            P(("lat", "ha")),
        ),
        out_specs=(P(None, "ha", "lat", None), P(None, "ha", "lat", None), P("lat", None)),
        check_vma=False,
    )
```

```python
import functools

import jax
import jax.numpy as jnp
from jax import lax
from jax.experimental import pallas as pl
from jax.experimental.pallas import tpu as pltpu
from jax.sharding import PartitionSpec as P

RADIUS = 16

sharpness = 8.0
threshold = 0.5
time_step = 0.5
epsilon = 1e-05

MESH = pl.DeviceIdType.MESH


def cone(offset):
    return jnp.maximum(RADIUS + 1 - jnp.abs(offset), 0).astype(jnp.float32) / (RADIUS + 1) ** 2


def filter_rows(padded, rows):
    width = padded.shape[1]
    i = lax.broadcasted_iota(jnp.int32, (width, width), 0)
    j = lax.broadcasted_iota(jnp.int32, (width, width), 1)
    smoothed = jnp.dot(
        padded, cone(i - j), precision=lax.Precision.HIGHEST, preferred_element_type=jnp.float32
    )
    row_out = lax.broadcasted_iota(jnp.int32, (rows, rows + 2 * RADIUS), 0)
    row_in = lax.broadcasted_iota(jnp.int32, (rows, rows + 2 * RADIUS), 1)
    return jnp.dot(
        cone(row_in - RADIUS - row_out),
        smoothed,
        precision=lax.Precision.HIGHEST,
        preferred_element_type=jnp.float32,
    )


def kernel(
    n_lat,
    n_ha,
    adj_e,
    adj_h,
    saved,
    labels,
    eps_table,
    chi_table,
    density,
    cells,
    weight,
    out_e,
    out_h,
    out_g,
    e,
    h0,
    sv,
    lb,
    dens,
    cl,
    wt,
    wgrid,
    s,
    hh,
    rinv,
    plane,
    dens_lo,
    dens_hi,
    deriv,
    hz,
    hr_out,
    hr,
    zl,
    zu,
    rl_out,
    rl,
    ru_out,
    ru,
    ca_out,
    ca,
    cb_out,
    cb,
    pw_out,
    pw_in,
    plane_ha,
    plane_lo,
    plane_hi,
    local_sem,
    send_sem,
    recv_sem,
):
    steps, comps, depth, rows, width = sv.shape
    regions = eps_table.shape[0]
    entries = cl.shape[1]
    last = steps - 1
    devices = n_lat * n_ha
    lat = lax.axis_index("lat")
    ha = lax.axis_index("ha")
    lat_dn, lat_up = lat > 0, lat < n_lat - 1
    ha_dn, ha_up = ha > 0, ha < n_ha - 1
    lat_prev, lat_next = jnp.maximum(lat - 1, 0), jnp.minimum(lat + 1, n_lat - 1)
    ha_prev, ha_next = jnp.maximum(ha - 1, 0), jnp.minimum(ha + 1, n_ha - 1)

    pairs = [
        (cells, cl),
        (weight, wt),
        (saved, sv),
        (labels, lb),
        (adj_h, h0),
        (adj_e, e),
        (density, dens),
    ]
    loads = [pltpu.make_async_copy(a, b, local_sem.at[i]) for i, (a, b) in enumerate(pairs)]
    for load in loads:
        load.start()

    barrier = pltpu.get_barrier_semaphore()

    def peer(d):
        there = lax.rem(lat * n_ha + ha + d, devices)
        return (lax.div(there, n_ha), lax.rem(there, n_ha))

    for d in range(1, devices):
        pl.semaphore_signal(barrier, inc=1, device_id=peer(d), device_id_type=MESH)

    issued = []

    def exchange(src, dst, target, sends=None, receives=None):
        index = len(issued)

        def copy():
            return pltpu.make_async_remote_copy(
                src_ref=src,
                dst_ref=dst,
                send_sem=send_sem.at[index],
                recv_sem=recv_sem.at[index],
                device_id=target,
                device_id_type=MESH,
            )

        def guarded(condition, action):
            if condition is None:
                action()
            else:
                pl.when(condition)(action)

        issued.append(lambda: guarded(sends, lambda: copy().wait_send()))
        guarded(sends, lambda: copy().start())

        def arrive():
            guarded(receives, lambda: copy().wait_recv())
            if receives is not None:

                @pl.when(jnp.logical_not(receives))
                def _():
                    dst[...] = jnp.zeros(dst.shape, dst.dtype)

        return arrive

    loads[0].wait()
    loads[1].wait()
    cell = cl[...]
    amount = wt[...]
    first = amount.astype(jnp.bfloat16)
    left = amount - first.astype(jnp.float32)
    second = left.astype(jnp.bfloat16)
    third = (left - second.astype(jnp.float32)).astype(jnp.bfloat16)
    line = lax.broadcasted_iota(jnp.int32, (depth * rows, entries), 0) == cell // width
    lane_hit = lax.broadcasted_iota(jnp.int32, (width, entries), 0) == lax.rem(cell, width)
    line = jnp.where(line, 1.0, 0.0).astype(jnp.bfloat16)
    total = jnp.zeros((depth * rows, width), jnp.float32)
    for part in (third, second, first):
        spread = jnp.where(lane_hit, part.astype(jnp.float32), 0.0).astype(jnp.bfloat16)
        total = total + lax.dot_general(
            line, spread, (((1,), (1,)), ((), ())), preferred_element_type=jnp.float32
        )
    for z in range(depth):
        wgrid[z] = total[z * rows : (z + 1) * rows]

    loads[2].wait()

    def field(k, c, z):
        return sv[k, c, z].astype(jnp.float32)

    for k in range(steps):
        acc = jnp.zeros((rows, width), jnp.float32)
        for z in range(depth):
            square = jnp.zeros((rows, width), jnp.float32)
            for c in range(comps):
                f = field(k, c, z)
                square = square + f * f
            acc = acc + wgrid[z] * square
        pw_out[k : k + 1, :] = jnp.sum(acc, 0, keepdims=True)

    pl.semaphore_wait(barrier, devices - 1)
    power_in = [exchange(pw_out, pw_in.at[d - 1], peer(d)) for d in range(1, devices)]

    loads[4].wait()
    for c in range(1, comps):
        for z in range(depth):
            slot = (c - 1) * depth + z
            hr_out[slot : slot + 1, :] = h0[c, z, 0:1]
    hz_in = exchange(h0.at[pl.ds(0, 2), 0], hz.at[steps], (lat, ha_prev), ha_dn, ha_up)
    hr_in = exchange(hr_out, hr.at[steps], (lat_prev, ha), lat_dn, lat_up)
    loads[6].wait()
    dens_lo_in = exchange(
        dens.at[pl.ds(rows - 2 * RADIUS, 2 * RADIUS)], dens_lo, (lat_next, ha), lat_up, lat_dn
    )
    dens_hi_in = exchange(
        dens.at[pl.ds(0, 2 * RADIUS)], dens_hi, (lat_prev, ha), lat_dn, lat_up
    )

    loads[3].wait()
    for z in range(depth):
        label = lb[z]
        eps = jnp.full((rows, width), eps_table[0], jnp.float32)
        chi = jnp.full((rows, width), 3.0 * chi_table[0], jnp.float32)
        for region in range(1, regions):
            member = label == region
            eps = jnp.where(member, eps_table[region], eps)
            chi = jnp.where(member, 3.0 * chi_table[region], chi)
        for k in range(steps):
            for c in range(comps):
                f = field(k, c, z)
                rinv[k, c, z] = 1.0 / (eps + chi * f * f)

    loads[5].wait()
    for arrive in power_in:
        arrive()
    power_rows = pw_out[...]
    for d in range(1, devices):
        power_rows = power_rows + pw_in[d - 1]
    power = jnp.sum(power_rows, 1, keepdims=True) / (entries * devices) + epsilon
    inverse_power = 1.0 / power

    lane = lax.broadcasted_iota(jnp.int32, (rows, width), 1)
    row = lax.broadcasted_iota(jnp.int32, (rows, width), 0)
    lane_few = lax.broadcasted_iota(jnp.int32, (depth, width), 1)
    inside_ha = ha_up.astype(jnp.float32)
    inside_lat = lat_up.astype(jnp.float32)

    def y_lower(v):
        return jnp.where(lane == 0, 0.0, pltpu.roll(v, 1, 1))

    def y_lower_few(v):
        return jnp.where(lane_few == 0, 0.0, pltpu.roll(v, 1, 1))

    def y_upper(v):
        return jnp.where(lane == width - 1, 0.0, pltpu.roll(v, width - 1, 1))

    def x_lower(v, edge):
        return jnp.where(row == 0, edge, pltpu.roll(v, 1, 0))

    def x_upper(v, edge):
        return jnp.where(row == rows - 1, edge, pltpu.roll(v, rows - 1, 0))

    def scale_layer(k, z, fields, acc):
        gain = inverse_power[k : k + 1, :]
        inner = jnp.zeros((rows, width), jnp.float32)
        for c in range(comps):
            f = field(k, c, z)
            now = fields[c] + gain * (wgrid[z] * f)
            value = now * rinv[k, c, z]
            e[c, z] = now
            s[k, c, z] = value
            inner = inner + value * f
            slot = c * depth + z
            ru_out[k, slot : slot + 1, :] = value[0:1]
            if c > 0:
                slot = slot - depth
                rl_out[k, slot : slot + 1, :] = value[rows - 1 : rows]
            if c == 0 and z == depth - 1:
                ca_out[k] = value[0:1]
            if c == 2 and z == 0:
                cb_out[k] = value[rows - 1 : rows]
        return acc + jnp.where(lb[z] == 0, inner, 0.0)

    def send_bottom(k):
        return exchange(s.at[k, :, 0], zu.at[k], (lat, ha_prev), ha_dn, ha_up)

    def send_top(k):
        return exchange(s.at[k, pl.ds(0, 2), depth - 1], zl.at[k], (lat, ha_next), ha_up, ha_dn)

    def send_rows(k):
        return (
            exchange(rl_out.at[k], rl.at[k], (lat_next, ha), lat_up, lat_dn),
            exchange(ru_out.at[k], ru.at[k], (lat_prev, ha), lat_dn, lat_up),
            exchange(
                ca_out.at[k],
                ca.at[k],
                (lat_prev, ha_next),
                jnp.logical_and(lat_dn, ha_up),
                jnp.logical_and(lat_up, ha_dn),
            ),
            exchange(
                cb_out.at[k],
                cb.at[k],
                (lat_next, ha_prev),
                jnp.logical_and(lat_up, ha_dn),
                jnp.logical_and(lat_dn, ha_up),
            ),
        )

    acc = jnp.zeros((rows, width), jnp.float32)
    order = [0] + ([depth - 1] if depth > 1 else []) + list(range(1, depth - 1))
    for z in order:
        acc = scale_layer(last, z, [e[c, z] for c in range(comps)], acc)
        if z == 0:
            zu_in = send_bottom(last)
        if z == depth - 1:
            zl_in = send_top(last)
    rl_in, ru_in, ca_in, cb_in = send_rows(last)

    dens_lo_in()
    dens_hi_in()
    extended = jnp.concatenate([dens_lo[...], dens[...], dens_hi[...]], 0)
    filtered = filter_rows(extended, rows + 2 * RADIUS)
    slope = jnp.tanh(sharpness * (filtered - threshold))
    deriv[...] = (
        sharpness
        * (1.0 - slope * slope)
        / (jnp.tanh(sharpness * threshold) + jnp.tanh(sharpness * (1.0 - threshold)))
    )
    hz_in()
    hr_in()

    for k in reversed(range(steps)):

        def before(c, z):
            return h0[c, z] if k == last else hh[k + 1, c, z]

        def put(c, z, value):
            if k == 0:
                out_h[c, z] = value
            else:
                hh[k, c, z] = value

        def after(c, z):
            return out_h[c, z] if k == 0 else hh[k, c, z]

        def lower_layer(z, below_x, below_y):
            sx, sy, sz = s[k, 0, z], s[k, 1, z], s[k, 2, z]
            edge_y = low_rows[z : z + 1]
            edge_z = low_rows[depth + z : depth + z + 1]
            curl_x = sz - y_lower(sz) - (sy - below_y)
            curl_y = sx - below_x - (sz - x_lower(sz, edge_z))
            curl_z = sy - x_lower(sy, edge_y) - (sx - y_lower(sx))
            put(0, z, before(0, z) - time_step * curl_x)
            put(1, z, before(1, z) - time_step * curl_y)
            put(2, z, before(2, z) - time_step * curl_z)

        rl_in()
        low_rows = rl[k]
        for z in range(1, depth):
            lower_layer(z, s[k, 0, z - 1], s[k, 1, z - 1])

        ru_in()
        ca_in()
        hx_rows = ru[k, pl.ds(0, depth), :]
        hy_rows = ru[k, pl.ds(depth, depth), :]
        hz_rows = ru[k, pl.ds(2 * depth, depth), :]
        own_y = jnp.concatenate([s[k, 1, z, rows - 1 : rows] for z in range(depth)], 0)
        own_z = jnp.concatenate([s[k, 2, z, rows - 1 : rows] for z in range(depth)], 0)
        under = ca[k]
        if depth > 1:
            under = jnp.concatenate([under, hx_rows[0 : depth - 1]], 0)
        old_y = hr[k + 1, pl.ds(0, depth), :]
        old_z = hr[k + 1, pl.ds(depth, depth), :]
        high_y = old_y - time_step * (hx_rows - under - (hz_rows - own_z))
        high_z = old_z - time_step * (hy_rows - own_y - (hx_rows - y_lower_few(hx_rows)))
        high_y = high_y * inside_lat
        high_z = high_z * inside_lat
        hr[k, pl.ds(0, depth), :] = high_y
        hr[k, pl.ds(depth, depth), :] = high_z

        zl_in()
        lower_layer(0, zl[k, 0], zl[k, 1])

        def upper_layer(z, above_x, above_y):
            hx, hy, hv = after(0, z), after(1, z), after(2, z)
            edge_y = high_y[z : z + 1]
            edge_z = high_z[z : z + 1]
            curl_x = y_upper(hv) - hv - (above_y - hy)
            curl_y = above_x - hx - (x_upper(hv, edge_z) - hv)
            curl_z = x_upper(hy, edge_y) - hy - (y_upper(hx) - hx)
            return (
                e[0, z] + time_step * curl_x,
                e[1, z] + time_step * curl_y,
                e[2, z] + time_step * curl_z,
            )

        def finish_layer(z, above_x, above_y, acc):
            fields = upper_layer(z, above_x, above_y)
            if k > 0:
                return scale_layer(k - 1, z, fields, acc)
            for c in range(comps):
                out_e[c, z] = fields[c]
            return acc

        for z in range(depth - 1):
            acc = finish_layer(z, after(0, z + 1), after(1, z + 1), acc)
            if z == 0 and k > 0:
                zu_next = send_bottom(k - 1)

        zu_in()
        cb_in()
        top = depth - 1
        nx, ny, nz = zu[k, 0], zu[k, 1], zu[k, 2]
        above_x = hz[k + 1, 0] - time_step * (nz - y_lower(nz) - (ny - s[k, 1, top]))
        above_y = hz[k + 1, 1] - time_step * (nx - s[k, 0, top] - (nz - x_lower(nz, cb[k])))
        above_x = above_x * inside_ha
        above_y = above_y * inside_ha
        hz[k, 0] = above_x
        hz[k, 1] = above_y
        acc = finish_layer(top, above_x, above_y, acc)

        if k > 0:
            if depth == 1:
                zu_next = send_bottom(k - 1)
            zu_in = zu_next
            zl_in = send_top(k - 1)
            rl_in, ru_in, ca_in, cb_in = send_rows(k - 1)
        if k == min(1, last):
            plane[...] = acc
            plane_in = []
            for d in range(n_ha):
                other = lax.rem(ha + d, n_ha)
                if d > 0:
                    plane_in.append(exchange(plane, plane_ha.at[d - 1], (lat, other)))
                plane_in.append(
                    exchange(
                        plane.at[pl.ds(rows - RADIUS, RADIUS)],
                        plane_lo.at[d],
                        (lat_next, other),
                        lat_up,
                        lat_dn,
                    )
                )
                plane_in.append(
                    exchange(
                        plane.at[pl.ds(0, RADIUS)],
                        plane_hi.at[d],
                        (lat_prev, other),
                        lat_dn,
                        lat_up,
                    )
                )

    for arrive in plane_in:
        arrive()
    middle = plane[...]
    low = plane_lo[0]
    high = plane_hi[0]
    for d in range(1, n_ha):
        middle = middle + plane_ha[d - 1]
        low = low + plane_lo[d]
        high = high + plane_hi[d]
    product = jnp.concatenate([low, middle, high], 0) * deriv[...]
    out_g[...] = filter_rows(product, rows)
    for finish in issued:
        finish()


def store(e, h, g, out_e, out_h, out_g, sem):
    copies = [
        pltpu.make_async_copy(e, out_e, sem.at[0]),
        pltpu.make_async_copy(h, out_h, sem.at[1]),
        pltpu.make_async_copy(g, out_g, sem.at[2]),
    ]
    for copy in copies:
        copy.start()
    for copy in copies:
        copy.wait()


def body(
    adjoint_e, adjoint_h, saved_e, labels, eps_table, chi_table, density, mon_cells, mon_weight
):
    n_lat, n_ha = lax.axis_size("lat"), lax.axis_size("ha")
    steps, comps, depth, rows, width = saved_e.shape
    entries = mon_cells.shape[0]
    f32 = jnp.float32
    block = (comps, depth, rows, width)
    copies = (n_lat * n_ha - 1) + 4 + 6 * steps + 3 * n_ha - 1
    vmem = pl.BlockSpec(memory_space=pltpu.VMEM)
    hbm = pl.BlockSpec(memory_space=pltpu.HBM)
    scalars = pl.BlockSpec(memory_space=pltpu.SMEM)
    scratch = [
        pltpu.VMEM(block, f32),
        pltpu.VMEM(block, f32),
        pltpu.VMEM(saved_e.shape, saved_e.dtype),
        pltpu.VMEM(labels.shape, labels.dtype),
        pltpu.VMEM((rows, width), f32),
        pltpu.VMEM((1, entries), mon_cells.dtype),
        pltpu.VMEM((1, entries), f32),
        pltpu.VMEM((depth, rows, width), f32),
        pltpu.VMEM((steps,) + block, f32),
        pltpu.VMEM((steps,) + block, f32),
        pltpu.VMEM((steps,) + block, f32),
        pltpu.VMEM((rows, width), f32),
        pltpu.VMEM((2 * RADIUS, width), f32),
        pltpu.VMEM((2 * RADIUS, width), f32),
        pltpu.VMEM((rows + 2 * RADIUS, width), f32),
        pltpu.VMEM((steps + 1, 2, rows, width), f32),
        pltpu.VMEM((2 * depth, width), f32),
        pltpu.VMEM((steps + 1, 2 * depth, width), f32),
        pltpu.VMEM((steps, 2, rows, width), f32),
        pltpu.VMEM((steps, 3, rows, width), f32),
        pltpu.VMEM((steps, 2 * depth, width), f32),
        pltpu.VMEM((steps, 2 * depth, width), f32),
        pltpu.VMEM((steps, 3 * depth, width), f32),
        pltpu.VMEM((steps, 3 * depth, width), f32),
        pltpu.VMEM((steps, 1, width), f32),
        pltpu.VMEM((steps, 1, width), f32),
        pltpu.VMEM((steps, 1, width), f32),
        pltpu.VMEM((steps, 1, width), f32),
        pltpu.VMEM((steps, width), f32),
        pltpu.VMEM((n_lat * n_ha - 1, steps, width), f32),
        pltpu.VMEM((max(n_ha - 1, 1), rows, width), f32),
        pltpu.VMEM((n_ha, RADIUS, width), f32),
        pltpu.VMEM((n_ha, RADIUS, width), f32),
        pltpu.SemaphoreType.DMA((7,)),
        pltpu.SemaphoreType.DMA((copies,)),
        pltpu.SemaphoreType.DMA((copies,)),
    ]
    results = pl.pallas_call(
        functools.partial(kernel, n_lat, n_ha),
        out_shape=(
            pltpu.VMEM(block, f32),
            pltpu.VMEM(block, f32),
            pltpu.VMEM((rows, width), f32),
        ),
        in_specs=[hbm] * 4 + [scalars] * 2 + [hbm] * 3,
        out_specs=(vmem, vmem, vmem),
        scratch_shapes=scratch,
        compiler_params=pltpu.CompilerParams(
            collective_id=0, has_side_effects=True, vmem_limit_bytes=63 * 2**20
        ),
    )(
        adjoint_e,
        adjoint_h,
        saved_e,
        labels,
        eps_table,
        chi_table,
        density,
        mon_cells.reshape(1, entries),
        mon_weight.reshape(1, entries),
    )
    return pl.pallas_call(
        store,
        out_shape=(
            jax.ShapeDtypeStruct(block, f32),
            jax.ShapeDtypeStruct(block, f32),
            jax.ShapeDtypeStruct((rows, width), f32),
        ),
        in_specs=[vmem] * 3,
        out_specs=(hbm, hbm, hbm),
        scratch_shapes=[pltpu.SemaphoreType.DMA((3,))],
    )(*results)


def solution(mesh):
    return jax.shard_map(
        body,
        mesh=mesh,
        in_specs=(
            P(None, "ha", "lat", None),
            P(None, "ha", "lat", None),
            P(None, None, "ha", "lat", None),
            P("ha", "lat", None),
            P(),
            P(),
            P("lat", None),
            P(("lat", "ha")),
            P(("lat", "ha")),
        ),
        out_specs=(P(None, "ha", "lat", None), P(None, "ha", "lat", None), P("lat", None)),
        check_vma=False,
    )
```

```python
import functools

import jax
import jax.numpy as jnp
from jax import lax
from jax.experimental import pallas as pl
from jax.experimental.pallas import tpu as pltpu
from jax.sharding import PartitionSpec as P

RADIUS = 16

sharpness = 8.0
threshold = 0.5
time_step = 0.5
epsilon = 1e-05

MESH = pl.DeviceIdType.MESH


def cone(offset):
    return jnp.maximum(RADIUS + 1 - jnp.abs(offset), 0).astype(jnp.float32) / (RADIUS + 1) ** 2


def filter_rows(padded, rows):
    width = padded.shape[1]
    i = lax.broadcasted_iota(jnp.int32, (width, width), 0)
    j = lax.broadcasted_iota(jnp.int32, (width, width), 1)
    smoothed = jnp.dot(
        padded, cone(i - j), precision=lax.Precision.HIGHEST, preferred_element_type=jnp.float32
    )
    row_out = lax.broadcasted_iota(jnp.int32, (rows, rows + 2 * RADIUS), 0)
    row_in = lax.broadcasted_iota(jnp.int32, (rows, rows + 2 * RADIUS), 1)
    return jnp.dot(
        cone(row_in - RADIUS - row_out),
        smoothed,
        precision=lax.Precision.HIGHEST,
        preferred_element_type=jnp.float32,
    )


def kernel(
    n_lat,
    n_ha,
    adj_e,
    adj_h,
    saved,
    labels,
    eps_table,
    chi_table,
    density,
    cells,
    weight,
    out_e,
    out_h,
    out_g,
    e,
    h0,
    sv,
    lb,
    dens,
    cl,
    wt,
    wgrid,
    s,
    hh,
    rinv,
    plane,
    dens_lo,
    dens_hi,
    deriv,
    hz_out,
    zl,
    zu,
    rl_out,
    rl,
    ru_out,
    ru,
    ca_out,
    ca,
    cb_out,
    cb,
    pw_out,
    pw_in,
    plane_ha,
    plane_lo,
    plane_hi,
    local_sem,
    send_sem,
    recv_sem,
):
    steps, comps, depth, rows, width = sv.shape
    regions = eps_table.shape[0]
    entries = cl.shape[1]
    last, top = steps - 1, depth - 1
    devices = n_lat * n_ha
    lat = lax.axis_index("lat")
    ha = lax.axis_index("ha")
    lat_dn, lat_up = lat > 0, lat < n_lat - 1
    ha_dn, ha_up = ha > 0, ha < n_ha - 1
    lat_prev, lat_next = jnp.maximum(lat - 1, 0), jnp.minimum(lat + 1, n_lat - 1)
    ha_prev, ha_next = jnp.maximum(ha - 1, 0), jnp.minimum(ha + 1, n_ha - 1)

    pairs = [
        (cells, cl),
        (weight, wt),
        (saved, sv),
        (labels, lb),
        (adj_h, h0),
        (adj_e, e),
        (density, dens),
    ]
    loads = [pltpu.make_async_copy(a, b, local_sem.at[i]) for i, (a, b) in enumerate(pairs)]
    for load in loads:
        load.start()

    barrier = pltpu.get_barrier_semaphore()

    def peer(d):
        there = lax.rem(lat * n_ha + ha + d, devices)
        return (lax.div(there, n_ha), lax.rem(there, n_ha))

    for d in range(1, devices):
        pl.semaphore_signal(barrier, inc=1, device_id=peer(d), device_id_type=MESH)

    issued = []

    def exchange(src, dst, target, sends=None, receives=None):
        index = len(issued)

        def copy():
            return pltpu.make_async_remote_copy(
                src_ref=src,
                dst_ref=dst,
                send_sem=send_sem.at[index],
                recv_sem=recv_sem.at[index],
                device_id=target,
                device_id_type=MESH,
            )

        def guarded(condition, action):
            if condition is None:
                action()
            else:
                pl.when(condition)(action)

        issued.append(lambda: guarded(sends, lambda: copy().wait_send()))
        guarded(sends, lambda: copy().start())

        def arrive():
            guarded(receives, lambda: copy().wait_recv())
            if receives is not None:

                @pl.when(jnp.logical_not(receives))
                def _():
                    dst[...] = jnp.zeros(dst.shape, dst.dtype)

        return arrive

    loads[0].wait()
    loads[1].wait()
    cell = cl[...]
    amount = wt[...]
    first = amount.astype(jnp.bfloat16)
    left = amount - first.astype(jnp.float32)
    second = left.astype(jnp.bfloat16)
    third = (left - second.astype(jnp.float32)).astype(jnp.bfloat16)
    line = lax.broadcasted_iota(jnp.int32, (depth * rows, entries), 0) == cell // width
    lane_hit = lax.broadcasted_iota(jnp.int32, (width, entries), 0) == lax.rem(cell, width)
    line = jnp.where(line, 1.0, 0.0).astype(jnp.bfloat16)
    total = jnp.zeros((depth * rows, width), jnp.float32)
    for part in (third, second, first):
        spread = jnp.where(lane_hit, part.astype(jnp.float32), 0.0).astype(jnp.bfloat16)
        total = total + lax.dot_general(
            line, spread, (((1,), (1,)), ((), ())), preferred_element_type=jnp.float32
        )
    for z in range(depth):
        wgrid[z] = total[z * rows : (z + 1) * rows]

    loads[2].wait()

    def field(k, c, z):
        return sv[k, c, z].astype(jnp.float32)

    for k in range(steps):
        acc = jnp.zeros((rows, width), jnp.float32)
        for z in range(depth):
            square = jnp.zeros((rows, width), jnp.float32)
            for c in range(comps):
                f = field(k, c, z)
                square = square + f * f
            acc = acc + wgrid[z] * square
        pw_out[k : k + 1, :] = jnp.sum(acc, 0, keepdims=True)

    pl.semaphore_wait(barrier, devices - 1)
    power_in = [exchange(pw_out, pw_in.at[d - 1], peer(d)) for d in range(1, devices)]

    loads[6].wait()
    dens_lo_in = exchange(
        dens.at[pl.ds(rows - 2 * RADIUS, 2 * RADIUS)], dens_lo, (lat_next, ha), lat_up, lat_dn
    )
    dens_hi_in = exchange(
        dens.at[pl.ds(0, 2 * RADIUS)], dens_hi, (lat_prev, ha), lat_dn, lat_up
    )

    loads[3].wait()
    for z in range(depth):
        label = lb[z]
        eps = jnp.full((rows, width), eps_table[0], jnp.float32)
        chi = jnp.full((rows, width), 3.0 * chi_table[0], jnp.float32)
        for region in range(1, regions):
            member = label == region
            eps = jnp.where(member, eps_table[region], eps)
            chi = jnp.where(member, 3.0 * chi_table[region], chi)
        for k in range(steps):
            for c in range(comps):
                f = field(k, c, z)
                rinv[k, c, z] = 1.0 / (eps + chi * f * f)

    loads[4].wait()
    loads[5].wait()
    for arrive in power_in:
        arrive()
    power_rows = pw_out[...]
    for d in range(1, devices):
        power_rows = power_rows + pw_in[d - 1]
    power = jnp.sum(power_rows, 1, keepdims=True) / (entries * devices) + epsilon
    inverse_power = 1.0 / power

    lane = lax.broadcasted_iota(jnp.int32, (rows, width), 1)
    row = lax.broadcasted_iota(jnp.int32, (rows, width), 0)
    inside_ha = ha_up.astype(jnp.float32)
    inside_lat = lat_up.astype(jnp.float32)

    def y_lower(v):
        return jnp.where(lane == 0, 0.0, pltpu.roll(v, 1, 1))

    def y_upper(v):
        return jnp.where(lane == width - 1, 0.0, pltpu.roll(v, width - 1, 1))

    def x_lower(v, edge):
        return jnp.where(row == 0, edge, pltpu.roll(v, 1, 0))

    def x_upper(v, edge):
        return jnp.where(row == rows - 1, edge, pltpu.roll(v, rows - 1, 0))

    def scale_layer(k, z, fields, acc):
        gain = inverse_power[k : k + 1, :]
        inner = jnp.zeros((rows, width), jnp.float32)
        for c in range(comps):
            f = field(k, c, z)
            now = fields[c] + gain * (wgrid[z] * f)
            value = now * rinv[k, c, z]
            e[c, z] = now
            s[k, c, z] = value
            inner = inner + value * f
            if c > 0:
                slot = (c - 1) * depth + z
                rl_out[k, slot : slot + 1, :] = value[rows - 1 : rows]
            if c == 0 and z == top:
                ca_out[k] = value[0:1]
            if c == 2 and z == 0:
                cb_out[k] = value[rows - 1 : rows]
        return acc + jnp.where(lb[z] == 0, inner, 0.0)

    def magnetic(k):
        return out_h if k == 0 else hh.at[k]

    def lower_layer(k, z):
        old = h0 if k == last else magnetic(k + 1)
        new = magnetic(k)
        sx, sy, sz = s[k, 0, z], s[k, 1, z], s[k, 2, z]
        curl_x = sz - y_lower(sz) - sy
        curl_y = sx - (sz - x_lower(sz, 0.0))
        curl_z = sy - x_lower(sy, 0.0) - (sx - y_lower(sx))
        if z > 0:
            curl_x = curl_x + s[k, 1, z - 1]
            curl_y = curl_y - s[k, 0, z - 1]
        values = (
            old[0, z] - time_step * curl_x,
            old[1, z] - time_step * curl_y,
            old[2, z] - time_step * curl_z,
        )
        for c in range(comps):
            new[c, z] = values[c]
            if z == 0 and c < 2:
                hz_out[k, c] = values[c]
            if c > 0:
                slot = (c - 1) * depth + z
                ru_out[k, slot : slot + 1, :] = values[c][0:1]

    def send_bottom(k):
        return exchange(hz_out.at[k], zu.at[k], (lat, ha_prev), ha_dn, ha_up)

    def send_top(k):
        return exchange(s.at[k, pl.ds(0, 2), top], zl.at[k], (lat, ha_next), ha_up, ha_dn)

    def send_edges(k):
        return (
            exchange(rl_out.at[k], rl.at[k], (lat_next, ha), lat_up, lat_dn),
            exchange(
                ca_out.at[k],
                ca.at[k],
                (lat_prev, ha_next),
                jnp.logical_and(lat_dn, ha_up),
                jnp.logical_and(lat_up, ha_dn),
            ),
            exchange(
                cb_out.at[k],
                cb.at[k],
                (lat_next, ha_prev),
                jnp.logical_and(lat_up, ha_dn),
                jnp.logical_and(lat_dn, ha_up),
            ),
        )

    def send_plane(acc):
        plane[...] = acc
        arrivals = []
        for d in range(n_ha):
            other = lax.rem(ha + d, n_ha)
            if d > 0:
                arrivals.append(exchange(plane, plane_ha.at[d - 1], (lat, other)))
            arrivals.append(
                exchange(
                    plane.at[pl.ds(rows - RADIUS, RADIUS)],
                    plane_lo.at[d],
                    (lat_next, other),
                    lat_up,
                    lat_dn,
                )
            )
            arrivals.append(
                exchange(
                    plane.at[pl.ds(0, RADIUS)],
                    plane_hi.at[d],
                    (lat_prev, other),
                    lat_dn,
                    lat_up,
                )
            )
        return arrivals

    acc = jnp.zeros((rows, width), jnp.float32)
    for z in [0] + list(range(top, 0, -1)):
        acc = scale_layer(last, z, [e[c, z] for c in range(comps)], acc)
        if z == 0:
            lower_layer(last, 0)
            zu_in = send_bottom(last)
        if z == top:
            zl_in = send_top(last)

    for k in reversed(range(steps)):
        rl_in, ca_in, cb_in = send_edges(k)
        if k == 0:
            plane_in = send_plane(acc)
        for z in range(1, depth):
            lower_layer(k, z)
        ru_in = exchange(ru_out.at[k], ru.at[k], (lat_prev, ha), lat_dn, lat_up)

        if k == last:
            dens_lo_in()
            dens_hi_in()
            extended = jnp.concatenate([dens_lo[...], dens[...], dens_hi[...]], 0)
            filtered = filter_rows(extended, rows + 2 * RADIUS)
            slope = jnp.tanh(sharpness * (filtered - threshold))
            deriv[...] = (
                sharpness
                * (1.0 - slope * slope)
                / (jnp.tanh(sharpness * threshold) + jnp.tanh(sharpness * (1.0 - threshold)))
            )

        new = magnetic(k)
        rl_in()
        for z in range(depth):
            new[1, z, 0:1] = new[1, z, 0:1] - time_step * rl[k, depth + z : depth + z + 1, :]
            new[2, z, 0:1] = new[2, z, 0:1] + time_step * rl[k, z : z + 1, :]

        ru_in()
        ca_in()
        own_y = jnp.concatenate([s[k, 1, z, rows - 1 : rows] for z in range(depth)], 0)
        own_z = jnp.concatenate([s[k, 2, z, rows - 1 : rows] for z in range(depth)], 0)
        high_y = (ru[k, pl.ds(0, depth), :] - time_step * own_z) * inside_lat
        high_z = (ru[k, pl.ds(depth, depth), :] + time_step * own_y) * inside_lat
        first_y = high_y[0:1] + time_step * inside_lat * ca[k]

        def finish_layer(z, above_x, above_y, acc):
            hx, hy, hv = new[0, z], new[1, z], new[2, z]
            edge_y = first_y if z == 0 else high_y[z : z + 1]
            edge_z = high_z[z : z + 1]
            curl_x = y_upper(hv) - hv - (above_y - hy)
            curl_y = above_x - hx - (x_upper(hv, edge_z) - hv)
            curl_z = x_upper(hy, edge_y) - hy - (y_upper(hx) - hx)
            fields = (
                e[0, z] + time_step * curl_x,
                e[1, z] + time_step * curl_y,
                e[2, z] + time_step * curl_z,
            )
            if k > 0:
                return scale_layer(k - 1, z, fields, acc)
            for c in range(comps):
                out_e[c, z] = fields[c]
            return acc

        for z in range(1, top):
            acc = finish_layer(z, new[0, z + 1], new[1, z + 1], acc)

        zl_in()
        new[0, 0] = new[0, 0] - time_step * zl[k, 1]
        new[1, 0] = new[1, 0] + time_step * zl[k, 0]
        if top > 0:
            acc = finish_layer(0, new[0, 1], new[1, 1], acc)
            if k > 0:
                lower_layer(k - 1, 0)
                zu_next = send_bottom(k - 1)

        zu_in()
        cb_in()
        above_x = zu[k, 0] - time_step * s[k, 1, top]
        above_y = zu[k, 1] + time_step * s[k, 0, top]
        above_y = above_y - jnp.where(row == 0, time_step * cb[k], 0.0)
        acc = finish_layer(top, above_x * inside_ha, above_y * inside_ha, acc)
        if k > 0:
            if top == 0:
                lower_layer(k - 1, 0)
                zu_next = send_bottom(k - 1)
            zu_in = zu_next
            zl_in = send_top(k - 1)

    for arrive in plane_in:
        arrive()
    middle = plane[...]
    low = plane_lo[0]
    high = plane_hi[0]
    for d in range(1, n_ha):
        middle = middle + plane_ha[d - 1]
        low = low + plane_lo[d]
        high = high + plane_hi[d]
    product = jnp.concatenate([low, middle, high], 0) * deriv[...]
    out_g[...] = filter_rows(product, rows)
    for finish in issued:
        finish()


def store(e, h, g, out_e, out_h, out_g, sem):
    copies = [
        pltpu.make_async_copy(e, out_e, sem.at[0]),
        pltpu.make_async_copy(h, out_h, sem.at[1]),
        pltpu.make_async_copy(g, out_g, sem.at[2]),
    ]
    for copy in copies:
        copy.start()
    for copy in copies:
        copy.wait()


def body(
    adjoint_e, adjoint_h, saved_e, labels, eps_table, chi_table, density, mon_cells, mon_weight
):
    n_lat, n_ha = lax.axis_size("lat"), lax.axis_size("ha")
    steps, comps, depth, rows, width = saved_e.shape
    entries = mon_cells.shape[0]
    f32 = jnp.float32
    block = (comps, depth, rows, width)
    copies = (n_lat * n_ha - 1) + 2 + 6 * steps + 3 * n_ha - 1
    vmem = pl.BlockSpec(memory_space=pltpu.VMEM)
    hbm = pl.BlockSpec(memory_space=pltpu.HBM)
    scalars = pl.BlockSpec(memory_space=pltpu.SMEM)
    scratch = [
        pltpu.VMEM(block, f32),
        pltpu.VMEM(block, f32),
        pltpu.VMEM(saved_e.shape, saved_e.dtype),
        pltpu.VMEM(labels.shape, labels.dtype),
        pltpu.VMEM((rows, width), f32),
        pltpu.VMEM((1, entries), mon_cells.dtype),
        pltpu.VMEM((1, entries), f32),
        pltpu.VMEM((depth, rows, width), f32),
        pltpu.VMEM((steps,) + block, f32),
        pltpu.VMEM((steps,) + block, f32),
        pltpu.VMEM((steps,) + block, f32),
        pltpu.VMEM((rows, width), f32),
        pltpu.VMEM((2 * RADIUS, width), f32),
        pltpu.VMEM((2 * RADIUS, width), f32),
        pltpu.VMEM((rows + 2 * RADIUS, width), f32),
        pltpu.VMEM((steps, 2, rows, width), f32),
        pltpu.VMEM((steps, 2, rows, width), f32),
        pltpu.VMEM((steps, 2, rows, width), f32),
        pltpu.VMEM((steps, 2 * depth, width), f32),
        pltpu.VMEM((steps, 2 * depth, width), f32),
        pltpu.VMEM((steps, 2 * depth, width), f32),
        pltpu.VMEM((steps, 2 * depth, width), f32),
        pltpu.VMEM((steps, 1, width), f32),
        pltpu.VMEM((steps, 1, width), f32),
        pltpu.VMEM((steps, 1, width), f32),
        pltpu.VMEM((steps, 1, width), f32),
        pltpu.VMEM((steps, width), f32),
        pltpu.VMEM((n_lat * n_ha - 1, steps, width), f32),
        pltpu.VMEM((max(n_ha - 1, 1), rows, width), f32),
        pltpu.VMEM((n_ha, RADIUS, width), f32),
        pltpu.VMEM((n_ha, RADIUS, width), f32),
        pltpu.SemaphoreType.DMA((7,)),
        pltpu.SemaphoreType.DMA((copies,)),
        pltpu.SemaphoreType.DMA((copies,)),
    ]
    results = pl.pallas_call(
        functools.partial(kernel, n_lat, n_ha),
        out_shape=(
            pltpu.VMEM(block, f32),
            pltpu.VMEM(block, f32),
            pltpu.VMEM((rows, width), f32),
        ),
        in_specs=[hbm] * 4 + [scalars] * 2 + [hbm] * 3,
        out_specs=(vmem, vmem, vmem),
        scratch_shapes=scratch,
        compiler_params=pltpu.CompilerParams(
            collective_id=0, has_side_effects=True, vmem_limit_bytes=63 * 2**20
        ),
    )(
        adjoint_e,
        adjoint_h,
        saved_e,
        labels,
        eps_table,
        chi_table,
        density,
        mon_cells.reshape(1, entries),
        mon_weight.reshape(1, entries),
    )
    return pl.pallas_call(
        store,
        out_shape=(
            jax.ShapeDtypeStruct(block, f32),
            jax.ShapeDtypeStruct(block, f32),
            jax.ShapeDtypeStruct((rows, width), f32),
        ),
        in_specs=[vmem] * 3,
        out_specs=(hbm, hbm, hbm),
        scratch_shapes=[pltpu.SemaphoreType.DMA((3,))],
        compiler_params=pltpu.CompilerParams(vmem_limit_bytes=2**20),
    )(*results)


def solution(mesh):
    return jax.shard_map(
        body,
        mesh=mesh,
        in_specs=(
            P(None, "ha", "lat", None),
            P(None, "ha", "lat", None),
            P(None, None, "ha", "lat", None),
            P("ha", "lat", None),
            P(),
            P(),
            P("lat", None),
            P(("lat", "ha")),
            P(("lat", "ha")),
        ),
        out_specs=(P(None, "ha", "lat", None), P(None, "ha", "lat", None), P("lat", None)),
        check_vma=False,
    )
```

```python
import functools

import jax
import jax.numpy as jnp
from jax import lax
from jax.experimental import pallas as pl
from jax.experimental.pallas import tpu as pltpu
from jax.sharding import PartitionSpec as P

RADIUS = 16

sharpness = 8.0
threshold = 0.5
time_step = 0.5
epsilon = 1e-05

MESH = pl.DeviceIdType.MESH


def cone(offset):
    return jnp.maximum(RADIUS + 1 - jnp.abs(offset), 0).astype(jnp.float32) / (RADIUS + 1) ** 2


def filter_rows(padded, rows):
    width = padded.shape[1]
    i = lax.broadcasted_iota(jnp.int32, (width, width), 0)
    j = lax.broadcasted_iota(jnp.int32, (width, width), 1)
    smoothed = jnp.dot(
        padded, cone(i - j), precision=lax.Precision.HIGHEST, preferred_element_type=jnp.float32
    )
    row_out = lax.broadcasted_iota(jnp.int32, (rows, rows + 2 * RADIUS), 0)
    row_in = lax.broadcasted_iota(jnp.int32, (rows, rows + 2 * RADIUS), 1)
    return jnp.dot(
        cone(row_in - RADIUS - row_out),
        smoothed,
        precision=lax.Precision.HIGHEST,
        preferred_element_type=jnp.float32,
    )


def kernel(
    n_lat,
    n_ha,
    adj_e,
    adj_h,
    saved,
    labels,
    eps_table,
    chi_table,
    density,
    cells,
    weight,
    out_e,
    out_h,
    out_g,
    e,
    h0,
    sv,
    lb,
    dens,
    cl,
    wt,
    wgrid,
    s,
    hh,
    rinv,
    plane,
    dens_lo,
    dens_hi,
    deriv,
    hz_out,
    zl,
    zu,
    rl_out,
    rl,
    ru_out,
    ru,
    ca_out,
    ca,
    cb_out,
    cb,
    pw_out,
    pw_in,
    pw_sum,
    pw_all,
    ab,
    pab,
    hzab_out,
    zuab,
    zlab,
    rlab_out,
    rlab,
    ruab_out,
    ruab,
    caab_out,
    caab,
    cbab_out,
    cbab,
    plane_ha,
    plane_lo,
    plane_hi,
    local_sem,
    send_sem,
    recv_sem,
):
    steps, comps, depth, rows, width = sv.shape
    regions = eps_table.shape[0]
    entries = cl.shape[1]
    last, top = steps - 1, depth - 1
    devices = n_lat * n_ha
    lat = lax.axis_index("lat")
    ha = lax.axis_index("ha")
    lat_dn, lat_up = lat > 0, lat < n_lat - 1
    ha_dn, ha_up = ha > 0, ha < n_ha - 1
    lat_prev, lat_next = jnp.maximum(lat - 1, 0), jnp.minimum(lat + 1, n_lat - 1)
    ha_prev, ha_next = jnp.maximum(ha - 1, 0), jnp.minimum(ha + 1, n_ha - 1)

    pairs = [
        (cells, cl),
        (weight, wt),
        (saved, sv),
        (labels, lb),
        (adj_h, h0),
        (adj_e, e),
        (density, dens),
    ]
    loads = [pltpu.make_async_copy(a, b, local_sem.at[i]) for i, (a, b) in enumerate(pairs)]
    for load in loads:
        load.start()

    group = 2 if n_lat % 2 == 0 else 1
    place, number = lax.rem(lat, group), lax.div(lat, group)
    members, groups = group * n_ha, n_lat // group

    def member(d):
        there = lax.rem(place * n_ha + ha + d, members)
        return (number * group + lax.div(there, n_ha), lax.rem(there, n_ha))

    def counterpart(d):
        return (lax.rem(number + d, groups) * group + place, ha)

    barrier = pltpu.get_barrier_semaphore()

    def greet(target):
        pl.semaphore_signal(barrier, inc=1, device_id=target, device_id_type=MESH)

    for d in range(1, members):
        greet(member(d))
    for d in range(1, groups):
        greet(counterpart(d))
    greeted = (members - 1) + (groups - 1)
    if group == 2:
        outer = lat - 1 + 2 * place
        exists = jnp.logical_and(outer >= 0, outer < n_lat)
        beyond = [(exists, outer, d) for d in range(n_ha)]
    else:
        beyond = [(lat_dn, lat_prev, d) for d in range(1, n_ha)]
        beyond += [(lat_up, lat_next, d) for d in range(1, n_ha)]
    for condition, there, d in beyond:
        pl.when(condition)(functools.partial(greet, (there, lax.rem(ha + d, n_ha))))
        greeted = greeted + condition.astype(jnp.int32)

    issued = []
    numbers = iter(range(send_sem.shape[0]))

    def finish_sends(kept=0):
        while len(issued) > kept:
            issued.pop(0)()

    def exchange(src, dst, target, sends=None, receives=None):
        index = next(numbers)

        def copy():
            return pltpu.make_async_remote_copy(
                src_ref=src,
                dst_ref=dst,
                send_sem=send_sem.at[index],
                recv_sem=recv_sem.at[index],
                device_id=target,
                device_id_type=MESH,
            )

        def guarded(condition, action):
            if condition is None:
                action()
            else:
                pl.when(condition)(action)

        issued.append(lambda: guarded(sends, lambda: copy().wait_send()))
        guarded(sends, lambda: copy().start())

        def arrive():
            guarded(receives, lambda: copy().wait_recv())
            if receives is not None:

                @pl.when(jnp.logical_not(receives))
                def _():
                    dst[...] = jnp.zeros(dst.shape, dst.dtype)

        return arrive

    loads[0].wait()
    loads[1].wait()
    cell = cl[...]
    amount = wt[...]
    first = amount.astype(jnp.bfloat16)
    left = amount - first.astype(jnp.float32)
    second = left.astype(jnp.bfloat16)
    third = (left - second.astype(jnp.float32)).astype(jnp.bfloat16)
    line = lax.broadcasted_iota(jnp.int32, (depth * rows, entries), 0) == cell // width
    lane_hit = lax.broadcasted_iota(jnp.int32, (width, entries), 0) == lax.rem(cell, width)
    line = jnp.where(line, 1.0, 0.0).astype(jnp.bfloat16)
    total = jnp.zeros((depth * rows, width), jnp.float32)
    for part in (third, second, first):
        spread = jnp.where(lane_hit, part.astype(jnp.float32), 0.0).astype(jnp.bfloat16)
        total = total + lax.dot_general(
            line, spread, (((1,), (1,)), ((), ())), preferred_element_type=jnp.float32
        )
    for z in range(depth):
        wgrid[z] = total[z * rows : (z + 1) * rows]

    loads[2].wait()

    def field(k, c, z):
        return sv[k, c, z].astype(jnp.float32)

    for k in range(steps):
        acc = jnp.zeros((rows, width), jnp.float32)
        for z in range(depth):
            square = jnp.zeros((rows, width), jnp.float32)
            for c in range(comps):
                f = field(k, c, z)
                square = square + f * f
            acc = acc + wgrid[z] * square
        pw_out[k : k + 1, :] = jnp.sum(acc, 0, keepdims=True)

    pl.semaphore_wait(barrier, greeted)
    members_in = [exchange(pw_out, pw_in.at[d - 1], member(d)) for d in range(1, members)]

    lane = lax.broadcasted_iota(jnp.int32, (rows, width), 1)
    row = lax.broadcasted_iota(jnp.int32, (rows, width), 0)
    inside_ha = ha_up.astype(jnp.float32)
    inside_lat = lat_up.astype(jnp.float32)

    def y_lower(v):
        return jnp.where(lane == 0, 0.0, pltpu.roll(v, 1, 1))

    def y_upper(v):
        return jnp.where(lane == width - 1, 0.0, pltpu.roll(v, width - 1, 1))

    def x_lower(v, edge):
        return jnp.where(row == 0, edge, pltpu.roll(v, 1, 0))

    def x_upper(v, edge):
        return jnp.where(row == rows - 1, edge, pltpu.roll(v, rows - 1, 0))

    def material(z):
        label = lb[z]
        eps = jnp.full((rows, width), eps_table[0], jnp.float32)
        chi = jnp.full((rows, width), 3.0 * chi_table[0], jnp.float32)
        for region in range(1, regions):
            hit = label == region
            eps = jnp.where(hit, eps_table[region], eps)
            chi = jnp.where(hit, 3.0 * chi_table[region], chi)
        return eps, chi

    def lower_parts(src, z):
        sx, sy, sz = src[0, z], src[1, z], src[2, z]
        curl_x = sz - y_lower(sz) - sy
        curl_y = sx - (sz - x_lower(sz, 0.0))
        curl_z = sy - x_lower(sy, 0.0) - (sx - y_lower(sx))
        if z > 0:
            curl_x = curl_x + src[1, z - 1]
            curl_y = curl_y - src[0, z - 1]
        return curl_x, curl_y, curl_z

    def both_parts(z):
        eps, chi = material(z)
        inner = [jnp.zeros((rows, width), jnp.float32) for _ in range(2)]
        for c in range(comps):
            f = field(last, c, z)
            inverse = 1.0 / (eps + chi * f * f)
            for i, value in enumerate((e[c, z] * inverse, wgrid[z] * f * inverse)):
                ab[i, c, z] = value
                inner[i] = inner[i] + value * f
                if c > 0:
                    slot = (2 * i + c - 1) * depth + z
                    rlab_out[slot : slot + 1, :] = value[rows - 1 : rows]
                if c == 0 and z == top:
                    caab_out[i : i + 1, :] = value[0:1]
                if c == 2 and z == 0:
                    cbab_out[i : i + 1, :] = value[rows - 1 : rows]
        return [jnp.where(lb[z] == 0, value, 0.0) for value in inner]

    def both_curls(z):
        for i in range(2):
            curl = lower_parts(ab.at[i], z)
            for c in range(comps):
                value = -time_step * curl[c]
                if i == 0:
                    value = h0[c, z] + value
                pab[i, c, z] = value
                if z == 0 and c < 2:
                    hzab_out[i, c] = value
                if c > 0:
                    slot = (2 * i + c - 1) * depth + z
                    ruab_out[slot : slot + 1, :] = value[0:1]

    loads[3].wait()
    loads[4].wait()
    loads[5].wait()
    inner = [jnp.zeros((rows, width), jnp.float32) for _ in range(2)]
    for z in [0] + list(range(top, 0, -1)):
        inner = [old + more for old, more in zip(inner, both_parts(z))]
        if z == 0:
            both_curls(0)
            zuab_in = exchange(hzab_out, zuab, (lat, ha_prev), ha_dn, ha_up)
        if z == top:
            zlab_in = exchange(ab.at[:, pl.ds(0, 2), top], zlab, (lat, ha_next), ha_up, ha_dn)
    corner_a = (
        (lat_prev, ha_next),
        jnp.logical_and(lat_dn, ha_up),
        jnp.logical_and(lat_up, ha_dn),
    )
    corner_b = (
        (lat_next, ha_prev),
        jnp.logical_and(lat_up, ha_dn),
        jnp.logical_and(lat_dn, ha_up),
    )
    rlab_in = exchange(rlab_out, rlab, (lat_next, ha), lat_up, lat_dn)
    caab_in = exchange(caab_out, caab, *corner_a)
    cbab_in = exchange(cbab_out, cbab, *corner_b)

    for arrive in members_in:
        arrive()
    power_rows = pw_out[...]
    for d in range(1, members):
        power_rows = power_rows + pw_in[d - 1]
    pw_sum[...] = power_rows
    groups_in = [exchange(pw_sum, pw_all.at[d - 1], counterpart(d)) for d in range(1, groups)]

    for z in range(1, depth):
        both_curls(z)
    ruab_in = exchange(ruab_out, ruab, (lat_prev, ha), lat_dn, lat_up)

    loads[6].wait()
    dens_lo_in = exchange(
        dens.at[pl.ds(rows - 2 * RADIUS, 2 * RADIUS)], dens_lo, (lat_next, ha), lat_up, lat_dn
    )
    dens_hi_in = exchange(
        dens.at[pl.ds(0, 2 * RADIUS)], dens_hi, (lat_prev, ha), lat_dn, lat_up
    )

    for z in range(depth):
        eps, chi = material(z)
        for k in range(last):
            for c in range(comps):
                f = field(k, c, z)
                rinv[k, c, z] = 1.0 / (eps + chi * f * f)

    for arrive in groups_in:
        arrive()
    for d in range(1, groups):
        power_rows = power_rows + pw_all[d - 1]
    power = jnp.sum(power_rows, 1, keepdims=True) / (entries * devices) + epsilon
    inverse_power = 1.0 / power

    def scale_layer(k, z, fields, acc):
        gain = inverse_power[k : k + 1, :]
        inner = jnp.zeros((rows, width), jnp.float32)
        for c in range(comps):
            f = field(k, c, z)
            now = fields[c] + gain * (wgrid[z] * f)
            value = now * rinv[k, c, z]
            e[c, z] = now
            s[k, c, z] = value
            inner = inner + value * f
            if c > 0:
                slot = (c - 1) * depth + z
                rl_out[k, slot : slot + 1, :] = value[rows - 1 : rows]
            if c == 0 and z == top:
                ca_out[k] = value[0:1]
            if c == 2 and z == 0:
                cb_out[k] = value[rows - 1 : rows]
        return acc + jnp.where(lb[z] == 0, inner, 0.0)

    def magnetic(k):
        return out_h if k == 0 else hh.at[k]

    def lower_layer(k, z):
        old = magnetic(k + 1)
        new = magnetic(k)
        curl_x, curl_y, curl_z = lower_parts(s.at[k], z)
        values = (
            old[0, z] - time_step * curl_x,
            old[1, z] - time_step * curl_y,
            old[2, z] - time_step * curl_z,
        )
        for c in range(comps):
            new[c, z] = values[c]
            if z == 0 and c < 2:
                hz_out[k, c] = values[c]
            if c > 0:
                slot = (c - 1) * depth + z
                ru_out[k, slot : slot + 1, :] = values[c][0:1]

    def send_bottom(k):
        return exchange(hz_out.at[k], zu.at[k], (lat, ha_prev), ha_dn, ha_up)

    def send_top(k):
        return exchange(s.at[k, pl.ds(0, 2), top], zl.at[k], (lat, ha_next), ha_up, ha_dn)

    def send_edges(k):
        return (
            exchange(rl_out.at[k], rl.at[k], (lat_next, ha), lat_up, lat_dn),
            exchange(ca_out.at[k], ca.at[k], *corner_a),
            exchange(cb_out.at[k], cb.at[k], *corner_b),
        )

    def send_plane(acc):
        plane[...] = acc
        arrivals = []
        for d in range(n_ha):
            other = lax.rem(ha + d, n_ha)
            if d > 0:
                arrivals.append(exchange(plane, plane_ha.at[d - 1], (lat, other)))
            arrivals.append(
                exchange(
                    plane.at[pl.ds(rows - RADIUS, RADIUS)],
                    plane_lo.at[d],
                    (lat_next, other),
                    lat_up,
                    lat_dn,
                )
            )
            arrivals.append(
                exchange(
                    plane.at[pl.ds(0, RADIUS)],
                    plane_hi.at[d],
                    (lat_prev, other),
                    lat_dn,
                    lat_up,
                )
            )
        return arrivals

    gain = inverse_power[last : last + 1, :]
    acc = inner[0] + gain * inner[1]
    for z in range(depth):
        for c in range(comps):
            magnetic(last)[c, z] = pab[0, c, z] + gain * pab[1, c, z]

    def joined(ref):
        half = ref.shape[0] // 2
        return ref[pl.ds(0, half)] + gain * ref[pl.ds(half, half)]

    for k in reversed(range(steps)):
        if k == last:
            rl_in, ru_in, zl_in, zu_in, ca_in, cb_in = (
                rlab_in,
                ruab_in,
                zlab_in,
                zuab_in,
                caab_in,
                cbab_in,
            )
        else:
            kept = len(issued)
            rl_in, ca_in, cb_in = send_edges(k)
            if k == 0:
                plane_in = send_plane(acc)
            for z in range(1, depth):
                lower_layer(k, z)
            ru_in = exchange(ru_out.at[k], ru.at[k], (lat_prev, ha), lat_dn, lat_up)
            finish_sends(len(issued) - kept + 2)

        if k == last:
            dens_lo_in()
            dens_hi_in()
            extended = jnp.concatenate([dens_lo[...], dens[...], dens_hi[...]], 0)
            filtered = filter_rows(extended, rows + 2 * RADIUS)
            slope = jnp.tanh(sharpness * (filtered - threshold))
            deriv[...] = (
                sharpness
                * (1.0 - slope * slope)
                / (jnp.tanh(sharpness * threshold) + jnp.tanh(sharpness * (1.0 - threshold)))
            )

        new = magnetic(k)
        rl_in()
        low = joined(rlab) if k == last else rl[k]
        for z in range(depth):
            new[1, z, 0:1] = new[1, z, 0:1] - time_step * low[depth + z : depth + z + 1]
            new[2, z, 0:1] = new[2, z, 0:1] + time_step * low[z : z + 1]

        ru_in()
        ca_in()
        own = joined(rlab_out) if k == last else rl_out[k]
        high = joined(ruab) if k == last else ru[k]
        corner = joined(caab) if k == last else ca[k]
        high_y = (high[0:depth] - time_step * own[depth : 2 * depth]) * inside_lat
        high_z = (high[depth : 2 * depth] + time_step * own[0:depth]) * inside_lat
        first_y = high_y[0:1] + time_step * inside_lat * corner

        def finish_layer(z, above_x, above_y, acc):
            hx, hy, hv = new[0, z], new[1, z], new[2, z]
            edge_y = first_y if z == 0 else high_y[z : z + 1]
            edge_z = high_z[z : z + 1]
            curl_x = y_upper(hv) - hv - (above_y - hy)
            curl_y = above_x - hx - (x_upper(hv, edge_z) - hv)
            curl_z = x_upper(hy, edge_y) - hy - (y_upper(hx) - hx)
            fields = [
                e[0, z] + time_step * curl_x,
                e[1, z] + time_step * curl_y,
                e[2, z] + time_step * curl_z,
            ]
            if k == last:
                for c in range(comps):
                    fields[c] = fields[c] + gain * (wgrid[z] * field(k, c, z))
            if k > 0:
                return scale_layer(k - 1, z, fields, acc)
            for c in range(comps):
                out_e[c, z] = fields[c]
            return acc

        for z in range(1, top):
            acc = finish_layer(z, new[0, z + 1], new[1, z + 1], acc)

        zl_in()
        if k == last:
            below_x, below_y = zlab[0, 0] + gain * zlab[1, 0], zlab[0, 1] + gain * zlab[1, 1]
        else:
            below_x, below_y = zl[k, 0], zl[k, 1]
        new[0, 0] = new[0, 0] - time_step * below_y
        new[1, 0] = new[1, 0] + time_step * below_x
        if top > 0:
            acc = finish_layer(0, new[0, 1], new[1, 1], acc)
            if k > 0:
                lower_layer(k - 1, 0)
                zu_next = send_bottom(k - 1)

        zu_in()
        cb_in()
        if k == last:
            above_x, above_y = zuab[0, 0] + gain * zuab[1, 0], zuab[0, 1] + gain * zuab[1, 1]
            own_x, own_y = ab[0, 0, top] + gain * ab[1, 0, top], ab[0, 1, top] + gain * ab[1, 1, top]
            corner = joined(cbab)
        else:
            above_x, above_y = zu[k, 0], zu[k, 1]
            own_x, own_y = s[k, 0, top], s[k, 1, top]
            corner = cb[k]
        above_x = above_x - time_step * own_y
        above_y = above_y + time_step * own_x
        above_y = above_y - jnp.where(row == 0, time_step * corner, 0.0)
        acc = finish_layer(top, above_x * inside_ha, above_y * inside_ha, acc)
        if k > 0:
            if top == 0:
                lower_layer(k - 1, 0)
                zu_next = send_bottom(k - 1)
            zu_in = zu_next
            zl_in = send_top(k - 1)

    for arrive in plane_in:
        arrive()
    middle = plane[...]
    low = plane_lo[0]
    high = plane_hi[0]
    for d in range(1, n_ha):
        middle = middle + plane_ha[d - 1]
        low = low + plane_lo[d]
        high = high + plane_hi[d]
    product = jnp.concatenate([low, middle, high], 0) * deriv[...]
    out_g[...] = filter_rows(product, rows)
    finish_sends()


def store(e, h, g, out_e, out_h, out_g, sem):
    copies = [
        pltpu.make_async_copy(e, out_e, sem.at[0]),
        pltpu.make_async_copy(h, out_h, sem.at[1]),
        pltpu.make_async_copy(g, out_g, sem.at[2]),
    ]
    for copy in copies:
        copy.start()
    for copy in copies:
        copy.wait()


def body(
    adjoint_e, adjoint_h, saved_e, labels, eps_table, chi_table, density, mon_cells, mon_weight
):
    n_lat, n_ha = lax.axis_size("lat"), lax.axis_size("ha")
    steps, comps, depth, rows, width = saved_e.shape
    entries = mon_cells.shape[0]
    f32 = jnp.float32
    block = (comps, depth, rows, width)
    group = 2 if n_lat % 2 == 0 else 1
    members, groups = group * n_ha, n_lat // group
    copies = (members - 1) + (groups - 1) + 2 + 6 * steps + 3 * n_ha - 1
    vmem = pl.BlockSpec(memory_space=pltpu.VMEM)
    hbm = pl.BlockSpec(memory_space=pltpu.HBM)
    scalars = pl.BlockSpec(memory_space=pltpu.SMEM)
    scratch = [
        pltpu.VMEM(block, f32),
        pltpu.VMEM(block, f32),
        pltpu.VMEM(saved_e.shape, saved_e.dtype),
        pltpu.VMEM(labels.shape, labels.dtype),
        pltpu.VMEM((rows, width), f32),
        pltpu.VMEM((1, entries), mon_cells.dtype),
        pltpu.VMEM((1, entries), f32),
        pltpu.VMEM((depth, rows, width), f32),
        pltpu.VMEM((steps,) + block, f32),
        pltpu.VMEM((steps,) + block, f32),
        pltpu.VMEM((steps,) + block, f32),
        pltpu.VMEM((rows, width), f32),
        pltpu.VMEM((2 * RADIUS, width), f32),
        pltpu.VMEM((2 * RADIUS, width), f32),
        pltpu.VMEM((rows + 2 * RADIUS, width), f32),
        pltpu.VMEM((steps, 2, rows, width), f32),
        pltpu.VMEM((steps, 2, rows, width), f32),
        pltpu.VMEM((steps, 2, rows, width), f32),
        pltpu.VMEM((steps, 2 * depth, width), f32),
        pltpu.VMEM((steps, 2 * depth, width), f32),
        pltpu.VMEM((steps, 2 * depth, width), f32),
        pltpu.VMEM((steps, 2 * depth, width), f32),
        pltpu.VMEM((steps, 1, width), f32),
        pltpu.VMEM((steps, 1, width), f32),
        pltpu.VMEM((steps, 1, width), f32),
        pltpu.VMEM((steps, 1, width), f32),
        pltpu.VMEM((steps, width), f32),
        pltpu.VMEM((max(members - 1, 1), steps, width), f32),
        pltpu.VMEM((steps, width), f32),
        pltpu.VMEM((max(groups - 1, 1), steps, width), f32),
        pltpu.VMEM((2,) + block, f32),
        pltpu.VMEM((2,) + block, f32),
        pltpu.VMEM((2, 2, rows, width), f32),
        pltpu.VMEM((2, 2, rows, width), f32),
        pltpu.VMEM((2, 2, rows, width), f32),
        pltpu.VMEM((4 * depth, width), f32),
        pltpu.VMEM((4 * depth, width), f32),
        pltpu.VMEM((4 * depth, width), f32),
        pltpu.VMEM((4 * depth, width), f32),
        pltpu.VMEM((2, width), f32),
        pltpu.VMEM((2, width), f32),
        pltpu.VMEM((2, width), f32),
        pltpu.VMEM((2, width), f32),
        pltpu.VMEM((max(n_ha - 1, 1), rows, width), f32),
        pltpu.VMEM((n_ha, RADIUS, width), f32),
        pltpu.VMEM((n_ha, RADIUS, width), f32),
        pltpu.SemaphoreType.DMA((7,)),
        pltpu.SemaphoreType.DMA((copies,)),
        pltpu.SemaphoreType.DMA((copies,)),
    ]
    results = pl.pallas_call(
        functools.partial(kernel, n_lat, n_ha),
        out_shape=(
            pltpu.VMEM(block, f32),
            pltpu.VMEM(block, f32),
            pltpu.VMEM((rows, width), f32),
        ),
        in_specs=[hbm] * 4 + [scalars] * 2 + [hbm] * 3,
        out_specs=(vmem, vmem, vmem),
        scratch_shapes=scratch,
        compiler_params=pltpu.CompilerParams(
            collective_id=0, has_side_effects=True, vmem_limit_bytes=63 * 2**20
        ),
    )(
        adjoint_e,
        adjoint_h,
        saved_e,
        labels,
        eps_table,
        chi_table,
        density,
        mon_cells.reshape(1, entries),
        mon_weight.reshape(1, entries),
    )
    return pl.pallas_call(
        store,
        out_shape=(
            jax.ShapeDtypeStruct(block, f32),
            jax.ShapeDtypeStruct(block, f32),
            jax.ShapeDtypeStruct((rows, width), f32),
        ),
        in_specs=[vmem] * 3,
        out_specs=(hbm, hbm, hbm),
        scratch_shapes=[pltpu.SemaphoreType.DMA((3,))],
        compiler_params=pltpu.CompilerParams(vmem_limit_bytes=2**20),
    )(*results)


def solution(mesh):
    return jax.shard_map(
        body,
        mesh=mesh,
        in_specs=(
            P(None, "ha", "lat", None),
            P(None, "ha", "lat", None),
            P(None, None, "ha", "lat", None),
            P("ha", "lat", None),
            P(),
            P(),
            P("lat", None),
            P(("lat", "ha")),
            P(("lat", "ha")),
        ),
        out_specs=(P(None, "ha", "lat", None), P(None, "ha", "lat", None), P("lat", None)),
        check_vma=False,
    )
```

```python
import functools

import jax
import jax.numpy as jnp
from jax import lax
from jax.experimental import pallas as pl
from jax.experimental.pallas import tpu as pltpu
from jax.sharding import PartitionSpec as P

RADIUS = 16

sharpness = 8.0
threshold = 0.5
time_step = 0.5
epsilon = 1e-05

MESH = pl.DeviceIdType.MESH


def cone(offset):
    return jnp.maximum(RADIUS + 1 - jnp.abs(offset), 0).astype(jnp.float32) / (RADIUS + 1) ** 2


def filter_rows(padded, rows):
    width = padded.shape[1]
    i = lax.broadcasted_iota(jnp.int32, (width, width), 0)
    j = lax.broadcasted_iota(jnp.int32, (width, width), 1)
    smoothed = jnp.dot(
        padded, cone(i - j), precision=lax.Precision.HIGHEST, preferred_element_type=jnp.float32
    )
    row_out = lax.broadcasted_iota(jnp.int32, (rows, rows + 2 * RADIUS), 0)
    row_in = lax.broadcasted_iota(jnp.int32, (rows, rows + 2 * RADIUS), 1)
    return jnp.dot(
        cone(row_in - RADIUS - row_out),
        smoothed,
        precision=lax.Precision.HIGHEST,
        preferred_element_type=jnp.float32,
    )


def kernel(
    n_lat,
    n_ha,
    adj_e,
    adj_h,
    saved,
    labels,
    eps_table,
    chi_table,
    density,
    cells,
    weight,
    out_e,
    out_h,
    out_g,
    e,
    h0,
    sv,
    lb,
    dens,
    cl,
    wt,
    wgrid,
    s,
    hh,
    rinv,
    plane,
    dens_lo,
    dens_hi,
    deriv,
    hz_out,
    zl,
    zu,
    rl_out,
    rl,
    ru_out,
    ru,
    ca_out,
    ca,
    cb_out,
    cb,
    eps_of,
    chi_of,
    pw_out,
    pw_in,
    pw_sum,
    pw_all,
    ab,
    pab,
    hzab_out,
    zuab,
    zlab,
    rlab_out,
    rlab,
    ruab_out,
    ruab,
    caab_out,
    caab,
    cbab_out,
    cbab,
    plane_ha,
    plane_lo,
    plane_hi,
    local_sem,
    send_sem,
    recv_sem,
):
    steps, comps, depth, rows, width = sv.shape
    regions = eps_table.shape[0]
    entries = cl.shape[1]
    last, top = steps - 1, depth - 1
    devices = n_lat * n_ha
    lat = lax.axis_index("lat")
    ha = lax.axis_index("ha")
    lat_dn, lat_up = lat > 0, lat < n_lat - 1
    ha_dn, ha_up = ha > 0, ha < n_ha - 1
    lat_prev, lat_next = jnp.maximum(lat - 1, 0), jnp.minimum(lat + 1, n_lat - 1)
    ha_prev, ha_next = jnp.maximum(ha - 1, 0), jnp.minimum(ha + 1, n_ha - 1)

    pairs = [
        (cells, cl),
        (weight, wt),
        (saved, sv),
        (labels, lb),
        (adj_h, h0),
        (adj_e, e),
        (density, dens),
        (eps_table, eps_of),
        (chi_table, chi_of),
    ]
    loads = [pltpu.make_async_copy(a, b, local_sem.at[i]) for i, (a, b) in enumerate(pairs)]
    for load in loads:
        load.start()

    group = 2 if n_lat % 2 == 0 else 1
    place, number = lax.rem(lat, group), lax.div(lat, group)
    members, groups = group * n_ha, n_lat // group

    def member(d):
        there = lax.rem(place * n_ha + ha + d, members)
        return (number * group + lax.div(there, n_ha), lax.rem(there, n_ha))

    def counterpart(d):
        return (lax.rem(number + d, groups) * group + place, ha)

    barrier = pltpu.get_barrier_semaphore()

    def greet(target):
        pl.semaphore_signal(barrier, inc=1, device_id=target, device_id_type=MESH)

    for d in range(1, members):
        greet(member(d))
    for d in range(1, groups):
        greet(counterpart(d))
    greeted = (members - 1) + (groups - 1)
    if group == 2:
        outer = lat - 1 + 2 * place
        exists = jnp.logical_and(outer >= 0, outer < n_lat)
        beyond = [(exists, outer, d) for d in range(n_ha)]
    else:
        beyond = [(lat_dn, lat_prev, d) for d in range(1, n_ha)]
        beyond += [(lat_up, lat_next, d) for d in range(1, n_ha)]
    for condition, there, d in beyond:
        pl.when(condition)(functools.partial(greet, (there, lax.rem(ha + d, n_ha))))
        greeted = greeted + condition.astype(jnp.int32)

    issued = []
    numbers = iter(range(send_sem.shape[0]))

    def finish_sends(kept=0):
        while len(issued) > kept:
            issued.pop(0)()

    def exchange(src, dst, target, sends=None, receives=None):
        index = next(numbers)

        def copy():
            return pltpu.make_async_remote_copy(
                src_ref=src,
                dst_ref=dst,
                send_sem=send_sem.at[index],
                recv_sem=recv_sem.at[index],
                device_id=target,
                device_id_type=MESH,
            )

        def guarded(condition, action):
            if condition is None:
                action()
            else:
                pl.when(condition)(action)

        issued.append(lambda: guarded(sends, lambda: copy().wait_send()))
        guarded(sends, lambda: copy().start())

        def arrive():
            guarded(receives, lambda: copy().wait_recv())
            if receives is not None:

                @pl.when(jnp.logical_not(receives))
                def _():
                    dst[...] = jnp.zeros(dst.shape, dst.dtype)

        return arrive

    def field(k, c, z):
        return sv[k, c, z].astype(jnp.float32)

    lane = lax.broadcasted_iota(jnp.int32, (rows, width), 1)
    row = lax.broadcasted_iota(jnp.int32, (rows, width), 0)
    inside_ha = ha_up.astype(jnp.float32)
    inside_lat = lat_up.astype(jnp.float32)

    def y_lower(v):
        return jnp.where(lane == 0, 0.0, pltpu.roll(v, 1, 1))

    def y_upper(v):
        return jnp.where(lane == width - 1, 0.0, pltpu.roll(v, width - 1, 1))

    def x_lower(v, edge):
        return jnp.where(row == 0, edge, pltpu.roll(v, 1, 0))

    def x_upper(v, edge):
        return jnp.where(row == rows - 1, edge, pltpu.roll(v, rows - 1, 0))

    def material(z):
        label = lb[z]
        eps = jnp.full((rows, width), eps_of[0], jnp.float32)
        chi = jnp.full((rows, width), 3.0 * chi_of[0], jnp.float32)
        for region in range(1, regions):
            hit = label == region
            eps = jnp.where(hit, eps_of[region], eps)
            chi = jnp.where(hit, 3.0 * chi_of[region], chi)
        return eps, chi

    def lower_parts(src, z):
        sx, sy, sz = src[0, z], src[1, z], src[2, z]
        curl_x = sz - y_lower(sz) - sy
        curl_y = sx - (sz - x_lower(sz, 0.0))
        curl_z = sy - x_lower(sy, 0.0) - (sx - y_lower(sx))
        if z > 0:
            curl_x = curl_x + src[1, z - 1]
            curl_y = curl_y - src[0, z - 1]
        return curl_x, curl_y, curl_z

    def part_a(z):
        eps, chi = material(z)
        inner = jnp.zeros((rows, width), jnp.float32)
        for c in range(comps):
            f = field(last, c, z)
            inverse = 1.0 / (eps + chi * f * f)
            ab[1, c, z] = f * inverse
            inner = inner + put_part(0, c, z, e[c, z] * inverse) * f
        return jnp.where(lb[z] == 0, inner, 0.0)

    def part_b(z):
        inner = jnp.zeros((rows, width), jnp.float32)
        for c in range(comps):
            inner = inner + put_part(1, c, z, wgrid[z] * ab[1, c, z]) * field(last, c, z)
        return jnp.where(lb[z] == 0, inner, 0.0)

    def put_part(i, c, z, value):
        ab[i, c, z] = value
        if c > 0:
            slot = (2 * i + c - 1) * depth + z
            rlab_out[slot : slot + 1, :] = value[rows - 1 : rows]
        if c == 0 and z == top:
            caab_out[i : i + 1, :] = value[0:1]
        if c == 2 and z == 0:
            cbab_out[i : i + 1, :] = value[rows - 1 : rows]
        return value

    def part_curl(i, z):
        curl = lower_parts(ab.at[i], z)
        for c in range(comps):
            value = -time_step * curl[c]
            if i == 0:
                value = h0[c, z] + value
            pab[i, c, z] = value
            if z == 0 and c < 2:
                hzab_out[i, c] = value
            if c > 0:
                slot = (2 * i + c - 1) * depth + z
                ruab_out[slot : slot + 1, :] = value[0:1]

    def ends(part, i, wait=None):
        inner = part(0)
        part_curl(i, 0)
        if wait is not None:
            wait()
        arrivals = [exchange(hzab_out.at[i], zuab.at[i], (lat, ha_prev), ha_dn, ha_up)]
        if top > 0:
            inner = inner + part(top)
        arrivals.append(
            exchange(ab.at[i, pl.ds(0, 2), top], zlab.at[i], (lat, ha_next), ha_up, ha_dn)
        )
        return inner, arrivals

    for index in (2, 3, 4, 5, 7, 8):
        loads[index].wait()
    inner_a, (zua_in, zla_in) = ends(
        part_a, 0, lambda: pl.semaphore_wait(barrier, greeted)
    )

    loads[0].wait()
    loads[1].wait()
    cell = cl[...]
    amount = wt[...]
    first = amount.astype(jnp.bfloat16)
    left = amount - first.astype(jnp.float32)
    second = left.astype(jnp.bfloat16)
    third = (left - second.astype(jnp.float32)).astype(jnp.bfloat16)
    line = lax.broadcasted_iota(jnp.int32, (depth * rows, entries), 0) == cell // width
    lane_hit = lax.broadcasted_iota(jnp.int32, (width, entries), 0) == lax.rem(cell, width)
    line = jnp.where(line, 1.0, 0.0).astype(jnp.bfloat16)
    total = jnp.zeros((depth * rows, width), jnp.float32)
    for part in (third, second, first):
        spread = jnp.where(lane_hit, part.astype(jnp.float32), 0.0).astype(jnp.bfloat16)
        total = total + lax.dot_general(
            line, spread, (((1,), (1,)), ((), ())), preferred_element_type=jnp.float32
        )
    for z in range(depth):
        wgrid[z] = total[z * rows : (z + 1) * rows]

    for k in range(steps):
        acc = jnp.zeros((rows, width), jnp.float32)
        for z in range(depth):
            square = jnp.zeros((rows, width), jnp.float32)
            for c in range(comps):
                f = field(k, c, z)
                square = square + f * f
            acc = acc + wgrid[z] * square
        pw_out[k : k + 1, :] = jnp.sum(acc, 0, keepdims=True)

    members_in = [exchange(pw_out, pw_in.at[d - 1], member(d)) for d in range(1, members)]

    inner_b, (zub_in, zlb_in) = ends(part_b, 1)
    for z in range(1, top):
        inner_a = inner_a + part_a(z)
        inner_b = inner_b + part_b(z)
    corner_a = (
        (lat_prev, ha_next),
        jnp.logical_and(lat_dn, ha_up),
        jnp.logical_and(lat_up, ha_dn),
    )
    corner_b = (
        (lat_next, ha_prev),
        jnp.logical_and(lat_up, ha_dn),
        jnp.logical_and(lat_dn, ha_up),
    )
    rlab_in = exchange(rlab_out, rlab, (lat_next, ha), lat_up, lat_dn)
    caab_in = exchange(caab_out, caab, *corner_a)
    cbab_in = exchange(cbab_out, cbab, *corner_b)

    for arrive in members_in:
        arrive()
    power_rows = pw_out[...]
    for d in range(1, members):
        power_rows = power_rows + pw_in[d - 1]
    pw_sum[...] = power_rows
    groups_in = [exchange(pw_sum, pw_all.at[d - 1], counterpart(d)) for d in range(1, groups)]

    for z in range(1, depth):
        part_curl(0, z)
        part_curl(1, z)
    ruab_in = exchange(ruab_out, ruab, (lat_prev, ha), lat_dn, lat_up)

    loads[6].wait()
    dens_lo_in = exchange(
        dens.at[pl.ds(rows - 2 * RADIUS, 2 * RADIUS)], dens_lo, (lat_next, ha), lat_up, lat_dn
    )
    dens_hi_in = exchange(
        dens.at[pl.ds(0, 2 * RADIUS)], dens_hi, (lat_prev, ha), lat_dn, lat_up
    )

    for z in range(depth):
        eps, chi = material(z)
        for k in range(last):
            for c in range(comps):
                f = field(k, c, z)
                rinv[k, c, z] = 1.0 / (eps + chi * f * f)

    for arrive in groups_in:
        arrive()
    for d in range(1, groups):
        power_rows = power_rows + pw_all[d - 1]
    power = jnp.sum(power_rows, 1, keepdims=True) / (entries * devices) + epsilon
    inverse_power = 1.0 / power

    def scale_layer(k, z, fields, acc):
        gain = inverse_power[k : k + 1, :]
        inner = jnp.zeros((rows, width), jnp.float32)
        for c in range(comps):
            f = field(k, c, z)
            now = fields[c] + gain * (wgrid[z] * f)
            value = now * rinv[k, c, z]
            e[c, z] = now
            s[k, c, z] = value
            inner = inner + value * f
            if c > 0:
                slot = (c - 1) * depth + z
                rl_out[k, slot : slot + 1, :] = value[rows - 1 : rows]
            if c == 0 and z == top:
                ca_out[k] = value[0:1]
            if c == 2 and z == 0:
                cb_out[k] = value[rows - 1 : rows]
        return acc + jnp.where(lb[z] == 0, inner, 0.0)

    def magnetic(k):
        return out_h if k == 0 else hh.at[k]

    def lower_layer(k, z):
        old = magnetic(k + 1)
        new = magnetic(k)
        curl_x, curl_y, curl_z = lower_parts(s.at[k], z)
        values = (
            old[0, z] - time_step * curl_x,
            old[1, z] - time_step * curl_y,
            old[2, z] - time_step * curl_z,
        )
        for c in range(comps):
            new[c, z] = values[c]
            if z == 0 and c < 2:
                hz_out[k, c] = values[c]
            if c > 0:
                slot = (c - 1) * depth + z
                ru_out[k, slot : slot + 1, :] = values[c][0:1]

    def send_bottom(k):
        return exchange(hz_out.at[k], zu.at[k], (lat, ha_prev), ha_dn, ha_up)

    def send_top(k):
        return exchange(s.at[k, pl.ds(0, 2), top], zl.at[k], (lat, ha_next), ha_up, ha_dn)

    def send_edges(k):
        return (
            exchange(rl_out.at[k], rl.at[k], (lat_next, ha), lat_up, lat_dn),
            exchange(ca_out.at[k], ca.at[k], *corner_a),
            exchange(cb_out.at[k], cb.at[k], *corner_b),
        )

    def send_plane(acc):
        plane[...] = acc
        arrivals = []
        for d in range(n_ha):
            other = lax.rem(ha + d, n_ha)
            if d > 0:
                arrivals.append(exchange(plane, plane_ha.at[d - 1], (lat, other)))
            arrivals.append(
                exchange(
                    plane.at[pl.ds(rows - RADIUS, RADIUS)],
                    plane_lo.at[d],
                    (lat_next, other),
                    lat_up,
                    lat_dn,
                )
            )
            arrivals.append(
                exchange(
                    plane.at[pl.ds(0, RADIUS)],
                    plane_hi.at[d],
                    (lat_prev, other),
                    lat_dn,
                    lat_up,
                )
            )
        return arrivals

    gain = inverse_power[last : last + 1, :]
    acc = inner_a + gain * inner_b
    for z in range(depth):
        for c in range(comps):
            magnetic(last)[c, z] = pab[0, c, z] + gain * pab[1, c, z]

    def joined(ref):
        half = ref.shape[0] // 2
        return ref[pl.ds(0, half)] + gain * ref[pl.ds(half, half)]

    if last == 0:
        plane_in = send_plane(acc)
    for k in reversed(range(steps)):
        if k == last:
            rl_in, ru_in, ca_in, cb_in = rlab_in, ruab_in, caab_in, cbab_in
        else:
            kept = len(issued)
            rl_in, ca_in, cb_in = send_edges(k)
            for z in range(1, depth):
                lower_layer(k, z)
            ru_in = exchange(ru_out.at[k], ru.at[k], (lat_prev, ha), lat_dn, lat_up)
            finish_sends(len(issued) - kept + 1 + 3 * n_ha)

        if k == last:
            dens_lo_in()
            dens_hi_in()
            extended = jnp.concatenate([dens_lo[...], dens[...], dens_hi[...]], 0)
            filtered = filter_rows(extended, rows + 2 * RADIUS)
            slope = jnp.tanh(sharpness * (filtered - threshold))
            deriv[...] = (
                sharpness
                * (1.0 - slope * slope)
                / (jnp.tanh(sharpness * threshold) + jnp.tanh(sharpness * (1.0 - threshold)))
            )

        new = magnetic(k)
        rl_in()
        low = joined(rlab) if k == last else rl[k]
        for z in range(depth):
            new[1, z, 0:1] = new[1, z, 0:1] - time_step * low[depth + z : depth + z + 1]
            new[2, z, 0:1] = new[2, z, 0:1] + time_step * low[z : z + 1]

        ru_in()
        ca_in()
        own = joined(rlab_out) if k == last else rl_out[k]
        high = joined(ruab) if k == last else ru[k]
        corner = joined(caab) if k == last else ca[k]
        high_y = (high[0:depth] - time_step * own[depth : 2 * depth]) * inside_lat
        high_z = (high[depth : 2 * depth] + time_step * own[0:depth]) * inside_lat
        first_y = high_y[0:1] + time_step * inside_lat * corner

        def finish_layer(z, above_x, above_y, acc):
            hx, hy, hv = new[0, z], new[1, z], new[2, z]
            edge_y = first_y if z == 0 else high_y[z : z + 1]
            edge_z = high_z[z : z + 1]
            curl_x = y_upper(hv) - hv - (above_y - hy)
            curl_y = above_x - hx - (x_upper(hv, edge_z) - hv)
            curl_z = x_upper(hy, edge_y) - hy - (y_upper(hx) - hx)
            fields = [
                e[0, z] + time_step * curl_x,
                e[1, z] + time_step * curl_y,
                e[2, z] + time_step * curl_z,
            ]
            if k == last:
                for c in range(comps):
                    fields[c] = fields[c] + gain * (wgrid[z] * field(k, c, z))
            if k > 0:
                return scale_layer(k - 1, z, fields, acc)
            for c in range(comps):
                out_e[c, z] = fields[c]
            return acc

        for z in range(1, top):
            acc = finish_layer(z, new[0, z + 1], new[1, z + 1], acc)

        if k == 0:
            for arrive in plane_in:
                arrive()
            whole = plane[...]
            low = plane_lo[0]
            high = plane_hi[0]
            for d in range(1, n_ha):
                whole = whole + plane_ha[d - 1]
                low = low + plane_lo[d]
                high = high + plane_hi[d]
            product = jnp.concatenate([low, whole, high], 0) * deriv[...]
            out_g[...] = filter_rows(product, rows)

        if k == last:
            zla_in()
            zlb_in()
            below_x, below_y = zlab[0, 0] + gain * zlab[1, 0], zlab[0, 1] + gain * zlab[1, 1]
        else:
            zl_in()
            below_x, below_y = zl[k, 0], zl[k, 1]
        new[0, 0] = new[0, 0] - time_step * below_y
        new[1, 0] = new[1, 0] + time_step * below_x
        if top > 0:
            acc = finish_layer(0, new[0, 1], new[1, 1], acc)
            if k > 0:
                lower_layer(k - 1, 0)
                if k > 1:
                    zu_next = send_bottom(k - 1)

        cb_in()
        if k == last:
            zua_in()
            zub_in()
            above_x, above_y = zuab[0, 0] + gain * zuab[1, 0], zuab[0, 1] + gain * zuab[1, 1]
            own_x, own_y = ab[0, 0, top] + gain * ab[1, 0, top], ab[0, 1, top] + gain * ab[1, 1, top]
            corner = joined(cbab)
        else:
            zu_in()
            above_x, above_y = zu[k, 0], zu[k, 1]
            own_x, own_y = s[k, 0, top], s[k, 1, top]
            corner = cb[k]
        above_x = above_x - time_step * own_y
        above_y = above_y + time_step * own_x
        above_y = above_y - jnp.where(row == 0, time_step * corner, 0.0)
        acc = finish_layer(top, above_x * inside_ha, above_y * inside_ha, acc)
        if k == 1:
            plane_in = send_plane(acc)
        if k > 0:
            if top == 0:
                lower_layer(k - 1, 0)
            if top == 0 or k == 1:
                zu_next = send_bottom(k - 1)
            zu_in = zu_next
            zl_in = send_top(k - 1)

    finish_sends()


def store(e, h, g, out_e, out_h, out_g, sem):
    copies = [
        pltpu.make_async_copy(e, out_e, sem.at[0]),
        pltpu.make_async_copy(h, out_h, sem.at[1]),
        pltpu.make_async_copy(g, out_g, sem.at[2]),
    ]
    for copy in copies:
        copy.start()
    for copy in copies:
        copy.wait()


def body(
    adjoint_e, adjoint_h, saved_e, labels, eps_table, chi_table, density, mon_cells, mon_weight
):
    n_lat, n_ha = lax.axis_size("lat"), lax.axis_size("ha")
    steps, comps, depth, rows, width = saved_e.shape
    entries = mon_cells.shape[0]
    f32 = jnp.float32
    block = (comps, depth, rows, width)
    group = 2 if n_lat % 2 == 0 else 1
    members, groups = group * n_ha, n_lat // group
    copies = (members - 1) + (groups - 1) + 4 + 6 * steps + 3 * n_ha - 1
    vmem = pl.BlockSpec(memory_space=pltpu.VMEM)
    hbm = pl.BlockSpec(memory_space=pltpu.HBM)
    scratch = [
        pltpu.VMEM(block, f32),
        pltpu.VMEM(block, f32),
        pltpu.VMEM(saved_e.shape, saved_e.dtype),
        pltpu.VMEM(labels.shape, labels.dtype),
        pltpu.VMEM((rows, width), f32),
        pltpu.VMEM((1, entries), mon_cells.dtype),
        pltpu.VMEM((1, entries), f32),
        pltpu.VMEM((depth, rows, width), f32),
        pltpu.VMEM((steps,) + block, f32),
        pltpu.VMEM((steps,) + block, f32),
        pltpu.VMEM((steps,) + block, f32),
        pltpu.VMEM((rows, width), f32),
        pltpu.VMEM((2 * RADIUS, width), f32),
        pltpu.VMEM((2 * RADIUS, width), f32),
        pltpu.VMEM((rows + 2 * RADIUS, width), f32),
        pltpu.VMEM((steps, 2, rows, width), f32),
        pltpu.VMEM((steps, 2, rows, width), f32),
        pltpu.VMEM((steps, 2, rows, width), f32),
        pltpu.VMEM((steps, 2 * depth, width), f32),
        pltpu.VMEM((steps, 2 * depth, width), f32),
        pltpu.VMEM((steps, 2 * depth, width), f32),
        pltpu.VMEM((steps, 2 * depth, width), f32),
        pltpu.VMEM((steps, 1, width), f32),
        pltpu.VMEM((steps, 1, width), f32),
        pltpu.VMEM((steps, 1, width), f32),
        pltpu.VMEM((steps, 1, width), f32),
        pltpu.SMEM(eps_table.shape, f32),
        pltpu.SMEM(chi_table.shape, f32),
        pltpu.VMEM((steps, width), f32),
        pltpu.VMEM((max(members - 1, 1), steps, width), f32),
        pltpu.VMEM((steps, width), f32),
        pltpu.VMEM((max(groups - 1, 1), steps, width), f32),
        pltpu.VMEM((2,) + block, f32),
        pltpu.VMEM((2,) + block, f32),
        pltpu.VMEM((2, 2, rows, width), f32),
        pltpu.VMEM((2, 2, rows, width), f32),
        pltpu.VMEM((2, 2, rows, width), f32),
        pltpu.VMEM((4 * depth, width), f32),
        pltpu.VMEM((4 * depth, width), f32),
        pltpu.VMEM((4 * depth, width), f32),
        pltpu.VMEM((4 * depth, width), f32),
        pltpu.VMEM((2, width), f32),
        pltpu.VMEM((2, width), f32),
        pltpu.VMEM((2, width), f32),
        pltpu.VMEM((2, width), f32),
        pltpu.VMEM((max(n_ha - 1, 1), rows, width), f32),
        pltpu.VMEM((n_ha, RADIUS, width), f32),
        pltpu.VMEM((n_ha, RADIUS, width), f32),
        pltpu.SemaphoreType.DMA((9,)),
        pltpu.SemaphoreType.DMA((copies,)),
        pltpu.SemaphoreType.DMA((copies,)),
    ]
    results = pl.pallas_call(
        functools.partial(kernel, n_lat, n_ha),
        out_shape=(
            pltpu.VMEM(block, f32),
            pltpu.VMEM(block, f32),
            pltpu.VMEM((rows, width), f32),
        ),
        in_specs=[hbm] * 9,
        out_specs=(vmem, vmem, vmem),
        scratch_shapes=scratch,
        compiler_params=pltpu.CompilerParams(
            collective_id=0, has_side_effects=True, vmem_limit_bytes=63 * 2**20
        ),
    )(
        adjoint_e,
        adjoint_h,
        saved_e,
        labels,
        eps_table,
        chi_table,
        density,
        mon_cells.reshape(1, entries),
        mon_weight.reshape(1, entries),
    )
    return pl.pallas_call(
        store,
        out_shape=(
            jax.ShapeDtypeStruct(block, f32),
            jax.ShapeDtypeStruct(block, f32),
            jax.ShapeDtypeStruct((rows, width), f32),
        ),
        in_specs=[vmem] * 3,
        out_specs=(hbm, hbm, hbm),
        scratch_shapes=[pltpu.SemaphoreType.DMA((3,))],
        compiler_params=pltpu.CompilerParams(vmem_limit_bytes=2**20),
    )(*results)


def solution(mesh):
    return jax.shard_map(
        body,
        mesh=mesh,
        in_specs=(
            P(None, "ha", "lat", None),
            P(None, "ha", "lat", None),
            P(None, None, "ha", "lat", None),
            P("ha", "lat", None),
            P(),
            P(),
            P("lat", None),
            P(("lat", "ha")),
            P(("lat", "ha")),
        ),
        out_specs=(P(None, "ha", "lat", None), P(None, "ha", "lat", None), P("lat", None)),
        check_vma=False,
    )
```

```python
import functools

import jax
import jax.numpy as jnp
from jax import lax
from jax.experimental import pallas as pl
from jax.experimental.pallas import tpu as pltpu
from jax.sharding import PartitionSpec as P

RADIUS = 16

sharpness = 8.0
threshold = 0.5
time_step = 0.5
epsilon = 1e-05

MESH = pl.DeviceIdType.MESH


def cone(offset):
    return jnp.maximum(RADIUS + 1 - jnp.abs(offset), 0).astype(jnp.float32) / (RADIUS + 1) ** 2


def filter_rows(padded, rows):
    width = padded.shape[1]
    i = lax.broadcasted_iota(jnp.int32, (width, width), 0)
    j = lax.broadcasted_iota(jnp.int32, (width, width), 1)
    smoothed = jnp.dot(
        padded, cone(i - j), precision=lax.Precision.HIGHEST, preferred_element_type=jnp.float32
    )
    row_out = lax.broadcasted_iota(jnp.int32, (rows, rows + 2 * RADIUS), 0)
    row_in = lax.broadcasted_iota(jnp.int32, (rows, rows + 2 * RADIUS), 1)
    return jnp.dot(
        cone(row_in - RADIUS - row_out),
        smoothed,
        precision=lax.Precision.HIGHEST,
        preferred_element_type=jnp.float32,
    )


def kernel(
    n_lat,
    n_ha,
    adj_e,
    adj_h,
    saved,
    labels,
    eps_table,
    chi_table,
    density,
    cells,
    weight,
    out_e,
    out_h,
    out_g,
    e,
    h0,
    sv,
    lb,
    dens,
    cl,
    wt,
    wgrid,
    s,
    hh,
    rinv,
    plane,
    dens_lo,
    dens_hi,
    deriv,
    hz_out,
    zl,
    zu,
    rl_out,
    rl,
    ru_out,
    ru,
    ca_out,
    ca,
    cb_out,
    cb,
    eps_of,
    chi_of,
    pw_out,
    pw_in,
    pw_sum,
    pw_all,
    ab,
    pab,
    hzab_out,
    zuab,
    zlab,
    rlab_out,
    rlab,
    ruab_out,
    ruab,
    caab_out,
    caab,
    cbab_out,
    cbab,
    plane_ha,
    plane_lo,
    plane_hi,
    local_sem,
    send_sem,
    recv_sem,
):
    steps, comps, depth, rows, width = sv.shape
    regions = eps_table.shape[0]
    entries = cl.shape[1]
    last, top = steps - 1, depth - 1
    devices = n_lat * n_ha
    lat = lax.axis_index("lat")
    ha = lax.axis_index("ha")
    lat_dn, lat_up = lat > 0, lat < n_lat - 1
    ha_dn, ha_up = ha > 0, ha < n_ha - 1
    lat_prev, lat_next = jnp.maximum(lat - 1, 0), jnp.minimum(lat + 1, n_lat - 1)
    ha_prev, ha_next = jnp.maximum(ha - 1, 0), jnp.minimum(ha + 1, n_ha - 1)

    pairs = [
        (cells, cl),
        (weight, wt),
        (saved, sv),
        (labels, lb),
        (adj_h, h0),
        (adj_e, e),
        (density, dens),
        (eps_table, eps_of),
        (chi_table, chi_of),
    ]
    loads = [pltpu.make_async_copy(a, b, local_sem.at[i]) for i, (a, b) in enumerate(pairs)]
    for load in loads:
        load.start()

    group = 2 if n_lat % 2 == 0 else 1
    place, number = lax.rem(lat, group), lax.div(lat, group)
    members, groups = group * n_ha, n_lat // group

    def member(d):
        there = lax.rem(place * n_ha + ha + d, members)
        return (number * group + lax.div(there, n_ha), lax.rem(there, n_ha))

    def counterpart(d):
        return (lax.rem(number + d, groups) * group + place, ha)

    barrier = pltpu.get_barrier_semaphore()

    def greet(target):
        pl.semaphore_signal(barrier, inc=1, device_id=target, device_id_type=MESH)

    for d in range(1, members):
        greet(member(d))
    for d in range(1, groups):
        greet(counterpart(d))
    greeted = (members - 1) + (groups - 1)
    if group == 2:
        outer = lat - 1 + 2 * place
        exists = jnp.logical_and(outer >= 0, outer < n_lat)
        beyond = [(exists, outer, d) for d in range(n_ha)]
    else:
        beyond = [(lat_dn, lat_prev, d) for d in range(1, n_ha)]
        beyond += [(lat_up, lat_next, d) for d in range(1, n_ha)]
    for condition, there, d in beyond:
        pl.when(condition)(functools.partial(greet, (there, lax.rem(ha + d, n_ha))))
        greeted = greeted + condition.astype(jnp.int32)

    issued = []
    numbers = iter(range(send_sem.shape[0]))

    def finish_sends(kept=0):
        while len(issued) > kept:
            issued.pop(0)()

    def exchange(src, dst, target, sends=None, receives=None):
        index = next(numbers)

        def copy():
            return pltpu.make_async_remote_copy(
                src_ref=src,
                dst_ref=dst,
                send_sem=send_sem.at[index],
                recv_sem=recv_sem.at[index],
                device_id=target,
                device_id_type=MESH,
            )

        def guarded(condition, action):
            if condition is None:
                action()
            else:
                pl.when(condition)(action)

        issued.append(lambda: guarded(sends, lambda: copy().wait_send()))
        guarded(sends, lambda: copy().start())

        def arrive():
            guarded(receives, lambda: copy().wait_recv())
            if receives is not None:

                @pl.when(jnp.logical_not(receives))
                def _():
                    dst[...] = jnp.zeros(dst.shape, dst.dtype)

        return arrive

    def field(k, c, z):
        return sv[k, c, z].astype(jnp.float32)

    lane = lax.broadcasted_iota(jnp.int32, (rows, width), 1)
    row = lax.broadcasted_iota(jnp.int32, (rows, width), 0)
    inside_ha = ha_up.astype(jnp.float32)
    inside_lat = lat_up.astype(jnp.float32)

    def y_lower(v):
        return jnp.where(lane == 0, 0.0, pltpu.roll(v, 1, 1))

    def y_upper(v):
        return jnp.where(lane == width - 1, 0.0, pltpu.roll(v, width - 1, 1))

    def x_lower(v, edge):
        return jnp.where(row == 0, edge, pltpu.roll(v, 1, 0))

    def x_upper(v, edge):
        return jnp.where(row == rows - 1, edge, pltpu.roll(v, rows - 1, 0))

    def material(z):
        label = lb[z]
        eps = jnp.full((rows, width), eps_of[0], jnp.float32)
        chi = jnp.full((rows, width), 3.0 * chi_of[0], jnp.float32)
        for region in range(1, regions):
            hit = label == region
            eps = jnp.where(hit, eps_of[region], eps)
            chi = jnp.where(hit, 3.0 * chi_of[region], chi)
        return eps, chi

    def lower_parts(src, z):
        sx, sy, sz = src[0, z], src[1, z], src[2, z]
        curl_x = sz - y_lower(sz) - sy
        curl_y = sx - (sz - x_lower(sz, 0.0))
        curl_z = sy - x_lower(sy, 0.0) - (sx - y_lower(sx))
        if z > 0:
            curl_x = curl_x + src[1, z - 1]
            curl_y = curl_y - src[0, z - 1]
        return curl_x, curl_y, curl_z

    def part_a(z):
        eps, chi = material(z)
        inner = jnp.zeros((rows, width), jnp.float32)
        for c in range(comps):
            f = field(last, c, z)
            inverse = 1.0 / (eps + chi * f * f)
            ab[1, c, z] = f * inverse
            inner = inner + put_part(0, c, z, e[c, z] * inverse) * f
        return jnp.where(lb[z] == 0, inner, 0.0)

    def part_b(z):
        inner = jnp.zeros((rows, width), jnp.float32)
        for c in range(comps):
            inner = inner + put_part(1, c, z, wgrid[z] * ab[1, c, z]) * field(last, c, z)
        return jnp.where(lb[z] == 0, inner, 0.0)

    def put_part(i, c, z, value):
        ab[i, c, z] = value
        if c > 0:
            slot = (2 * i + c - 1) * depth + z
            rlab_out[slot : slot + 1, :] = value[rows - 1 : rows]
        if c == 0 and z == top:
            caab_out[i : i + 1, :] = value[0:1]
        if c == 2 and z == 0:
            cbab_out[i : i + 1, :] = value[rows - 1 : rows]
        return value

    def part_curl(i, z):
        curl = lower_parts(ab.at[i], z)
        for c in range(comps):
            value = -time_step * curl[c]
            if i == 0:
                value = h0[c, z] + value
            pab[i, c, z] = value
            if z == 0 and c < 2:
                hzab_out[i, c] = value
            if c > 0:
                slot = (2 * i + c - 1) * depth + z
                ruab_out[slot : slot + 1, :] = value[0:1]

    def ends(part, i):
        inner = part(0)
        part_curl(i, 0)
        arrivals = [exchange(hzab_out.at[i], zuab.at[i], (lat, ha_prev), ha_dn, ha_up)]
        if top > 0:
            inner = inner + part(top)
        arrivals.append(
            exchange(ab.at[i, pl.ds(0, 2), top], zlab.at[i], (lat, ha_next), ha_up, ha_dn)
        )
        return inner, arrivals

    loads[0].wait()
    loads[1].wait()
    cell = cl[...]
    amount = wt[...]
    first = amount.astype(jnp.bfloat16)
    left = amount - first.astype(jnp.float32)
    second = left.astype(jnp.bfloat16)
    third = (left - second.astype(jnp.float32)).astype(jnp.bfloat16)
    line = lax.broadcasted_iota(jnp.int32, (depth * rows, entries), 0) == cell // width
    lane_hit = lax.broadcasted_iota(jnp.int32, (width, entries), 0) == lax.rem(cell, width)
    line = jnp.where(line, 1.0, 0.0).astype(jnp.bfloat16)
    total = jnp.zeros((depth * rows, width), jnp.float32)
    for part in (third, second, first):
        spread = jnp.where(lane_hit, part.astype(jnp.float32), 0.0).astype(jnp.bfloat16)
        total = total + lax.dot_general(
            line, spread, (((1,), (1,)), ((), ())), preferred_element_type=jnp.float32
        )
    for z in range(depth):
        wgrid[z] = total[z * rows : (z + 1) * rows]

    loads[2].wait()
    for k in range(steps):
        acc = jnp.zeros((rows, width), jnp.float32)
        for z in range(depth):
            square = jnp.zeros((rows, width), jnp.float32)
            for c in range(comps):
                f = field(k, c, z)
                square = square + f * f
            acc = acc + wgrid[z] * square
        pw_out[k : k + 1, :] = jnp.sum(acc, 0, keepdims=True)

    pl.semaphore_wait(barrier, greeted)
    members_in = [exchange(pw_out, pw_in.at[d - 1], member(d)) for d in range(1, members)]

    for index in (3, 4, 5, 7, 8):
        loads[index].wait()
    inner_a, (zua_in, zla_in) = ends(part_a, 0)
    inner_b, (zub_in, zlb_in) = ends(part_b, 1)
    for z in range(1, top):
        inner_a = inner_a + part_a(z)
        inner_b = inner_b + part_b(z)
    corner_a = (
        (lat_prev, ha_next),
        jnp.logical_and(lat_dn, ha_up),
        jnp.logical_and(lat_up, ha_dn),
    )
    corner_b = (
        (lat_next, ha_prev),
        jnp.logical_and(lat_up, ha_dn),
        jnp.logical_and(lat_dn, ha_up),
    )
    rlab_in = exchange(rlab_out, rlab, (lat_next, ha), lat_up, lat_dn)
    caab_in = exchange(caab_out, caab, *corner_a)
    cbab_in = exchange(cbab_out, cbab, *corner_b)

    for arrive in members_in:
        arrive()
    power_rows = pw_out[...]
    for d in range(1, members):
        power_rows = power_rows + pw_in[d - 1]
    pw_sum[...] = power_rows
    groups_in = [exchange(pw_sum, pw_all.at[d - 1], counterpart(d)) for d in range(1, groups)]

    for z in range(1, depth):
        part_curl(0, z)
        part_curl(1, z)
    ruab_in = exchange(ruab_out, ruab, (lat_prev, ha), lat_dn, lat_up)

    loads[6].wait()
    dens_lo_in = exchange(
        dens.at[pl.ds(rows - 2 * RADIUS, 2 * RADIUS)], dens_lo, (lat_next, ha), lat_up, lat_dn
    )
    dens_hi_in = exchange(
        dens.at[pl.ds(0, 2 * RADIUS)], dens_hi, (lat_prev, ha), lat_dn, lat_up
    )

    for z in range(depth):
        eps, chi = material(z)
        for k in range(last):
            for c in range(comps):
                f = field(k, c, z)
                rinv[k, c, z] = 1.0 / (eps + chi * f * f)

    for arrive in groups_in:
        arrive()
    for d in range(1, groups):
        power_rows = power_rows + pw_all[d - 1]
    power = jnp.sum(power_rows, 1, keepdims=True) / (entries * devices) + epsilon
    inverse_power = 1.0 / power

    def scale_layer(k, z, fields, acc):
        gain = inverse_power[k : k + 1, :]
        inner = jnp.zeros((rows, width), jnp.float32)
        for c in range(comps):
            f = field(k, c, z)
            now = fields[c] + gain * (wgrid[z] * f)
            value = now * rinv[k, c, z]
            e[c, z] = now
            s[k, c, z] = value
            inner = inner + value * f
            if c > 0:
                slot = (c - 1) * depth + z
                rl_out[k, slot : slot + 1, :] = value[rows - 1 : rows]
            if c == 0 and z == top:
                ca_out[k] = value[0:1]
            if c == 2 and z == 0:
                cb_out[k] = value[rows - 1 : rows]
        return acc + jnp.where(lb[z] == 0, inner, 0.0)

    def magnetic(k):
        return out_h if k == 0 else hh.at[k]

    def lower_layer(k, z):
        old = magnetic(k + 1)
        new = magnetic(k)
        curl_x, curl_y, curl_z = lower_parts(s.at[k], z)
        values = (
            old[0, z] - time_step * curl_x,
            old[1, z] - time_step * curl_y,
            old[2, z] - time_step * curl_z,
        )
        for c in range(comps):
            new[c, z] = values[c]
            if z == 0 and c < 2:
                hz_out[k, c] = values[c]
            if c > 0:
                slot = (c - 1) * depth + z
                ru_out[k, slot : slot + 1, :] = values[c][0:1]

    def send_bottom(k):
        return exchange(hz_out.at[k], zu.at[k], (lat, ha_prev), ha_dn, ha_up)

    def send_top(k):
        return exchange(s.at[k, pl.ds(0, 2), top], zl.at[k], (lat, ha_next), ha_up, ha_dn)

    def send_edges(k):
        return (
            exchange(rl_out.at[k], rl.at[k], (lat_next, ha), lat_up, lat_dn),
            exchange(ca_out.at[k], ca.at[k], *corner_a),
            exchange(cb_out.at[k], cb.at[k], *corner_b),
        )

    def send_plane(acc):
        plane[...] = acc
        arrivals = []
        for d in reversed(range(n_ha)):
            other = lax.rem(ha + d, n_ha)
            arrivals.append(
                exchange(
                    plane.at[pl.ds(rows - RADIUS, RADIUS)],
                    plane_lo.at[d],
                    (lat_next, other),
                    lat_up,
                    lat_dn,
                )
            )
            arrivals.append(
                exchange(
                    plane.at[pl.ds(0, RADIUS)],
                    plane_hi.at[d],
                    (lat_prev, other),
                    lat_dn,
                    lat_up,
                )
            )
        for d in range(1, n_ha):
            arrivals.append(exchange(plane, plane_ha.at[d - 1], (lat, lax.rem(ha + d, n_ha))))
        return arrivals

    gain = inverse_power[last : last + 1, :]
    acc = inner_a + gain * inner_b
    for z in range(depth):
        for c in range(comps):
            magnetic(last)[c, z] = pab[0, c, z] + gain * pab[1, c, z]

    def joined(ref):
        half = ref.shape[0] // 2
        return ref[pl.ds(0, half)] + gain * ref[pl.ds(half, half)]

    if last == 0:
        plane_in = send_plane(acc)
    for k in reversed(range(steps)):
        if k == last:
            rl_in, ru_in, ca_in, cb_in = rlab_in, ruab_in, caab_in, cbab_in
        else:
            kept = len(issued)
            rl_in, ca_in, cb_in = send_edges(k)
            for z in range(1, depth):
                lower_layer(k, z)
            ru_in = exchange(ru_out.at[k], ru.at[k], (lat_prev, ha), lat_dn, lat_up)
            finish_sends(len(issued) - kept + 1 + 3 * n_ha)

        if k == last:
            dens_lo_in()
            dens_hi_in()
            extended = jnp.concatenate([dens_lo[...], dens[...], dens_hi[...]], 0)
            filtered = filter_rows(extended, rows + 2 * RADIUS)
            slope = jnp.tanh(sharpness * (filtered - threshold))
            deriv[...] = (
                sharpness
                * (1.0 - slope * slope)
                / (jnp.tanh(sharpness * threshold) + jnp.tanh(sharpness * (1.0 - threshold)))
            )

        new = magnetic(k)
        rl_in()
        low = joined(rlab) if k == last else rl[k]
        for z in range(depth):
            new[1, z, 0:1] = new[1, z, 0:1] - time_step * low[depth + z : depth + z + 1]
            new[2, z, 0:1] = new[2, z, 0:1] + time_step * low[z : z + 1]

        ru_in()
        ca_in()
        own = joined(rlab_out) if k == last else rl_out[k]
        high = joined(ruab) if k == last else ru[k]
        corner = joined(caab) if k == last else ca[k]
        high_y = (high[0:depth] - time_step * own[depth : 2 * depth]) * inside_lat
        high_z = (high[depth : 2 * depth] + time_step * own[0:depth]) * inside_lat
        first_y = high_y[0:1] + time_step * inside_lat * corner

        def finish_layer(z, above_x, above_y, acc):
            hx, hy, hv = new[0, z], new[1, z], new[2, z]
            edge_y = first_y if z == 0 else high_y[z : z + 1]
            edge_z = high_z[z : z + 1]
            curl_x = y_upper(hv) - hv - (above_y - hy)
            curl_y = above_x - hx - (x_upper(hv, edge_z) - hv)
            curl_z = x_upper(hy, edge_y) - hy - (y_upper(hx) - hx)
            fields = [
                e[0, z] + time_step * curl_x,
                e[1, z] + time_step * curl_y,
                e[2, z] + time_step * curl_z,
            ]
            if k == last:
                for c in range(comps):
                    fields[c] = fields[c] + gain * (wgrid[z] * field(k, c, z))
            if k > 0:
                return scale_layer(k - 1, z, fields, acc)
            for c in range(comps):
                out_e[c, z] = fields[c]
            return acc

        for z in range(1, top):
            acc = finish_layer(z, new[0, z + 1], new[1, z + 1], acc)

        if k == last:
            zla_in()
            zlb_in()
            below_x, below_y = zlab[0, 0] + gain * zlab[1, 0], zlab[0, 1] + gain * zlab[1, 1]
        else:
            zl_in()
            below_x, below_y = zl[k, 0], zl[k, 1]
        new[0, 0] = new[0, 0] - time_step * below_y
        new[1, 0] = new[1, 0] + time_step * below_x
        if top > 0:
            acc = finish_layer(0, new[0, 1], new[1, 1], acc)
            if k > 0:
                lower_layer(k - 1, 0)
                zu_next = send_bottom(k - 1)

        cb_in()
        if k == last:
            zua_in()
            zub_in()
            above_x, above_y = zuab[0, 0] + gain * zuab[1, 0], zuab[0, 1] + gain * zuab[1, 1]
            own_x, own_y = ab[0, 0, top] + gain * ab[1, 0, top], ab[0, 1, top] + gain * ab[1, 1, top]
            corner = joined(cbab)
        else:
            zu_in()
            above_x, above_y = zu[k, 0], zu[k, 1]
            own_x, own_y = s[k, 0, top], s[k, 1, top]
            corner = cb[k]
        above_x = above_x - time_step * own_y
        above_y = above_y + time_step * own_x
        above_y = above_y - jnp.where(row == 0, time_step * corner, 0.0)
        acc = finish_layer(top, above_x * inside_ha, above_y * inside_ha, acc)
        if k > 0:
            if top == 0:
                lower_layer(k - 1, 0)
                zu_next = send_bottom(k - 1)
            zu_in = zu_next
            zl_in = send_top(k - 1)
        if k == 1:
            plane_in = send_plane(acc)

    for arrive in plane_in:
        arrive()
    whole = plane[...]
    low = plane_lo[0]
    high = plane_hi[0]
    for d in range(1, n_ha):
        whole = whole + plane_ha[d - 1]
        low = low + plane_lo[d]
        high = high + plane_hi[d]
    product = jnp.concatenate([low, whole, high], 0) * deriv[...]
    out_g[...] = filter_rows(product, rows)
    finish_sends()


def store(e, h, g, out_e, out_h, out_g, sem):
    copies = [
        pltpu.make_async_copy(e, out_e, sem.at[0]),
        pltpu.make_async_copy(h, out_h, sem.at[1]),
        pltpu.make_async_copy(g, out_g, sem.at[2]),
    ]
    for copy in copies:
        copy.start()
    for copy in copies:
        copy.wait()


def body(
    adjoint_e, adjoint_h, saved_e, labels, eps_table, chi_table, density, mon_cells, mon_weight
):
    n_lat, n_ha = lax.axis_size("lat"), lax.axis_size("ha")
    steps, comps, depth, rows, width = saved_e.shape
    entries = mon_cells.shape[0]
    f32 = jnp.float32
    block = (comps, depth, rows, width)
    group = 2 if n_lat % 2 == 0 else 1
    members, groups = group * n_ha, n_lat // group
    copies = (members - 1) + (groups - 1) + 4 + 6 * steps + 3 * n_ha - 1
    vmem = pl.BlockSpec(memory_space=pltpu.VMEM)
    hbm = pl.BlockSpec(memory_space=pltpu.HBM)
    scratch = [
        pltpu.VMEM(block, f32),
        pltpu.VMEM(block, f32),
        pltpu.VMEM(saved_e.shape, saved_e.dtype),
        pltpu.VMEM(labels.shape, labels.dtype),
        pltpu.VMEM((rows, width), f32),
        pltpu.VMEM((1, entries), mon_cells.dtype),
        pltpu.VMEM((1, entries), f32),
        pltpu.VMEM((depth, rows, width), f32),
        pltpu.VMEM((steps,) + block, f32),
        pltpu.VMEM((steps,) + block, f32),
        pltpu.VMEM((steps,) + block, f32),
        pltpu.VMEM((rows, width), f32),
        pltpu.VMEM((2 * RADIUS, width), f32),
        pltpu.VMEM((2 * RADIUS, width), f32),
        pltpu.VMEM((rows + 2 * RADIUS, width), f32),
        pltpu.VMEM((steps, 2, rows, width), f32),
        pltpu.VMEM((steps, 2, rows, width), f32),
        pltpu.VMEM((steps, 2, rows, width), f32),
        pltpu.VMEM((steps, 2 * depth, width), f32),
        pltpu.VMEM((steps, 2 * depth, width), f32),
        pltpu.VMEM((steps, 2 * depth, width), f32),
        pltpu.VMEM((steps, 2 * depth, width), f32),
        pltpu.VMEM((steps, 1, width), f32),
        pltpu.VMEM((steps, 1, width), f32),
        pltpu.VMEM((steps, 1, width), f32),
        pltpu.VMEM((steps, 1, width), f32),
        pltpu.SMEM(eps_table.shape, f32),
        pltpu.SMEM(chi_table.shape, f32),
        pltpu.VMEM((steps, width), f32),
        pltpu.VMEM((max(members - 1, 1), steps, width), f32),
        pltpu.VMEM((steps, width), f32),
        pltpu.VMEM((max(groups - 1, 1), steps, width), f32),
        pltpu.VMEM((2,) + block, f32),
        pltpu.VMEM((2,) + block, f32),
        pltpu.VMEM((2, 2, rows, width), f32),
        pltpu.VMEM((2, 2, rows, width), f32),
        pltpu.VMEM((2, 2, rows, width), f32),
        pltpu.VMEM((4 * depth, width), f32),
        pltpu.VMEM((4 * depth, width), f32),
        pltpu.VMEM((4 * depth, width), f32),
        pltpu.VMEM((4 * depth, width), f32),
        pltpu.VMEM((2, width), f32),
        pltpu.VMEM((2, width), f32),
        pltpu.VMEM((2, width), f32),
        pltpu.VMEM((2, width), f32),
        pltpu.VMEM((max(n_ha - 1, 1), rows, width), f32),
        pltpu.VMEM((n_ha, RADIUS, width), f32),
        pltpu.VMEM((n_ha, RADIUS, width), f32),
        pltpu.SemaphoreType.DMA((9,)),
        pltpu.SemaphoreType.DMA((copies,)),
        pltpu.SemaphoreType.DMA((copies,)),
    ]
    results = pl.pallas_call(
        functools.partial(kernel, n_lat, n_ha),
        out_shape=(
            pltpu.VMEM(block, f32),
            pltpu.VMEM(block, f32),
            pltpu.VMEM((rows, width), f32),
        ),
        in_specs=[hbm] * 9,
        out_specs=(vmem, vmem, vmem),
        scratch_shapes=scratch,
        compiler_params=pltpu.CompilerParams(
            collective_id=0, has_side_effects=True, vmem_limit_bytes=63 * 2**20
        ),
    )(
        adjoint_e,
        adjoint_h,
        saved_e,
        labels,
        eps_table,
        chi_table,
        density,
        mon_cells.reshape(1, entries),
        mon_weight.reshape(1, entries),
    )
    return pl.pallas_call(
        store,
        out_shape=(
            jax.ShapeDtypeStruct(block, f32),
            jax.ShapeDtypeStruct(block, f32),
            jax.ShapeDtypeStruct((rows, width), f32),
        ),
        in_specs=[vmem] * 3,
        out_specs=(hbm, hbm, hbm),
        scratch_shapes=[pltpu.SemaphoreType.DMA((3,))],
        compiler_params=pltpu.CompilerParams(vmem_limit_bytes=2**20),
    )(*results)


def solution(mesh):
    return jax.shard_map(
        body,
        mesh=mesh,
        in_specs=(
            P(None, "ha", "lat", None),
            P(None, "ha", "lat", None),
            P(None, None, "ha", "lat", None),
            P("ha", "lat", None),
            P(),
            P(),
            P("lat", None),
            P(("lat", "ha")),
            P(("lat", "ha")),
        ),
        out_specs=(P(None, "ha", "lat", None), P(None, "ha", "lat", None), P("lat", None)),
        check_vma=False,
    )
```

```python
import functools

import jax
import jax.numpy as jnp
from jax import lax
from jax.experimental import pallas as pl
from jax.experimental.pallas import tpu as pltpu
from jax.sharding import PartitionSpec as P

RADIUS = 16

sharpness = 8.0
threshold = 0.5
time_step = 0.5
epsilon = 1e-05

MESH = pl.DeviceIdType.MESH


def cone(shape, shift):
    offset = lax.broadcasted_iota(jnp.int32, shape, 1) - lax.broadcasted_iota(jnp.int32, shape, 0)
    weights = jnp.maximum(RADIUS + 1 - jnp.abs(offset - shift), 0)
    return weights.astype(jnp.float32).astype(jnp.bfloat16)


def pieces(value):
    first = value.astype(jnp.bfloat16)
    left = value - first.astype(jnp.float32)
    second = left.astype(jnp.bfloat16)
    third = (left - second.astype(jnp.float32)).astype(jnp.bfloat16)
    return third, second, first


def filter_rows(padded, across, downward):
    scale = 1.0 / (RADIUS + 1) ** 2
    smoothed = sum(
        jnp.dot(part, across, preferred_element_type=jnp.float32) for part in pieces(padded)
    )
    return scale * sum(
        jnp.dot(downward, part, preferred_element_type=jnp.float32)
        for part in pieces(scale * smoothed)
    )


def kernel(
    n_lat,
    n_ha,
    adj_e,
    adj_h,
    saved,
    labels,
    eps_table,
    chi_table,
    density,
    cells,
    weight,
    out_e,
    out_h,
    out_g,
    e,
    h0,
    sv,
    lb,
    dens,
    cl,
    wt,
    wgrid,
    s,
    hh,
    rinv,
    plane,
    dens_lo,
    dens_hi,
    deriv,
    hz_out,
    zl,
    zu,
    rl_out,
    rl,
    ru_out,
    ru,
    ca_out,
    ca,
    cb_out,
    cb,
    eps_of,
    chi_of,
    cone_y,
    cone_x,
    cone_wide,
    pw_out,
    pw_in,
    pw_sum,
    pw_all,
    ab,
    pab,
    hzab_out,
    zuab,
    zlab,
    rlab_out,
    rlab,
    ruab_out,
    ruab,
    caab_out,
    caab,
    cbab_out,
    cbab,
    plane_ha,
    plane_lo,
    plane_hi,
    local_sem,
    send_sem,
    recv_sem,
):
    steps, comps, depth, rows, width = sv.shape
    regions = eps_table.shape[0]
    entries = cl.shape[1]
    last, top = steps - 1, depth - 1
    devices = n_lat * n_ha
    lat = lax.axis_index("lat")
    ha = lax.axis_index("ha")
    lat_dn, lat_up = lat > 0, lat < n_lat - 1
    ha_dn, ha_up = ha > 0, ha < n_ha - 1
    lat_prev, lat_next = jnp.maximum(lat - 1, 0), jnp.minimum(lat + 1, n_lat - 1)
    ha_prev, ha_next = jnp.maximum(ha - 1, 0), jnp.minimum(ha + 1, n_ha - 1)

    pairs = [
        (cells, cl),
        (weight, wt),
        (saved, sv),
        (labels, lb),
        (adj_h, h0),
        (adj_e, e),
        (density, dens),
        (eps_table, eps_of),
        (chi_table, chi_of),
    ]
    loads = [pltpu.make_async_copy(a, b, local_sem.at[i]) for i, (a, b) in enumerate(pairs)]
    for load in loads:
        load.start()

    group = 2 if n_lat % 2 == 0 else 1
    place, number = lax.rem(lat, group), lax.div(lat, group)
    members, groups = group * n_ha, n_lat // group

    def member(d):
        there = lax.rem(place * n_ha + ha + d, members)
        return (number * group + lax.div(there, n_ha), lax.rem(there, n_ha))

    def counterpart(d):
        return (lax.rem(number + d, groups) * group + place, ha)

    barrier = pltpu.get_barrier_semaphore()

    def greet(target):
        pl.semaphore_signal(barrier, inc=1, device_id=target, device_id_type=MESH)

    for d in range(1, members):
        greet(member(d))
    for d in range(1, groups):
        greet(counterpart(d))
    greeted = (members - 1) + (groups - 1)
    if group == 2:
        outer = lat - 1 + 2 * place
        exists = jnp.logical_and(outer >= 0, outer < n_lat)
        beyond = [(exists, outer, d) for d in range(n_ha)]
    else:
        beyond = [(lat_dn, lat_prev, d) for d in range(1, n_ha)]
        beyond += [(lat_up, lat_next, d) for d in range(1, n_ha)]
    for condition, there, d in beyond:
        pl.when(condition)(functools.partial(greet, (there, lax.rem(ha + d, n_ha))))
        greeted = greeted + condition.astype(jnp.int32)

    issued = []
    numbers = iter(range(send_sem.shape[0]))

    def finish_sends(kept=0):
        while len(issued) > kept:
            issued.pop(0)()

    def exchange(src, dst, target, sends=None, receives=None):
        index = next(numbers)

        def copy():
            return pltpu.make_async_remote_copy(
                src_ref=src,
                dst_ref=dst,
                send_sem=send_sem.at[index],
                recv_sem=recv_sem.at[index],
                device_id=target,
                device_id_type=MESH,
            )

        def guarded(condition, action):
            if condition is None:
                action()
            else:
                pl.when(condition)(action)

        issued.append(lambda: guarded(sends, lambda: copy().wait_send()))
        guarded(sends, lambda: copy().start())

        def arrive():
            guarded(receives, lambda: copy().wait_recv())
            if receives is not None:

                @pl.when(jnp.logical_not(receives))
                def _():
                    dst[...] = jnp.zeros(dst.shape, dst.dtype)

        return arrive

    def field(k, c, z):
        return sv[k, c, z].astype(jnp.float32)

    lane = lax.broadcasted_iota(jnp.int32, (rows, width), 1)
    row = lax.broadcasted_iota(jnp.int32, (rows, width), 0)
    inside_ha = ha_up.astype(jnp.float32)
    inside_lat = lat_up.astype(jnp.float32)

    def y_lower(v):
        return jnp.where(lane == 0, 0.0, pltpu.roll(v, 1, 1))

    def y_upper(v):
        return jnp.where(lane == width - 1, 0.0, pltpu.roll(v, width - 1, 1))

    def x_lower(v, edge):
        return jnp.where(row == 0, edge, pltpu.roll(v, 1, 0))

    def x_upper(v, edge):
        return jnp.where(row == rows - 1, edge, pltpu.roll(v, rows - 1, 0))

    def material(z):
        label = lb[z]
        eps = jnp.full((rows, width), eps_of[0], jnp.float32)
        chi = jnp.full((rows, width), 3.0 * chi_of[0], jnp.float32)
        for region in range(1, regions):
            hit = label == region
            eps = jnp.where(hit, eps_of[region], eps)
            chi = jnp.where(hit, 3.0 * chi_of[region], chi)
        return eps, chi

    def lower_parts(src, z):
        sx, sy, sz = src[0, z], src[1, z], src[2, z]
        curl_x = sz - y_lower(sz) - sy
        curl_y = sx - (sz - x_lower(sz, 0.0))
        curl_z = sy - x_lower(sy, 0.0) - (sx - y_lower(sx))
        if z > 0:
            curl_x = curl_x + src[1, z - 1]
            curl_y = curl_y - src[0, z - 1]
        return curl_x, curl_y, curl_z

    def part_a(z):
        eps, chi = material(z)
        inner = jnp.zeros((rows, width), jnp.float32)
        for c in range(comps):
            f = field(last, c, z)
            inverse = 1.0 / (eps + chi * f * f)
            ab[1, c, z] = f * inverse
            inner = inner + put_part(0, c, z, e[c, z] * inverse) * f
        return jnp.where(lb[z] == 0, inner, 0.0)

    def part_b(z):
        inner = jnp.zeros((rows, width), jnp.float32)
        for c in range(comps):
            inner = inner + put_part(1, c, z, wgrid[z] * ab[1, c, z]) * field(last, c, z)
        return jnp.where(lb[z] == 0, inner, 0.0)

    def put_part(i, c, z, value):
        ab[i, c, z] = value
        if c > 0:
            slot = (2 * i + c - 1) * depth + z
            rlab_out[slot : slot + 1, :] = value[rows - 1 : rows]
        if c == 0 and z == top:
            caab_out[i] = value[0:1]
        if c == 2 and z == 0:
            cbab_out[i] = value[rows - 1 : rows]
        return value

    def part_curl(i, z):
        curl = lower_parts(ab.at[i], z)
        for c in range(comps):
            value = -time_step * curl[c]
            if i == 0:
                value = h0[c, z] + value
            pab[i, c, z] = value
            if z == 0 and c < 2:
                hzab_out[i, c] = value
            if c > 0:
                slot = (2 * i + c - 1) * depth + z
                ruab_out[slot : slot + 1, :] = value[0:1]

    def ends(part, i):
        inner = part(0)
        part_curl(i, 0)
        arrivals = [
            exchange(cbab_out.at[i], cbab.at[i], *corner_b),
            exchange(hzab_out.at[i], zuab.at[i], (lat, ha_prev), ha_dn, ha_up),
        ]
        if top > 0:
            inner = inner + part(top)
        arrivals.append(exchange(caab_out.at[i], caab.at[i], *corner_a))
        arrivals.append(
            exchange(ab.at[i, pl.ds(0, 2), top], zlab.at[i], (lat, ha_next), ha_up, ha_dn)
        )
        return inner, arrivals

    cone_y[...] = cone(cone_y.shape, 0)
    cone_x[...] = cone(cone_x.shape, RADIUS)
    cone_wide[...] = cone(cone_wide.shape, RADIUS)

    loads[0].wait()
    loads[1].wait()
    cell = cl[...]
    amount = wt[...]
    line = lax.broadcasted_iota(jnp.int32, (depth * rows, entries), 0) == cell // width
    lane_hit = lax.broadcasted_iota(jnp.int32, (width, entries), 0) == lax.rem(cell, width)
    line = jnp.where(line, 1.0, 0.0).astype(jnp.bfloat16)
    total = jnp.zeros((depth * rows, width), jnp.float32)
    for part in pieces(amount):
        spread = jnp.where(lane_hit, part.astype(jnp.float32), 0.0).astype(jnp.bfloat16)
        total = total + lax.dot_general(
            line, spread, (((1,), (1,)), ((), ())), preferred_element_type=jnp.float32
        )
    for z in range(depth):
        wgrid[z] = total[z * rows : (z + 1) * rows]

    loads[2].wait()
    for k in range(steps):
        acc = jnp.zeros((rows, width), jnp.float32)
        for z in range(depth):
            square = jnp.zeros((rows, width), jnp.float32)
            for c in range(comps):
                f = field(k, c, z)
                square = square + f * f
            acc = acc + wgrid[z] * square
        pw_out[k : k + 1, :] = jnp.sum(acc, 0, keepdims=True)

    pl.semaphore_wait(barrier, greeted)
    members_in = [exchange(pw_out, pw_in.at[d - 1], member(d)) for d in range(1, members)]

    corner_a = (
        (lat_prev, ha_next),
        jnp.logical_and(lat_dn, ha_up),
        jnp.logical_and(lat_up, ha_dn),
    )
    corner_b = (
        (lat_next, ha_prev),
        jnp.logical_and(lat_up, ha_dn),
        jnp.logical_and(lat_dn, ha_up),
    )
    for index in (3, 4, 5, 7, 8):
        loads[index].wait()
    inner_a, (cba_in, zua_in, caa_in, zla_in) = ends(part_a, 0)
    inner_b, (cbb_in, zub_in, cab_in, zlb_in) = ends(part_b, 1)
    for z in range(1, top):
        inner_a = inner_a + part_a(z)
        inner_b = inner_b + part_b(z)
    rlab_in = exchange(rlab_out, rlab, (lat_next, ha), lat_up, lat_dn)

    for arrive in members_in:
        arrive()
    power_rows = pw_out[...]
    for d in range(1, members):
        power_rows = power_rows + pw_in[d - 1]
    pw_sum[...] = power_rows
    groups_in = [exchange(pw_sum, pw_all.at[d - 1], counterpart(d)) for d in range(1, groups)]

    for z in range(1, depth):
        part_curl(0, z)
        part_curl(1, z)
    ruab_in = exchange(ruab_out, ruab, (lat_prev, ha), lat_dn, lat_up)

    loads[6].wait()
    dens_lo_in = exchange(
        dens.at[pl.ds(rows - 2 * RADIUS, 2 * RADIUS)], dens_lo, (lat_next, ha), lat_up, lat_dn
    )
    dens_hi_in = exchange(
        dens.at[pl.ds(0, 2 * RADIUS)], dens_hi, (lat_prev, ha), lat_dn, lat_up
    )

    for z in range(depth):
        eps, chi = material(z)
        for k in range(last):
            for c in range(comps):
                f = field(k, c, z)
                rinv[k, c, z] = 1.0 / (eps + chi * f * f)

    for arrive in groups_in:
        arrive()
    for d in range(1, groups):
        power_rows = power_rows + pw_all[d - 1]
    power = jnp.sum(power_rows, 1, keepdims=True) / (entries * devices) + epsilon
    inverse_power = 1.0 / power

    def scale_layer(k, z, fields, acc):
        gain = inverse_power[k : k + 1, :]
        inner = jnp.zeros((rows, width), jnp.float32)
        for c in range(comps):
            f = field(k, c, z)
            now = fields[c] + gain * (wgrid[z] * f)
            value = now * rinv[k, c, z]
            e[c, z] = now
            s[k, c, z] = value
            inner = inner + value * f
            if c > 0:
                slot = (c - 1) * depth + z
                rl_out[k, slot : slot + 1, :] = value[rows - 1 : rows]
            if c == 0 and z == top:
                ca_out[k] = value[0:1]
            if c == 2 and z == 0:
                cb_out[k] = value[rows - 1 : rows]
        return acc + jnp.where(lb[z] == 0, inner, 0.0)

    def magnetic(k):
        return out_h if k == 0 else hh.at[k]

    def lower_layer(k, z):
        old = magnetic(k + 1)
        new = magnetic(k)
        curl_x, curl_y, curl_z = lower_parts(s.at[k], z)
        values = (
            old[0, z] - time_step * curl_x,
            old[1, z] - time_step * curl_y,
            old[2, z] - time_step * curl_z,
        )
        for c in range(comps):
            new[c, z] = values[c]
            if z == 0 and c < 2:
                hz_out[k, c] = values[c]
            if c > 0:
                slot = (c - 1) * depth + z
                ru_out[k, slot : slot + 1, :] = values[c][0:1]

    def send_bottom(k):
        return (
            exchange(cb_out.at[k], cb.at[k], *corner_b),
            exchange(hz_out.at[k], zu.at[k], (lat, ha_prev), ha_dn, ha_up),
        )

    def send_top(k):
        return (
            exchange(ca_out.at[k], ca.at[k], *corner_a),
            exchange(s.at[k, pl.ds(0, 2), top], zl.at[k], (lat, ha_next), ha_up, ha_dn),
        )

    def send_plane(acc):
        plane[...] = acc
        arrivals = []
        for d in reversed(range(n_ha)):
            other = lax.rem(ha + d, n_ha)
            arrivals.append(
                exchange(
                    plane.at[pl.ds(rows - RADIUS, RADIUS)],
                    plane_lo.at[d],
                    (lat_next, other),
                    lat_up,
                    lat_dn,
                )
            )
            arrivals.append(
                exchange(
                    plane.at[pl.ds(0, RADIUS)],
                    plane_hi.at[d],
                    (lat_prev, other),
                    lat_dn,
                    lat_up,
                )
            )
        for d in range(1, n_ha):
            arrivals.append(exchange(plane, plane_ha.at[d - 1], (lat, lax.rem(ha + d, n_ha))))
        return arrivals

    gain = inverse_power[last : last + 1, :]
    acc = inner_a + gain * inner_b
    for z in range(depth):
        for c in range(comps):
            magnetic(last)[c, z] = pab[0, c, z] + gain * pab[1, c, z]

    def joined(ref):
        half = ref.shape[0] // 2
        return ref[pl.ds(0, half)] + gain * ref[pl.ds(half, half)]

    if last == 0:
        plane_in = send_plane(acc)
    for k in reversed(range(steps)):
        if k == last:
            rl_in, ru_in = rlab_in, ruab_in
        else:
            kept = len(issued)
            rl_in = exchange(rl_out.at[k], rl.at[k], (lat_next, ha), lat_up, lat_dn)
            for z in range(1, depth):
                lower_layer(k, z)
            ru_in = exchange(ru_out.at[k], ru.at[k], (lat_prev, ha), lat_dn, lat_up)
            finish_sends(len(issued) - kept + 3 + 3 * n_ha)

        if k == last:
            dens_lo_in()
            dens_hi_in()
            extended = jnp.concatenate([dens_lo[...], dens[...], dens_hi[...]], 0)
            filtered = filter_rows(extended, cone_y[...], cone_wide[...])
            slope = jnp.tanh(sharpness * (filtered - threshold))
            deriv[...] = (
                sharpness
                * (1.0 - slope * slope)
                / (jnp.tanh(sharpness * threshold) + jnp.tanh(sharpness * (1.0 - threshold)))
            )

        new = magnetic(k)
        rl_in()
        low = joined(rlab) if k == last else rl[k]
        for z in range(depth):
            new[1, z, 0:1] = new[1, z, 0:1] - time_step * low[depth + z : depth + z + 1]
            new[2, z, 0:1] = new[2, z, 0:1] + time_step * low[z : z + 1]

        ru_in()
        if k == last:
            caa_in()
            cab_in()
        else:
            ca_in()
        own = joined(rlab_out) if k == last else rl_out[k]
        high = joined(ruab) if k == last else ru[k]
        corner = caab[0] + gain * caab[1] if k == last else ca[k]
        high_y = (high[0:depth] - time_step * own[depth : 2 * depth]) * inside_lat
        high_z = (high[depth : 2 * depth] + time_step * own[0:depth]) * inside_lat
        first_y = high_y[0:1] + time_step * inside_lat * corner

        def finish_layer(z, above_x, above_y, acc):
            hx, hy, hv = new[0, z], new[1, z], new[2, z]
            edge_y = first_y if z == 0 else high_y[z : z + 1]
            edge_z = high_z[z : z + 1]
            curl_x = y_upper(hv) - hv - (above_y - hy)
            curl_y = above_x - hx - (x_upper(hv, edge_z) - hv)
            curl_z = x_upper(hy, edge_y) - hy - (y_upper(hx) - hx)
            fields = [
                e[0, z] + time_step * curl_x,
                e[1, z] + time_step * curl_y,
                e[2, z] + time_step * curl_z,
            ]
            if k == last:
                for c in range(comps):
                    fields[c] = fields[c] + gain * (wgrid[z] * field(k, c, z))
            if k > 0:
                return scale_layer(k - 1, z, fields, acc)
            for c in range(comps):
                out_e[c, z] = fields[c]
            return acc

        for z in range(1, top):
            acc = finish_layer(z, new[0, z + 1], new[1, z + 1], acc)

        if k == last:
            zla_in()
            zlb_in()
            below_x, below_y = zlab[0, 0] + gain * zlab[1, 0], zlab[0, 1] + gain * zlab[1, 1]
        else:
            zl_in()
            below_x, below_y = zl[k, 0], zl[k, 1]
        new[0, 0] = new[0, 0] - time_step * below_y
        new[1, 0] = new[1, 0] + time_step * below_x
        if top > 0:
            acc = finish_layer(0, new[0, 1], new[1, 1], acc)
            if k > 0:
                lower_layer(k - 1, 0)
                cb_next, zu_next = send_bottom(k - 1)

        if k == last:
            cba_in()
            cbb_in()
            zua_in()
            zub_in()
            above_x, above_y = zuab[0, 0] + gain * zuab[1, 0], zuab[0, 1] + gain * zuab[1, 1]
            own_x, own_y = ab[0, 0, top] + gain * ab[1, 0, top], ab[0, 1, top] + gain * ab[1, 1, top]
            corner = cbab[0] + gain * cbab[1]
        else:
            cb_in()
            zu_in()
            above_x, above_y = zu[k, 0], zu[k, 1]
            own_x, own_y = s[k, 0, top], s[k, 1, top]
            corner = cb[k]
        above_x = above_x - time_step * own_y
        above_y = above_y + time_step * own_x
        above_y = above_y - jnp.where(row == 0, time_step * corner, 0.0)
        acc = finish_layer(top, above_x * inside_ha, above_y * inside_ha, acc)
        if k > 0:
            if top == 0:
                lower_layer(k - 1, 0)
                cb_next, zu_next = send_bottom(k - 1)
            cb_in, zu_in = cb_next, zu_next
            ca_in, zl_in = send_top(k - 1)
        if k == 1:
            plane_in = send_plane(acc)

    finish_sends()
    for arrive in plane_in:
        arrive()
    whole = plane[...]
    low = plane_lo[0]
    high = plane_hi[0]
    for d in range(1, n_ha):
        whole = whole + plane_ha[d - 1]
        low = low + plane_lo[d]
        high = high + plane_hi[d]
    product = jnp.concatenate([low, whole, high], 0) * deriv[...]
    out_g[...] = filter_rows(product, cone_y[...], cone_x[...])


def store(e, h, g, out_e, out_h, out_g, sem):
    copies = [
        pltpu.make_async_copy(e, out_e, sem.at[0]),
        pltpu.make_async_copy(h, out_h, sem.at[1]),
        pltpu.make_async_copy(g, out_g, sem.at[2]),
    ]
    for copy in copies:
        copy.start()
    for copy in copies:
        copy.wait()


def body(
    adjoint_e, adjoint_h, saved_e, labels, eps_table, chi_table, density, mon_cells, mon_weight
):
    n_lat, n_ha = lax.axis_size("lat"), lax.axis_size("ha")
    steps, comps, depth, rows, width = saved_e.shape
    entries = mon_cells.shape[0]
    f32 = jnp.float32
    block = (comps, depth, rows, width)
    group = 2 if n_lat % 2 == 0 else 1
    members, groups = group * n_ha, n_lat // group
    copies = (members - 1) + (groups - 1) + 6 + 6 * steps + 3 * n_ha - 1
    vmem = pl.BlockSpec(memory_space=pltpu.VMEM)
    hbm = pl.BlockSpec(memory_space=pltpu.HBM)
    scratch = [
        pltpu.VMEM(block, f32),
        pltpu.VMEM(block, f32),
        pltpu.VMEM(saved_e.shape, saved_e.dtype),
        pltpu.VMEM(labels.shape, labels.dtype),
        pltpu.VMEM((rows, width), f32),
        pltpu.VMEM((1, entries), mon_cells.dtype),
        pltpu.VMEM((1, entries), f32),
        pltpu.VMEM((depth, rows, width), f32),
        pltpu.VMEM((steps,) + block, f32),
        pltpu.VMEM((steps,) + block, f32),
        pltpu.VMEM((steps,) + block, f32),
        pltpu.VMEM((rows, width), f32),
        pltpu.VMEM((2 * RADIUS, width), f32),
        pltpu.VMEM((2 * RADIUS, width), f32),
        pltpu.VMEM((rows + 2 * RADIUS, width), f32),
        pltpu.VMEM((steps, 2, rows, width), f32),
        pltpu.VMEM((steps, 2, rows, width), f32),
        pltpu.VMEM((steps, 2, rows, width), f32),
        pltpu.VMEM((steps, 2 * depth, width), f32),
        pltpu.VMEM((steps, 2 * depth, width), f32),
        pltpu.VMEM((steps, 2 * depth, width), f32),
        pltpu.VMEM((steps, 2 * depth, width), f32),
        pltpu.VMEM((steps, 1, width), f32),
        pltpu.VMEM((steps, 1, width), f32),
        pltpu.VMEM((steps, 1, width), f32),
        pltpu.VMEM((steps, 1, width), f32),
        pltpu.SMEM(eps_table.shape, f32),
        pltpu.SMEM(chi_table.shape, f32),
        pltpu.VMEM((width, width), jnp.bfloat16),
        pltpu.VMEM((rows, rows + 2 * RADIUS), jnp.bfloat16),
        pltpu.VMEM((rows + 2 * RADIUS, rows + 4 * RADIUS), jnp.bfloat16),
        pltpu.VMEM((steps, width), f32),
        pltpu.VMEM((max(members - 1, 1), steps, width), f32),
        pltpu.VMEM((steps, width), f32),
        pltpu.VMEM((max(groups - 1, 1), steps, width), f32),
        pltpu.VMEM((2,) + block, f32),
        pltpu.VMEM((2,) + block, f32),
        pltpu.VMEM((2, 2, rows, width), f32),
        pltpu.VMEM((2, 2, rows, width), f32),
        pltpu.VMEM((2, 2, rows, width), f32),
        pltpu.VMEM((4 * depth, width), f32),
        pltpu.VMEM((4 * depth, width), f32),
        pltpu.VMEM((4 * depth, width), f32),
        pltpu.VMEM((4 * depth, width), f32),
        pltpu.VMEM((2, 1, width), f32),
        pltpu.VMEM((2, 1, width), f32),
        pltpu.VMEM((2, 1, width), f32),
        pltpu.VMEM((2, 1, width), f32),
        pltpu.VMEM((max(n_ha - 1, 1), rows, width), f32),
        pltpu.VMEM((n_ha, RADIUS, width), f32),
        pltpu.VMEM((n_ha, RADIUS, width), f32),
        pltpu.SemaphoreType.DMA((9,)),
        pltpu.SemaphoreType.DMA((copies,)),
        pltpu.SemaphoreType.DMA((copies,)),
    ]
    results = pl.pallas_call(
        functools.partial(kernel, n_lat, n_ha),
        out_shape=(
            pltpu.VMEM(block, f32),
            pltpu.VMEM(block, f32),
            pltpu.VMEM((rows, width), f32),
        ),
        in_specs=[hbm] * 9,
        out_specs=(vmem, vmem, vmem),
        scratch_shapes=scratch,
        compiler_params=pltpu.CompilerParams(
            collective_id=0, has_side_effects=True, vmem_limit_bytes=63 * 2**20
        ),
    )(
        adjoint_e,
        adjoint_h,
        saved_e,
        labels,
        eps_table,
        chi_table,
        density,
        mon_cells.reshape(1, entries),
        mon_weight.reshape(1, entries),
    )
    return pl.pallas_call(
        store,
        out_shape=(
            jax.ShapeDtypeStruct(block, f32),
            jax.ShapeDtypeStruct(block, f32),
            jax.ShapeDtypeStruct((rows, width), f32),
        ),
        in_specs=[vmem] * 3,
        out_specs=(hbm, hbm, hbm),
        scratch_shapes=[pltpu.SemaphoreType.DMA((3,))],
        compiler_params=pltpu.CompilerParams(vmem_limit_bytes=2**20),
    )(*results)


def solution(mesh):
    return jax.shard_map(
        body,
        mesh=mesh,
        in_specs=(
            P(None, "ha", "lat", None),
            P(None, "ha", "lat", None),
            P(None, None, "ha", "lat", None),
            P("ha", "lat", None),
            P(),
            P(),
            P("lat", None),
            P(("lat", "ha")),
            P(("lat", "ha")),
        ),
        out_specs=(P(None, "ha", "lat", None), P(None, "ha", "lat", None), P("lat", None)),
        check_vma=False,
    )
```

```python
import functools

import jax
import jax.numpy as jnp
from jax import lax
from jax.experimental import pallas as pl
from jax.experimental.pallas import tpu as pltpu
from jax.sharding import PartitionSpec as P

RADIUS = 16

sharpness = 8.0
threshold = 0.5
time_step = 0.5
epsilon = 1e-05

MESH = pl.DeviceIdType.MESH


def cone(shape, shift):
    offset = lax.broadcasted_iota(jnp.int32, shape, 1) - lax.broadcasted_iota(jnp.int32, shape, 0)
    weights = jnp.maximum(RADIUS + 1 - jnp.abs(offset - shift), 0)
    return weights.astype(jnp.float32).astype(jnp.bfloat16)


def pieces(value):
    first = value.astype(jnp.bfloat16)
    left = value - first.astype(jnp.float32)
    second = left.astype(jnp.bfloat16)
    third = (left - second.astype(jnp.float32)).astype(jnp.bfloat16)
    return third, second, first


def filter_rows(padded, across, downward):
    scale = 1.0 / (RADIUS + 1) ** 2
    smoothed = sum(
        jnp.dot(part, across, preferred_element_type=jnp.float32) for part in pieces(padded)
    )
    return scale * sum(
        jnp.dot(downward, part, preferred_element_type=jnp.float32)
        for part in pieces(scale * smoothed)
    )


def kernel(
    n_lat,
    n_ha,
    adj_e,
    adj_h,
    saved,
    labels,
    eps_table,
    chi_table,
    density,
    cells,
    weight,
    out_e,
    out_h,
    out_g,
    e,
    h0,
    sv,
    lb,
    dens,
    cl,
    wt,
    wgrid,
    s,
    hh,
    rinv,
    plane,
    dens_lo,
    dens_hi,
    deriv,
    hz_out,
    zl,
    zu,
    rl_out,
    rl,
    ru_out,
    ru,
    ca_out,
    ca,
    cb_out,
    cb,
    eps_of,
    chi_of,
    cone_y,
    cone_x,
    cone_wide,
    pw_out,
    pw_in,
    pw_sum,
    pw_all,
    ab,
    pab,
    hzab_out,
    zuab,
    zlab,
    rlab_out,
    rlab,
    ruab_out,
    ruab,
    caab_out,
    caab,
    cbab_out,
    cbab,
    plane_ha,
    plane_lo,
    plane_hi,
    local_sem,
    send_sem,
    recv_sem,
):
    steps, comps, depth, rows, width = sv.shape
    regions = eps_table.shape[0]
    entries = cl.shape[1]
    last, top = steps - 1, depth - 1
    devices = n_lat * n_ha
    lat = lax.axis_index("lat")
    ha = lax.axis_index("ha")
    lat_dn, lat_up = lat > 0, lat < n_lat - 1
    ha_dn, ha_up = ha > 0, ha < n_ha - 1
    lat_prev, lat_next = jnp.maximum(lat - 1, 0), jnp.minimum(lat + 1, n_lat - 1)
    ha_prev, ha_next = jnp.maximum(ha - 1, 0), jnp.minimum(ha + 1, n_ha - 1)

    pairs = [
        (cells, cl),
        (weight, wt),
        (saved, sv),
        (labels, lb),
        (adj_h, h0),
        (adj_e, e),
        (density, dens),
        (eps_table, eps_of),
        (chi_table, chi_of),
    ]
    loads = [pltpu.make_async_copy(a, b, local_sem.at[i]) for i, (a, b) in enumerate(pairs)]
    for load in loads:
        load.start()

    group = 2 if n_lat % 2 == 0 else 1
    place, number = lax.rem(lat, group), lax.div(lat, group)
    members, groups = group * n_ha, n_lat // group

    def member(d):
        there = lax.rem(place * n_ha + ha + d, members)
        return (number * group + lax.div(there, n_ha), lax.rem(there, n_ha))

    def counterpart(d):
        return (lax.rem(number + d, groups) * group + place, ha)

    barrier = pltpu.get_barrier_semaphore()

    def greet(target):
        pl.semaphore_signal(barrier, inc=1, device_id=target, device_id_type=MESH)

    for d in range(1, members):
        greet(member(d))
    for d in range(1, groups):
        greet(counterpart(d))
    greeted = (members - 1) + (groups - 1)
    if group == 2:
        outer = lat - 1 + 2 * place
        exists = jnp.logical_and(outer >= 0, outer < n_lat)
        beyond = [(exists, outer, d) for d in range(n_ha)]
    else:
        beyond = [(lat_dn, lat_prev, d) for d in range(1, n_ha)]
        beyond += [(lat_up, lat_next, d) for d in range(1, n_ha)]
    for condition, there, d in beyond:
        pl.when(condition)(functools.partial(greet, (there, lax.rem(ha + d, n_ha))))
        greeted = greeted + condition.astype(jnp.int32)

    issued = []
    numbers = iter(range(send_sem.shape[0]))

    def finish_sends(kept=0):
        while len(issued) > kept:
            issued.pop(0)()

    def exchange(src, dst, target, sends=None, receives=None):
        index = next(numbers)

        def copy():
            return pltpu.make_async_remote_copy(
                src_ref=src,
                dst_ref=dst,
                send_sem=send_sem.at[index],
                recv_sem=recv_sem.at[index],
                device_id=target,
                device_id_type=MESH,
            )

        def guarded(condition, action):
            if condition is None:
                action()
            else:
                pl.when(condition)(action)

        issued.append(lambda: guarded(sends, lambda: copy().wait_send()))
        guarded(sends, lambda: copy().start())

        def arrive():
            guarded(receives, lambda: copy().wait_recv())
            if receives is not None:

                @pl.when(jnp.logical_not(receives))
                def _():
                    dst[...] = jnp.zeros(dst.shape, dst.dtype)

        return arrive

    def field(k, c, z):
        return sv[k, c, z].astype(jnp.float32)

    lane = lax.broadcasted_iota(jnp.int32, (rows, width), 1)
    row = lax.broadcasted_iota(jnp.int32, (rows, width), 0)
    inside_ha = ha_up.astype(jnp.float32)
    inside_lat = lat_up.astype(jnp.float32)

    def y_lower(v):
        return jnp.where(lane == 0, 0.0, pltpu.roll(v, 1, 1))

    def y_upper(v):
        return jnp.where(lane == width - 1, 0.0, pltpu.roll(v, width - 1, 1))

    def x_lower(v, edge):
        return jnp.where(row == 0, edge, pltpu.roll(v, 1, 0))

    def x_upper(v, edge):
        return jnp.where(row == rows - 1, edge, pltpu.roll(v, rows - 1, 0))

    def material(z):
        label = lb[z]
        eps = jnp.full((rows, width), eps_of[0], jnp.float32)
        chi = jnp.full((rows, width), 3.0 * chi_of[0], jnp.float32)
        for region in range(1, regions):
            hit = label == region
            eps = jnp.where(hit, eps_of[region], eps)
            chi = jnp.where(hit, 3.0 * chi_of[region], chi)
        return eps, chi

    def lower_parts(src, z):
        sx, sy, sz = src[0, z], src[1, z], src[2, z]
        curl_x = sz - y_lower(sz) - sy
        curl_y = sx - (sz - x_lower(sz, 0.0))
        curl_z = sy - x_lower(sy, 0.0) - (sx - y_lower(sx))
        if z > 0:
            curl_x = curl_x + src[1, z - 1]
            curl_y = curl_y - src[0, z - 1]
        return curl_x, curl_y, curl_z

    def part_a(z):
        eps, chi = material(z)
        inner = jnp.zeros((rows, width), jnp.float32)
        for c in range(comps):
            f = field(last, c, z)
            inverse = 1.0 / (eps + chi * f * f)
            ab[1, c, z] = f * inverse
            inner = inner + put_part(0, c, z, e[c, z] * inverse) * f
        return jnp.where(lb[z] == 0, inner, 0.0)

    def part_b(z):
        inner = jnp.zeros((rows, width), jnp.float32)
        for c in range(comps):
            inner = inner + put_part(1, c, z, wgrid[z] * ab[1, c, z]) * field(last, c, z)
        return jnp.where(lb[z] == 0, inner, 0.0)

    def put_part(i, c, z, value):
        ab[i, c, z] = value
        if c > 0:
            slot = (2 * i + c - 1) * depth + z
            rlab_out[slot : slot + 1, :] = value[rows - 1 : rows]
        if c == 0 and z == top:
            caab_out[i] = value[0:1]
        if c == 2 and z == 0:
            cbab_out[i] = value[rows - 1 : rows]
        return value

    def part_curl(i, z):
        curl = lower_parts(ab.at[i], z)
        for c in range(comps):
            value = -time_step * curl[c]
            if i == 0:
                value = h0[c, z] + value
            pab[i, c, z] = value
            if z == 0 and c < 2:
                hzab_out[i, c] = value
            if c > 0:
                slot = (2 * i + c - 1) * depth + z
                ruab_out[slot : slot + 1, :] = value[0:1]

    def ends(part, i):
        inner = part(0)
        part_curl(i, 0)
        arrivals = [
            exchange(cbab_out.at[i], cbab.at[i], *corner_b),
            exchange(hzab_out.at[i], zuab.at[i], (lat, ha_prev), ha_dn, ha_up),
        ]
        if top > 0:
            inner = inner + part(top)
        arrivals.append(exchange(caab_out.at[i], caab.at[i], *corner_a))
        arrivals.append(
            exchange(ab.at[i, pl.ds(0, 2), top], zlab.at[i], (lat, ha_next), ha_up, ha_dn)
        )
        return inner, arrivals

    cone_y[...] = cone(cone_y.shape, 0)
    cone_x[...] = cone(cone_x.shape, RADIUS)
    cone_wide[...] = cone(cone_wide.shape, RADIUS)

    loads[0].wait()
    loads[1].wait()
    cell = cl[...]
    amount = wt[...]
    line = lax.broadcasted_iota(jnp.int32, (depth * rows, entries), 0) == cell // width
    lane_hit = lax.broadcasted_iota(jnp.int32, (width, entries), 0) == lax.rem(cell, width)
    line = jnp.where(line, 1.0, 0.0).astype(jnp.bfloat16)
    total = jnp.zeros((depth * rows, width), jnp.float32)
    for part in pieces(amount):
        spread = jnp.where(lane_hit, part.astype(jnp.float32), 0.0).astype(jnp.bfloat16)
        total = total + lax.dot_general(
            line, spread, (((1,), (1,)), ((), ())), preferred_element_type=jnp.float32
        )
    for z in range(depth):
        wgrid[z] = total[z * rows : (z + 1) * rows]

    loads[2].wait()
    for k in range(steps):
        acc = jnp.zeros((rows, width), jnp.float32)
        for z in range(depth):
            square = jnp.zeros((rows, width), jnp.float32)
            for c in range(comps):
                f = field(k, c, z)
                square = square + f * f
            acc = acc + wgrid[z] * square
        pw_out[k : k + 1, :] = jnp.sum(acc, 0, keepdims=True)

    pl.semaphore_wait(barrier, greeted)
    members_in = [exchange(pw_out, pw_in.at[d - 1], member(d)) for d in range(1, members)]

    corner_a = (
        (lat_prev, ha_next),
        jnp.logical_and(lat_dn, ha_up),
        jnp.logical_and(lat_up, ha_dn),
    )
    corner_b = (
        (lat_next, ha_prev),
        jnp.logical_and(lat_up, ha_dn),
        jnp.logical_and(lat_dn, ha_up),
    )
    for index in (3, 4, 5, 7, 8):
        loads[index].wait()
    inner_a, (cba_in, zua_in, caa_in, zla_in) = ends(part_a, 0)
    inner_b, (cbb_in, zub_in, cab_in, zlb_in) = ends(part_b, 1)
    for z in range(1, top):
        inner_a = inner_a + part_a(z)
        inner_b = inner_b + part_b(z)
    rlab_in = exchange(rlab_out, rlab, (lat_next, ha), lat_up, lat_dn)

    for arrive in members_in:
        arrive()
    power_rows = pw_out[...]
    for d in range(1, members):
        power_rows = power_rows + pw_in[d - 1]
    pw_sum[...] = power_rows
    groups_in = [exchange(pw_sum, pw_all.at[d - 1], counterpart(d)) for d in range(1, groups)]

    for z in range(1, depth):
        part_curl(0, z)
        part_curl(1, z)
    ruab_in = exchange(ruab_out, ruab, (lat_prev, ha), lat_dn, lat_up)

    loads[6].wait()
    dens_lo_in = exchange(
        dens.at[pl.ds(rows - 2 * RADIUS, 2 * RADIUS)], dens_lo, (lat_next, ha), lat_up, lat_dn
    )
    dens_hi_in = exchange(
        dens.at[pl.ds(0, 2 * RADIUS)], dens_hi, (lat_prev, ha), lat_dn, lat_up
    )

    for z in range(depth):
        eps, chi = material(z)
        for k in range(last):
            for c in range(comps):
                f = field(k, c, z)
                rinv[k, c, z] = 1.0 / (eps + chi * f * f)

    dens_lo_in()
    dens_hi_in()
    extended = jnp.concatenate([dens_lo[...], dens[...], dens_hi[...]], 0)
    filtered = filter_rows(extended, cone_y[...], cone_wide[...])
    slope = jnp.tanh(sharpness * (filtered - threshold))
    deriv[...] = (
        sharpness
        * (1.0 - slope * slope)
        / (jnp.tanh(sharpness * threshold) + jnp.tanh(sharpness * (1.0 - threshold)))
    )

    for arrive in groups_in:
        arrive()
    for d in range(1, groups):
        power_rows = power_rows + pw_all[d - 1]
    power = jnp.sum(power_rows, 1, keepdims=True) / (entries * devices) + epsilon
    inverse_power = 1.0 / power

    def scale_layer(k, z, fields, acc):
        gain = inverse_power[k : k + 1, :]
        inner = jnp.zeros((rows, width), jnp.float32)
        for c in range(comps):
            f = field(k, c, z)
            now = fields[c] + gain * (wgrid[z] * f)
            value = now * rinv[k, c, z]
            e[c, z] = now
            s[k, c, z] = value
            inner = inner + value * f
            if c > 0:
                slot = (c - 1) * depth + z
                rl_out[k, slot : slot + 1, :] = value[rows - 1 : rows]
            if c == 0 and z == top:
                ca_out[k] = value[0:1]
            if c == 2 and z == 0:
                cb_out[k] = value[rows - 1 : rows]
        return acc + jnp.where(lb[z] == 0, inner, 0.0)

    def magnetic(k):
        return out_h if k == 0 else hh.at[k]

    def lower_layer(k, z):
        old = magnetic(k + 1)
        new = magnetic(k)
        curl_x, curl_y, curl_z = lower_parts(s.at[k], z)
        values = (
            old[0, z] - time_step * curl_x,
            old[1, z] - time_step * curl_y,
            old[2, z] - time_step * curl_z,
        )
        for c in range(comps):
            new[c, z] = values[c]
            if z == 0 and c < 2:
                hz_out[k, c] = values[c]
            if c > 0:
                slot = (c - 1) * depth + z
                ru_out[k, slot : slot + 1, :] = values[c][0:1]

    def send_bottom(k):
        return (
            exchange(cb_out.at[k], cb.at[k], *corner_b),
            exchange(hz_out.at[k], zu.at[k], (lat, ha_prev), ha_dn, ha_up),
        )

    def send_top(k):
        return (
            exchange(ca_out.at[k], ca.at[k], *corner_a),
            exchange(s.at[k, pl.ds(0, 2), top], zl.at[k], (lat, ha_next), ha_up, ha_dn),
        )

    def send_plane(acc):
        plane[...] = acc
        arrivals = []
        for d in reversed(range(n_ha)):
            other = lax.rem(ha + d, n_ha)
            arrivals.append(
                exchange(
                    plane.at[pl.ds(rows - RADIUS, RADIUS)],
                    plane_lo.at[d],
                    (lat_next, other),
                    lat_up,
                    lat_dn,
                )
            )
            arrivals.append(
                exchange(
                    plane.at[pl.ds(0, RADIUS)],
                    plane_hi.at[d],
                    (lat_prev, other),
                    lat_dn,
                    lat_up,
                )
            )
        for d in range(1, n_ha):
            arrivals.append(exchange(plane, plane_ha.at[d - 1], (lat, lax.rem(ha + d, n_ha))))
        return arrivals

    gain = inverse_power[last : last + 1, :]
    acc = inner_a + gain * inner_b
    for z in range(depth):
        for c in range(comps):
            magnetic(last)[c, z] = pab[0, c, z] + gain * pab[1, c, z]

    def joined(ref):
        half = ref.shape[0] // 2
        return ref[pl.ds(0, half)] + gain * ref[pl.ds(half, half)]

    if last == 0:
        plane_in = send_plane(acc)
    for k in reversed(range(steps)):
        if k == last:
            rl_in, ru_in = rlab_in, ruab_in
        else:
            kept = len(issued)
            rl_in = exchange(rl_out.at[k], rl.at[k], (lat_next, ha), lat_up, lat_dn)
            for z in range(1, depth):
                lower_layer(k, z)
            ru_in = exchange(ru_out.at[k], ru.at[k], (lat_prev, ha), lat_dn, lat_up)
            finish_sends(len(issued) - kept + 3 + 3 * n_ha)

        new = magnetic(k)
        rl_in()
        low = joined(rlab) if k == last else rl[k]
        for z in range(depth):
            new[1, z, 0:1] = new[1, z, 0:1] - time_step * low[depth + z : depth + z + 1]
            new[2, z, 0:1] = new[2, z, 0:1] + time_step * low[z : z + 1]

        ru_in()
        if k == last:
            caa_in()
            cab_in()
        else:
            ca_in()
        own = joined(rlab_out) if k == last else rl_out[k]
        high = joined(ruab) if k == last else ru[k]
        corner = caab[0] + gain * caab[1] if k == last else ca[k]
        high_y = (high[0:depth] - time_step * own[depth : 2 * depth]) * inside_lat
        high_z = (high[depth : 2 * depth] + time_step * own[0:depth]) * inside_lat
        first_y = high_y[0:1] + time_step * inside_lat * corner

        def finish_layer(z, above_x, above_y, acc):
            hx, hy, hv = new[0, z], new[1, z], new[2, z]
            edge_y = first_y if z == 0 else high_y[z : z + 1]
            edge_z = high_z[z : z + 1]
            curl_x = y_upper(hv) - hv - (above_y - hy)
            curl_y = above_x - hx - (x_upper(hv, edge_z) - hv)
            curl_z = x_upper(hy, edge_y) - hy - (y_upper(hx) - hx)
            fields = [
                e[0, z] + time_step * curl_x,
                e[1, z] + time_step * curl_y,
                e[2, z] + time_step * curl_z,
            ]
            if k == last:
                for c in range(comps):
                    fields[c] = fields[c] + gain * (wgrid[z] * field(k, c, z))
            if k > 0:
                return scale_layer(k - 1, z, fields, acc)
            for c in range(comps):
                out_e[c, z] = fields[c]
            return acc

        if k == 0:
            for z in range(1, top):
                acc = finish_layer(z, new[0, z + 1], new[1, z + 1], acc)

        if k == last:
            zla_in()
            zlb_in()
            below_x, below_y = zlab[0, 0] + gain * zlab[1, 0], zlab[0, 1] + gain * zlab[1, 1]
        else:
            zl_in()
            below_x, below_y = zl[k, 0], zl[k, 1]
        new[0, 0] = new[0, 0] - time_step * below_y
        new[1, 0] = new[1, 0] + time_step * below_x
        if top > 0:
            acc = finish_layer(0, new[0, 1], new[1, 1], acc)
            if k > 0:
                lower_layer(k - 1, 0)
                cb_next, zu_next = send_bottom(k - 1)

        if k == last:
            cba_in()
            cbb_in()
            zua_in()
            zub_in()
            above_x, above_y = zuab[0, 0] + gain * zuab[1, 0], zuab[0, 1] + gain * zuab[1, 1]
            own_x, own_y = ab[0, 0, top] + gain * ab[1, 0, top], ab[0, 1, top] + gain * ab[1, 1, top]
            corner = cbab[0] + gain * cbab[1]
        else:
            cb_in()
            zu_in()
            above_x, above_y = zu[k, 0], zu[k, 1]
            own_x, own_y = s[k, 0, top], s[k, 1, top]
            corner = cb[k]
        above_x = above_x - time_step * own_y
        above_y = above_y + time_step * own_x
        above_y = above_y - jnp.where(row == 0, time_step * corner, 0.0)
        acc = finish_layer(top, above_x * inside_ha, above_y * inside_ha, acc)
        if k > 0:
            if top == 0:
                lower_layer(k - 1, 0)
                cb_next, zu_next = send_bottom(k - 1)
            cb_in, zu_in = cb_next, zu_next
            ca_in, zl_in = send_top(k - 1)
            for z in range(1, top):
                acc = finish_layer(z, new[0, z + 1], new[1, z + 1], acc)
        if k == 1:
            plane_in = send_plane(acc)

    finish_sends()
    for arrive in plane_in:
        arrive()
    whole = plane[...]
    low = plane_lo[0]
    high = plane_hi[0]
    for d in range(1, n_ha):
        whole = whole + plane_ha[d - 1]
        low = low + plane_lo[d]
        high = high + plane_hi[d]
    product = jnp.concatenate([low, whole, high], 0) * deriv[...]
    out_g[...] = filter_rows(product, cone_y[...], cone_x[...])


def store(e, h, g, out_e, out_h, out_g, sem):
    copies = [
        pltpu.make_async_copy(e, out_e, sem.at[0]),
        pltpu.make_async_copy(h, out_h, sem.at[1]),
        pltpu.make_async_copy(g, out_g, sem.at[2]),
    ]
    for copy in copies:
        copy.start()
    for copy in copies:
        copy.wait()


def body(
    adjoint_e, adjoint_h, saved_e, labels, eps_table, chi_table, density, mon_cells, mon_weight
):
    n_lat, n_ha = lax.axis_size("lat"), lax.axis_size("ha")
    steps, comps, depth, rows, width = saved_e.shape
    entries = mon_cells.shape[0]
    f32 = jnp.float32
    block = (comps, depth, rows, width)
    group = 2 if n_lat % 2 == 0 else 1
    members, groups = group * n_ha, n_lat // group
    copies = (members - 1) + (groups - 1) + 6 + 6 * steps + 3 * n_ha - 1
    vmem = pl.BlockSpec(memory_space=pltpu.VMEM)
    hbm = pl.BlockSpec(memory_space=pltpu.HBM)
    scratch = [
        pltpu.VMEM(block, f32),
        pltpu.VMEM(block, f32),
        pltpu.VMEM(saved_e.shape, saved_e.dtype),
        pltpu.VMEM(labels.shape, labels.dtype),
        pltpu.VMEM((rows, width), f32),
        pltpu.VMEM((1, entries), mon_cells.dtype),
        pltpu.VMEM((1, entries), f32),
        pltpu.VMEM((depth, rows, width), f32),
        pltpu.VMEM((steps,) + block, f32),
        pltpu.VMEM((steps,) + block, f32),
        pltpu.VMEM((steps,) + block, f32),
        pltpu.VMEM((rows, width), f32),
        pltpu.VMEM((2 * RADIUS, width), f32),
        pltpu.VMEM((2 * RADIUS, width), f32),
        pltpu.VMEM((rows + 2 * RADIUS, width), f32),
        pltpu.VMEM((steps, 2, rows, width), f32),
        pltpu.VMEM((steps, 2, rows, width), f32),
        pltpu.VMEM((steps, 2, rows, width), f32),
        pltpu.VMEM((steps, 2 * depth, width), f32),
        pltpu.VMEM((steps, 2 * depth, width), f32),
        pltpu.VMEM((steps, 2 * depth, width), f32),
        pltpu.VMEM((steps, 2 * depth, width), f32),
        pltpu.VMEM((steps, 1, width), f32),
        pltpu.VMEM((steps, 1, width), f32),
        pltpu.VMEM((steps, 1, width), f32),
        pltpu.VMEM((steps, 1, width), f32),
        pltpu.SMEM(eps_table.shape, f32),
        pltpu.SMEM(chi_table.shape, f32),
        pltpu.VMEM((width, width), jnp.bfloat16),
        pltpu.VMEM((rows, rows + 2 * RADIUS), jnp.bfloat16),
        pltpu.VMEM((rows + 2 * RADIUS, rows + 4 * RADIUS), jnp.bfloat16),
        pltpu.VMEM((steps, width), f32),
        pltpu.VMEM((max(members - 1, 1), steps, width), f32),
        pltpu.VMEM((steps, width), f32),
        pltpu.VMEM((max(groups - 1, 1), steps, width), f32),
        pltpu.VMEM((2,) + block, f32),
        pltpu.VMEM((2,) + block, f32),
        pltpu.VMEM((2, 2, rows, width), f32),
        pltpu.VMEM((2, 2, rows, width), f32),
        pltpu.VMEM((2, 2, rows, width), f32),
        pltpu.VMEM((4 * depth, width), f32),
        pltpu.VMEM((4 * depth, width), f32),
        pltpu.VMEM((4 * depth, width), f32),
        pltpu.VMEM((4 * depth, width), f32),
        pltpu.VMEM((2, 1, width), f32),
        pltpu.VMEM((2, 1, width), f32),
        pltpu.VMEM((2, 1, width), f32),
        pltpu.VMEM((2, 1, width), f32),
        pltpu.VMEM((max(n_ha - 1, 1), rows, width), f32),
        pltpu.VMEM((n_ha, RADIUS, width), f32),
        pltpu.VMEM((n_ha, RADIUS, width), f32),
        pltpu.SemaphoreType.DMA((9,)),
        pltpu.SemaphoreType.DMA((copies,)),
        pltpu.SemaphoreType.DMA((copies,)),
    ]
    results = pl.pallas_call(
        functools.partial(kernel, n_lat, n_ha),
        out_shape=(
            pltpu.VMEM(block, f32),
            pltpu.VMEM(block, f32),
            pltpu.VMEM((rows, width), f32),
        ),
        in_specs=[hbm] * 9,
        out_specs=(vmem, vmem, vmem),
        scratch_shapes=scratch,
        compiler_params=pltpu.CompilerParams(
            collective_id=0, has_side_effects=True, vmem_limit_bytes=63 * 2**20
        ),
    )(
        adjoint_e,
        adjoint_h,
        saved_e,
        labels,
        eps_table,
        chi_table,
        density,
        mon_cells.reshape(1, entries),
        mon_weight.reshape(1, entries),
    )
    return pl.pallas_call(
        store,
        out_shape=(
            jax.ShapeDtypeStruct(block, f32),
            jax.ShapeDtypeStruct(block, f32),
            jax.ShapeDtypeStruct((rows, width), f32),
        ),
        in_specs=[vmem] * 3,
        out_specs=(hbm, hbm, hbm),
        scratch_shapes=[pltpu.SemaphoreType.DMA((3,))],
        compiler_params=pltpu.CompilerParams(vmem_limit_bytes=2**20),
    )(*results)


def solution(mesh):
    return jax.shard_map(
        body,
        mesh=mesh,
        in_specs=(
            P(None, "ha", "lat", None),
            P(None, "ha", "lat", None),
            P(None, None, "ha", "lat", None),
            P("ha", "lat", None),
            P(),
            P(),
            P("lat", None),
            P(("lat", "ha")),
            P(("lat", "ha")),
        ),
        out_specs=(P(None, "ha", "lat", None), P(None, "ha", "lat", None), P("lat", None)),
        check_vma=False,
    )
```

```python
import functools

import jax
import jax.numpy as jnp
from jax import lax
from jax.experimental import pallas as pl
from jax.experimental.pallas import tpu as pltpu
from jax.sharding import PartitionSpec as P

RADIUS = 16

sharpness = 8.0
threshold = 0.5
time_step = 0.5
epsilon = 1e-05

MESH = pl.DeviceIdType.MESH


def cone(shape, shift):
    offset = lax.broadcasted_iota(jnp.int32, shape, 1) - lax.broadcasted_iota(jnp.int32, shape, 0)
    weights = jnp.maximum(RADIUS + 1 - jnp.abs(offset - shift), 0)
    return weights.astype(jnp.float32).astype(jnp.bfloat16)


def pieces(value):
    first = value.astype(jnp.bfloat16)
    left = value - first.astype(jnp.float32)
    second = left.astype(jnp.bfloat16)
    third = (left - second.astype(jnp.float32)).astype(jnp.bfloat16)
    return third, second, first


def filter_rows(padded, across, downward):
    scale = 1.0 / (RADIUS + 1) ** 2
    smoothed = sum(
        jnp.dot(part, across, preferred_element_type=jnp.float32) for part in pieces(padded)
    )
    return scale * sum(
        jnp.dot(downward, part, preferred_element_type=jnp.float32)
        for part in pieces(scale * smoothed)
    )


def kernel(
    n_lat,
    n_ha,
    adj_e,
    adj_h,
    saved,
    labels,
    eps_table,
    chi_table,
    density,
    cells,
    weight,
    out_e,
    out_h,
    out_g,
    e,
    h0,
    sv,
    lb,
    dens,
    cl,
    wt,
    wgrid,
    s,
    hh,
    rinv,
    plane,
    dens_lo,
    dens_hi,
    deriv,
    hz_out,
    zl,
    zu,
    rl_out,
    rl,
    ru_out,
    ru,
    ca_out,
    ca,
    cb_out,
    cb,
    eps_of,
    chi_of,
    cone_y,
    cone_x,
    cone_wide,
    pw_out,
    pw_in,
    pw_sum,
    pw_all,
    ab,
    pab,
    hzab_out,
    zuab,
    zlab,
    rlab_out,
    rlab,
    ruab_out,
    ruab,
    caab_out,
    caab,
    cbab_out,
    cbab,
    plane_ha,
    plane_lo,
    plane_hi,
    local_sem,
    send_sem,
    recv_sem,
):
    steps, comps, depth, rows, width = sv.shape
    regions = eps_table.shape[0]
    entries = cl.shape[1]
    last, top = steps - 1, depth - 1
    devices = n_lat * n_ha
    lat = lax.axis_index("lat")
    ha = lax.axis_index("ha")
    lat_dn, lat_up = lat > 0, lat < n_lat - 1
    ha_dn, ha_up = ha > 0, ha < n_ha - 1
    lat_prev, lat_next = jnp.maximum(lat - 1, 0), jnp.minimum(lat + 1, n_lat - 1)
    ha_prev, ha_next = jnp.maximum(ha - 1, 0), jnp.minimum(ha + 1, n_ha - 1)

    pairs = [
        (cells, cl),
        (weight, wt),
        (saved, sv),
        (labels, lb),
        (adj_h, h0),
        (adj_e, e),
        (density, dens),
        (eps_table, eps_of),
        (chi_table, chi_of),
    ]
    loads = [pltpu.make_async_copy(a, b, local_sem.at[i]) for i, (a, b) in enumerate(pairs)]
    for load in loads:
        load.start()

    group = 2 if n_lat % 2 == 0 else 1
    place, number = lax.rem(lat, group), lax.div(lat, group)
    members, groups = group * n_ha, n_lat // group

    def member(d):
        there = lax.rem(place * n_ha + ha + d, members)
        return (number * group + lax.div(there, n_ha), lax.rem(there, n_ha))

    def counterpart(d):
        return (lax.rem(number + d, groups) * group + place, ha)

    barrier = pltpu.get_barrier_semaphore()

    def greet(target):
        pl.semaphore_signal(barrier, inc=1, device_id=target, device_id_type=MESH)

    for d in range(1, members):
        greet(member(d))
    for d in range(1, groups):
        greet(counterpart(d))
    greeted = (members - 1) + (groups - 1)
    if group == 2:
        outer = lat - 1 + 2 * place
        exists = jnp.logical_and(outer >= 0, outer < n_lat)
        beyond = [(exists, outer, d) for d in range(n_ha)]
    else:
        beyond = [(lat_dn, lat_prev, d) for d in range(1, n_ha)]
        beyond += [(lat_up, lat_next, d) for d in range(1, n_ha)]
    for condition, there, d in beyond:
        pl.when(condition)(functools.partial(greet, (there, lax.rem(ha + d, n_ha))))
        greeted = greeted + condition.astype(jnp.int32)

    issued = []
    numbers = iter(range(send_sem.shape[0]))

    def finish_sends(kept=0):
        while len(issued) > kept:
            issued.pop(0)()

    def exchange(src, dst, target, sends=None, receives=None):
        index = next(numbers)

        def copy():
            return pltpu.make_async_remote_copy(
                src_ref=src,
                dst_ref=dst,
                send_sem=send_sem.at[index],
                recv_sem=recv_sem.at[index],
                device_id=target,
                device_id_type=MESH,
            )

        def guarded(condition, action):
            if condition is None:
                action()
            else:
                pl.when(condition)(action)

        issued.append(lambda: guarded(sends, lambda: copy().wait_send()))
        guarded(sends, lambda: copy().start())

        def arrive():
            guarded(receives, lambda: copy().wait_recv())
            if receives is not None:

                @pl.when(jnp.logical_not(receives))
                def _():
                    dst[...] = jnp.zeros(dst.shape, dst.dtype)

        return arrive

    def field(k, c, z):
        return sv[k, c, z].astype(jnp.float32)

    lane = lax.broadcasted_iota(jnp.int32, (rows, width), 1)
    row = lax.broadcasted_iota(jnp.int32, (rows, width), 0)
    inside_ha = ha_up.astype(jnp.float32)
    inside_lat = lat_up.astype(jnp.float32)

    def y_lower(v):
        return jnp.where(lane == 0, 0.0, pltpu.roll(v, 1, 1))

    def y_upper(v):
        return jnp.where(lane == width - 1, 0.0, pltpu.roll(v, width - 1, 1))

    def x_lower(v, edge):
        return jnp.where(row == 0, edge, pltpu.roll(v, 1, 0))

    def x_upper(v, edge):
        return jnp.where(row == rows - 1, edge, pltpu.roll(v, rows - 1, 0))

    def material(z):
        label = lb[z]
        eps = jnp.full((rows, width), eps_of[0], jnp.float32)
        chi = jnp.full((rows, width), 3.0 * chi_of[0], jnp.float32)
        for region in range(1, regions):
            hit = label == region
            eps = jnp.where(hit, eps_of[region], eps)
            chi = jnp.where(hit, 3.0 * chi_of[region], chi)
        return eps, chi

    def lower_parts(src, z):
        sx, sy, sz = src[0, z], src[1, z], src[2, z]
        curl_x = sz - y_lower(sz) - sy
        curl_y = sx - (sz - x_lower(sz, 0.0))
        curl_z = sy - x_lower(sy, 0.0) - (sx - y_lower(sx))
        if z > 0:
            curl_x = curl_x + src[1, z - 1]
            curl_y = curl_y - src[0, z - 1]
        return curl_x, curl_y, curl_z

    def part_a(z):
        eps, chi = material(z)
        inner = jnp.zeros((rows, width), jnp.float32)
        for c in range(comps):
            f = field(last, c, z)
            inverse = 1.0 / (eps + chi * f * f)
            ab[1, c, z] = f * inverse
            inner = inner + put_part(0, c, z, e[c, z] * inverse) * f
        return jnp.where(lb[z] == 0, inner, 0.0)

    def part_b(z):
        inner = jnp.zeros((rows, width), jnp.float32)
        for c in range(comps):
            inner = inner + put_part(1, c, z, wgrid[z] * ab[1, c, z]) * field(last, c, z)
        return jnp.where(lb[z] == 0, inner, 0.0)

    def put_part(i, c, z, value):
        ab[i, c, z] = value
        if c > 0:
            slot = (2 * i + c - 1) * depth + z
            rlab_out[slot : slot + 1, :] = value[rows - 1 : rows]
        if c == 0 and z == top:
            caab_out[i] = value[0:1]
        if c == 2 and z == 0:
            cbab_out[i] = value[rows - 1 : rows]
        return value

    def part_curl(i, z):
        curl = lower_parts(ab.at[i], z)
        for c in range(comps):
            value = -time_step * curl[c]
            if i == 0:
                value = h0[c, z] + value
            pab[i, c, z] = value
            if z == 0 and c < 2:
                hzab_out[i, c] = value
            if c > 0:
                slot = (2 * i + c - 1) * depth + z
                ruab_out[slot : slot + 1, :] = value[0:1]

    def ends(part, i):
        inner = part(0)
        part_curl(i, 0)
        arrivals = [
            exchange(cbab_out.at[i], cbab.at[i], *corner_b),
            exchange(hzab_out.at[i], zuab.at[i], (lat, ha_prev), ha_dn, ha_up),
        ]
        if top > 0:
            inner = inner + part(top)
        arrivals.append(exchange(caab_out.at[i], caab.at[i], *corner_a))
        arrivals.append(
            exchange(ab.at[i, pl.ds(0, 2), top], zlab.at[i], (lat, ha_next), ha_up, ha_dn)
        )
        return inner, arrivals

    cone_y[...] = cone(cone_y.shape, 0)
    cone_x[...] = cone(cone_x.shape, RADIUS)
    cone_wide[...] = cone(cone_wide.shape, RADIUS)

    loads[0].wait()
    loads[1].wait()
    cell = cl[...]
    amount = wt[...]
    line = lax.broadcasted_iota(jnp.int32, (depth * rows, entries), 0) == cell // width
    lane_hit = lax.broadcasted_iota(jnp.int32, (width, entries), 0) == lax.rem(cell, width)
    line = jnp.where(line, 1.0, 0.0).astype(jnp.bfloat16)
    total = jnp.zeros((depth * rows, width), jnp.float32)
    for part in pieces(amount):
        spread = jnp.where(lane_hit, part.astype(jnp.float32), 0.0).astype(jnp.bfloat16)
        total = total + lax.dot_general(
            line, spread, (((1,), (1,)), ((), ())), preferred_element_type=jnp.float32
        )
    for z in range(depth):
        wgrid[z] = total[z * rows : (z + 1) * rows]

    loads[2].wait()
    for k in range(steps):
        acc = jnp.zeros((rows, width), jnp.float32)
        for z in range(depth):
            square = jnp.zeros((rows, width), jnp.float32)
            for c in range(comps):
                f = field(k, c, z)
                square = square + f * f
            acc = acc + wgrid[z] * square
        pw_out[k : k + 1, :] = jnp.sum(acc, 0, keepdims=True)

    pl.semaphore_wait(barrier, greeted)
    members_in = [exchange(pw_out, pw_in.at[d - 1], member(d)) for d in range(1, members)]

    corner_a = (
        (lat_prev, ha_next),
        jnp.logical_and(lat_dn, ha_up),
        jnp.logical_and(lat_up, ha_dn),
    )
    corner_b = (
        (lat_next, ha_prev),
        jnp.logical_and(lat_up, ha_dn),
        jnp.logical_and(lat_dn, ha_up),
    )
    for index in (3, 4, 5, 7, 8):
        loads[index].wait()
    inner_a, (cba_in, zua_in, caa_in, zla_in) = ends(part_a, 0)
    inner_b, (cbb_in, zub_in, cab_in, zlb_in) = ends(part_b, 1)
    for arrive in members_in:
        arrive()
    power_rows = pw_out[...]
    for d in range(1, members):
        power_rows = power_rows + pw_in[d - 1]
    pw_sum[...] = power_rows
    groups_in = [exchange(pw_sum, pw_all.at[d - 1], counterpart(d)) for d in range(1, groups)]

    for z in range(1, top):
        inner_a = inner_a + part_a(z)
        inner_b = inner_b + part_b(z)
    rlab_in = exchange(rlab_out, rlab, (lat_next, ha), lat_up, lat_dn)

    for z in range(1, depth):
        part_curl(0, z)
        part_curl(1, z)
    ruab_in = exchange(ruab_out, ruab, (lat_prev, ha), lat_dn, lat_up)

    loads[6].wait()
    dens_lo_in = exchange(
        dens.at[pl.ds(rows - 2 * RADIUS, 2 * RADIUS)], dens_lo, (lat_next, ha), lat_up, lat_dn
    )
    dens_hi_in = exchange(
        dens.at[pl.ds(0, 2 * RADIUS)], dens_hi, (lat_prev, ha), lat_dn, lat_up
    )

    for z in range(depth):
        eps, chi = material(z)
        for k in range(last):
            for c in range(comps):
                f = field(k, c, z)
                rinv[k, c, z] = 1.0 / (eps + chi * f * f)

    dens_lo_in()
    dens_hi_in()
    extended = jnp.concatenate([dens_lo[...], dens[...], dens_hi[...]], 0)
    filtered = filter_rows(extended, cone_y[...], cone_wide[...])
    slope = jnp.tanh(sharpness * (filtered - threshold))
    deriv[...] = (
        sharpness
        * (1.0 - slope * slope)
        / (jnp.tanh(sharpness * threshold) + jnp.tanh(sharpness * (1.0 - threshold)))
    )

    for arrive in groups_in:
        arrive()
    for d in range(1, groups):
        power_rows = power_rows + pw_all[d - 1]
    power = jnp.sum(power_rows, 1, keepdims=True) / (entries * devices) + epsilon
    inverse_power = 1.0 / power

    def scale_layer(k, z, fields, acc):
        gain = inverse_power[k : k + 1, :]
        inner = jnp.zeros((rows, width), jnp.float32)
        for c in range(comps):
            f = field(k, c, z)
            now = fields[c] + gain * (wgrid[z] * f)
            value = now * rinv[k, c, z]
            e[c, z] = now
            s[k, c, z] = value
            inner = inner + value * f
            if c > 0:
                slot = (c - 1) * depth + z
                rl_out[k, slot : slot + 1, :] = value[rows - 1 : rows]
            if c == 0 and z == top:
                ca_out[k] = value[0:1]
            if c == 2 and z == 0:
                cb_out[k] = value[rows - 1 : rows]
        return acc + jnp.where(lb[z] == 0, inner, 0.0)

    def magnetic(k):
        return out_h if k == 0 else hh.at[k]

    def lower_layer(k, z):
        old = magnetic(k + 1)
        new = magnetic(k)
        curl_x, curl_y, curl_z = lower_parts(s.at[k], z)
        values = (
            old[0, z] - time_step * curl_x,
            old[1, z] - time_step * curl_y,
            old[2, z] - time_step * curl_z,
        )
        for c in range(comps):
            new[c, z] = values[c]
            if z == 0 and c < 2:
                hz_out[k, c] = values[c]
            if c > 0:
                slot = (c - 1) * depth + z
                ru_out[k, slot : slot + 1, :] = values[c][0:1]

    def send_bottom(k):
        return (
            exchange(cb_out.at[k], cb.at[k], *corner_b),
            exchange(hz_out.at[k], zu.at[k], (lat, ha_prev), ha_dn, ha_up),
        )

    def send_top(k):
        return (
            exchange(ca_out.at[k], ca.at[k], *corner_a),
            exchange(s.at[k, pl.ds(0, 2), top], zl.at[k], (lat, ha_next), ha_up, ha_dn),
        )

    def send_plane(acc):
        plane[...] = acc
        arrivals = []
        for d in reversed(range(n_ha)):
            other = lax.rem(ha + d, n_ha)
            arrivals.append(
                exchange(
                    plane.at[pl.ds(rows - RADIUS, RADIUS)],
                    plane_lo.at[d],
                    (lat_next, other),
                    lat_up,
                    lat_dn,
                )
            )
            arrivals.append(
                exchange(
                    plane.at[pl.ds(0, RADIUS)],
                    plane_hi.at[d],
                    (lat_prev, other),
                    lat_dn,
                    lat_up,
                )
            )
        for d in range(1, n_ha):
            arrivals.append(exchange(plane, plane_ha.at[d - 1], (lat, lax.rem(ha + d, n_ha))))
        return arrivals

    gain = inverse_power[last : last + 1, :]
    acc = inner_a + gain * inner_b
    for z in range(depth):
        for c in range(comps):
            magnetic(last)[c, z] = pab[0, c, z] + gain * pab[1, c, z]

    def joined(ref):
        half = ref.shape[0] // 2
        return ref[pl.ds(0, half)] + gain * ref[pl.ds(half, half)]

    if last == 0:
        plane_in = send_plane(acc)
    for k in reversed(range(steps)):
        if k == last:
            rl_in, ru_in = rlab_in, ruab_in
        else:
            kept = len(issued)
            rl_in = exchange(rl_out.at[k], rl.at[k], (lat_next, ha), lat_up, lat_dn)
            for z in range(1, depth):
                lower_layer(k, z)
            ru_in = exchange(ru_out.at[k], ru.at[k], (lat_prev, ha), lat_dn, lat_up)
            finish_sends(len(issued) - kept + 3 + 3 * n_ha)

        new = magnetic(k)
        rl_in()
        low = joined(rlab) if k == last else rl[k]
        for z in range(depth):
            new[1, z, 0:1] = new[1, z, 0:1] - time_step * low[depth + z : depth + z + 1]
            new[2, z, 0:1] = new[2, z, 0:1] + time_step * low[z : z + 1]

        ru_in()
        if k == last:
            caa_in()
            cab_in()
        else:
            ca_in()
        own = joined(rlab_out) if k == last else rl_out[k]
        high = joined(ruab) if k == last else ru[k]
        corner = caab[0] + gain * caab[1] if k == last else ca[k]
        high_y = (high[0:depth] - time_step * own[depth : 2 * depth]) * inside_lat
        high_z = (high[depth : 2 * depth] + time_step * own[0:depth]) * inside_lat
        first_y = high_y[0:1] + time_step * inside_lat * corner

        def finish_layer(z, above_x, above_y, acc):
            hx, hy, hv = new[0, z], new[1, z], new[2, z]
            edge_y = first_y if z == 0 else high_y[z : z + 1]
            edge_z = high_z[z : z + 1]
            curl_x = y_upper(hv) - hv - (above_y - hy)
            curl_y = above_x - hx - (x_upper(hv, edge_z) - hv)
            curl_z = x_upper(hy, edge_y) - hy - (y_upper(hx) - hx)
            fields = [
                e[0, z] + time_step * curl_x,
                e[1, z] + time_step * curl_y,
                e[2, z] + time_step * curl_z,
            ]
            if k == last:
                for c in range(comps):
                    fields[c] = fields[c] + gain * (wgrid[z] * field(k, c, z))
            if k > 0:
                return scale_layer(k - 1, z, fields, acc)
            for c in range(comps):
                out_e[c, z] = fields[c]
            return acc

        if k == 0:
            for z in range(1, top):
                acc = finish_layer(z, new[0, z + 1], new[1, z + 1], acc)

        if k == last:
            zla_in()
            zlb_in()
            below_x, below_y = zlab[0, 0] + gain * zlab[1, 0], zlab[0, 1] + gain * zlab[1, 1]
        else:
            zl_in()
            below_x, below_y = zl[k, 0], zl[k, 1]
        new[0, 0] = new[0, 0] - time_step * below_y
        new[1, 0] = new[1, 0] + time_step * below_x
        if top > 0:
            acc = finish_layer(0, new[0, 1], new[1, 1], acc)
            if k > 0:
                lower_layer(k - 1, 0)
                cb_next, zu_next = send_bottom(k - 1)

        if k == last:
            cba_in()
            cbb_in()
            zua_in()
            zub_in()
            above_x, above_y = zuab[0, 0] + gain * zuab[1, 0], zuab[0, 1] + gain * zuab[1, 1]
            own_x, own_y = ab[0, 0, top] + gain * ab[1, 0, top], ab[0, 1, top] + gain * ab[1, 1, top]
            corner = cbab[0] + gain * cbab[1]
        else:
            cb_in()
            zu_in()
            above_x, above_y = zu[k, 0], zu[k, 1]
            own_x, own_y = s[k, 0, top], s[k, 1, top]
            corner = cb[k]
        above_x = above_x - time_step * own_y
        above_y = above_y + time_step * own_x
        above_y = above_y - jnp.where(row == 0, time_step * corner, 0.0)
        acc = finish_layer(top, above_x * inside_ha, above_y * inside_ha, acc)
        if k > 0:
            if top == 0:
                lower_layer(k - 1, 0)
                cb_next, zu_next = send_bottom(k - 1)
            cb_in, zu_in = cb_next, zu_next
            ca_in, zl_in = send_top(k - 1)
            for z in range(1, top):
                acc = finish_layer(z, new[0, z + 1], new[1, z + 1], acc)
        if k == 1:
            plane_in = send_plane(acc)

    finish_sends()
    for arrive in plane_in:
        arrive()
    whole = plane[...]
    low = plane_lo[0]
    high = plane_hi[0]
    for d in range(1, n_ha):
        whole = whole + plane_ha[d - 1]
        low = low + plane_lo[d]
        high = high + plane_hi[d]
    product = jnp.concatenate([low, whole, high], 0) * deriv[...]
    out_g[...] = filter_rows(product, cone_y[...], cone_x[...])


def store(e, h, g, out_e, out_h, out_g, sem):
    copies = [
        pltpu.make_async_copy(e, out_e, sem.at[0]),
        pltpu.make_async_copy(h, out_h, sem.at[1]),
        pltpu.make_async_copy(g, out_g, sem.at[2]),
    ]
    for copy in copies:
        copy.start()
    for copy in copies:
        copy.wait()


def body(
    adjoint_e, adjoint_h, saved_e, labels, eps_table, chi_table, density, mon_cells, mon_weight
):
    n_lat, n_ha = lax.axis_size("lat"), lax.axis_size("ha")
    steps, comps, depth, rows, width = saved_e.shape
    entries = mon_cells.shape[0]
    f32 = jnp.float32
    block = (comps, depth, rows, width)
    group = 2 if n_lat % 2 == 0 else 1
    members, groups = group * n_ha, n_lat // group
    copies = (members - 1) + (groups - 1) + 6 + 6 * steps + 3 * n_ha - 1
    vmem = pl.BlockSpec(memory_space=pltpu.VMEM)
    hbm = pl.BlockSpec(memory_space=pltpu.HBM)
    scratch = [
        pltpu.VMEM(block, f32),
        pltpu.VMEM(block, f32),
        pltpu.VMEM(saved_e.shape, saved_e.dtype),
        pltpu.VMEM(labels.shape, labels.dtype),
        pltpu.VMEM((rows, width), f32),
        pltpu.VMEM((1, entries), mon_cells.dtype),
        pltpu.VMEM((1, entries), f32),
        pltpu.VMEM((depth, rows, width), f32),
        pltpu.VMEM((steps,) + block, f32),
        pltpu.VMEM((steps,) + block, f32),
        pltpu.VMEM((steps,) + block, f32),
        pltpu.VMEM((rows, width), f32),
        pltpu.VMEM((2 * RADIUS, width), f32),
        pltpu.VMEM((2 * RADIUS, width), f32),
        pltpu.VMEM((rows + 2 * RADIUS, width), f32),
        pltpu.VMEM((steps, 2, rows, width), f32),
        pltpu.VMEM((steps, 2, rows, width), f32),
        pltpu.VMEM((steps, 2, rows, width), f32),
        pltpu.VMEM((steps, 2 * depth, width), f32),
        pltpu.VMEM((steps, 2 * depth, width), f32),
        pltpu.VMEM((steps, 2 * depth, width), f32),
        pltpu.VMEM((steps, 2 * depth, width), f32),
        pltpu.VMEM((steps, 1, width), f32),
        pltpu.VMEM((steps, 1, width), f32),
        pltpu.VMEM((steps, 1, width), f32),
        pltpu.VMEM((steps, 1, width), f32),
        pltpu.SMEM(eps_table.shape, f32),
        pltpu.SMEM(chi_table.shape, f32),
        pltpu.VMEM((width, width), jnp.bfloat16),
        pltpu.VMEM((rows, rows + 2 * RADIUS), jnp.bfloat16),
        pltpu.VMEM((rows + 2 * RADIUS, rows + 4 * RADIUS), jnp.bfloat16),
        pltpu.VMEM((steps, width), f32),
        pltpu.VMEM((max(members - 1, 1), steps, width), f32),
        pltpu.VMEM((steps, width), f32),
        pltpu.VMEM((max(groups - 1, 1), steps, width), f32),
        pltpu.VMEM((2,) + block, f32),
        pltpu.VMEM((2,) + block, f32),
        pltpu.VMEM((2, 2, rows, width), f32),
        pltpu.VMEM((2, 2, rows, width), f32),
        pltpu.VMEM((2, 2, rows, width), f32),
        pltpu.VMEM((4 * depth, width), f32),
        pltpu.VMEM((4 * depth, width), f32),
        pltpu.VMEM((4 * depth, width), f32),
        pltpu.VMEM((4 * depth, width), f32),
        pltpu.VMEM((2, 1, width), f32),
        pltpu.VMEM((2, 1, width), f32),
        pltpu.VMEM((2, 1, width), f32),
        pltpu.VMEM((2, 1, width), f32),
        pltpu.VMEM((max(n_ha - 1, 1), rows, width), f32),
        pltpu.VMEM((n_ha, RADIUS, width), f32),
        pltpu.VMEM((n_ha, RADIUS, width), f32),
        pltpu.SemaphoreType.DMA((9,)),
        pltpu.SemaphoreType.DMA((copies,)),
        pltpu.SemaphoreType.DMA((copies,)),
    ]
    results = pl.pallas_call(
        functools.partial(kernel, n_lat, n_ha),
        out_shape=(
            pltpu.VMEM(block, f32),
            pltpu.VMEM(block, f32),
            pltpu.VMEM((rows, width), f32),
        ),
        in_specs=[hbm] * 9,
        out_specs=(vmem, vmem, vmem),
        scratch_shapes=scratch,
        compiler_params=pltpu.CompilerParams(
            collective_id=0, has_side_effects=True, vmem_limit_bytes=63 * 2**20
        ),
    )(
        adjoint_e,
        adjoint_h,
        saved_e,
        labels,
        eps_table,
        chi_table,
        density,
        mon_cells.reshape(1, entries),
        mon_weight.reshape(1, entries),
    )
    return pl.pallas_call(
        store,
        out_shape=(
            jax.ShapeDtypeStruct(block, f32),
            jax.ShapeDtypeStruct(block, f32),
            jax.ShapeDtypeStruct((rows, width), f32),
        ),
        in_specs=[vmem] * 3,
        out_specs=(hbm, hbm, hbm),
        scratch_shapes=[pltpu.SemaphoreType.DMA((3,))],
        compiler_params=pltpu.CompilerParams(vmem_limit_bytes=2**20),
    )(*results)


def solution(mesh):
    return jax.shard_map(
        body,
        mesh=mesh,
        in_specs=(
            P(None, "ha", "lat", None),
            P(None, "ha", "lat", None),
            P(None, None, "ha", "lat", None),
            P("ha", "lat", None),
            P(),
            P(),
            P("lat", None),
            P(("lat", "ha")),
            P(("lat", "ha")),
        ),
        out_specs=(P(None, "ha", "lat", None), P(None, "ha", "lat", None), P("lat", None)),
        check_vma=False,
    )
```
